256 devices in a mesh: group: 4 (over x_hi, core), zslab: 64 (over z, x_lo, y).
Axes of the slice: x: 4 (x_hi: 2, x_lo: 2; x = x_hi * 2 + x_lo), y: 4, z: 8, core: 2. Of those that a mesh axis runs over, the one named last changes fastest.
Arguments:
- background: float32 [128, 32, 128], P('zslab'), may hold values from 2.1 to 12.1
- absorb: float32 [128, 32, 128], P('zslab'), may hold values from 0.3 to 1
- density: float32 [128, 32, 128], P('zslab'), may hold values from 0 to 1
- profiles: float32 [6, 2, 128, 32, 128], P(None, None, 'zslab'), may hold values from -6 to 6
- adjoint_source: float32 [16, 2, 128, 32, 128], P('group', None, 'zslab'), may hold values from -6 to 6
- port_modes: int32 [16], P('group'), may hold values from 0 to 5
- design_start: int32 [1], replicated, may hold values from 0 to 64
Outputs:
- forward_field: float32 [16, 2, 128, 32, 128], P('group', None, 'zslab')
- adjoint_field: float32 [16, 2, 128, 32, 128], P('group', None, 'zslab')
- new_density: float32 [128, 32, 128], P('zslab', 'group')
The draws below stay inside these ranges and needn't reach their ends.
Inputs may be any that keep to these rules, and one draw needn't show every extreme that they name: The design region is planes design_start to design_start + 63. Port p's forward source is the profile of mode port_modes[p].
All inputs are finite; a program needn't handle non-finite values.
Results may differ from the reference program's by a relative error of at most 0.0003.
Values sent between devices are 32-bit elements; how exact they have to be, the bound alone decides.
No kernel may reach another device: no remote copies, remote signals or barrier semaphores. Data moves between devices by JAX's collectives and lax.ppermute only.
A program may use at most 64 MiB of HBM per device.

```python
import jax
import jax.numpy as jnp
from jax import lax

NX = 128
NY = 32
PORTS = 16
MODES = 6
ITERS = 4
NZ = 128
DZ = 64


def plant(array, rng, least, high):
    spot = [jax.random.randint(jax.random.fold_in(rng, axis), (), 0, length) for axis, length in enumerate(array.shape)]
    longest = array.shape.index(max(array.shape))
    next_to = spot[:longest] + [(spot[longest] + 1) % array.shape[longest]] + spot[longest + 1:]
    return array.at[tuple(spot)].set(least).at[tuple(next_to)].set(high)


def block_scale(key, dims, shards, least, top_value):
    gain, own = 1.0, jax.random.fold_in(key, 6)
    for dim, shards_of in shards:
        draws = jnp.exp(jax.random.uniform(jax.random.fold_in(own, dim), (shards_of,), jnp.float32, least / len(shards), top_value / len(shards)))
        gain = gain * jnp.repeat(draws, dims[dim] // shards_of).reshape([-1 if axis == dim else 1 for axis in range(len(dims))])
    return gain


def centred(rng, shape, spread, limit, pieces=(), kind=jnp.bfloat16):
    loudness = block_scale(rng, shape, pieces, -0.22, 0.18) if pieces else 1.0
    entries = jax.random.normal(rng, shape, jnp.float32) * spread * loudness
    return jnp.minimum(jnp.maximum(entries, -limit), limit).astype(kind)


def setup_inputs(seed: int = 0) -> dict:
    keys = jax.random.split(jax.random.key(seed), 8)
    background = jnp.clip(2.1 + 10 * jax.random.uniform(keys[0], (NZ, NY, NX), jnp.float32) ** block_scale(keys[0], (NZ, NY, NX), ((0, 64),), -0.2, 0.2), 2.1, 12.1)
    absorb = jnp.clip(0.3 + 0.7 * jax.random.uniform(keys[1], (NZ, NY, NX), jnp.float32) ** block_scale(keys[1], (NZ, NY, NX), ((0, 64),), -0.2, 0.2), 0.3, 1.0)
    density = jnp.clip(1.0 * jax.random.uniform(keys[2], (NZ, NY, NX), jnp.float32) ** block_scale(keys[2], (NZ, NY, NX), ((0, 64),), -0.2, 0.2), 0.0, 1.0)
    profiles = centred(keys[3], (MODES, 2, NZ, NY, NX), 1.0, 6.0, ((2, 64),), jnp.float32)
    adjoint_source = centred(keys[4], (PORTS, 2, NZ, NY, NX), 1.0, 6.0, ((0, 4), (2, 64)), jnp.float32)
    port_modes = plant(jax.random.randint(keys[5], (PORTS,), 0, MODES), jax.random.fold_in(keys[5], 1), 0, MODES - 1).astype(jnp.int32)
    design_start = jax.random.randint(keys[6], (1,), 0, NZ - DZ + 1).astype(jnp.int32)
    return dict(background=background, absorb=absorb, density=density, profiles=profiles, adjoint_source=adjoint_source, port_modes=port_modes, design_start=design_start)


wave_sq = 0.1
step_size = 2.0
perm_span = 10.0
low_perm = 2.1
sharpness = 8.0
threshold = 0.5


def scaled(coef, field):
    coef_re = coef[0].reshape((-1, 1, 1, 1))
    coef_im = coef[1].reshape((-1, 1, 1, 1))
    real_part = coef_re * field[:, 0] - coef_im * field[:, 1]
    imag_part = coef_re * field[:, 1] + coef_im * field[:, 0]
    return jnp.stack([real_part, imag_part], axis=1)


def product_pair(left, right):
    real_part = jnp.sum(left[:, 0] * right[:, 0] + left[:, 1] * right[:, 1], axis=(1, 2, 3))
    imag_part = jnp.sum(left[:, 0] * right[:, 1] - left[:, 1] * right[:, 0], axis=(1, 2, 3))
    return real_part, imag_part


def divide_pair(top, bottom):
    denominator = bottom[0] * bottom[0] + bottom[1] * bottom[1]
    return ((top[0] * bottom[0] + top[1] * bottom[1]) / denominator,
            (top[1] * bottom[0] - top[0] * bottom[1]) / denominator)


def multiply_pair(left, right):
    return (left[0] * right[0] - left[1] * right[1], left[0] * right[1] + left[1] * right[0])


def operate(field, diag_re, diag_im):
    padded = jnp.pad(field, ((0, 0), (0, 0), (1, 1), (1, 1), (1, 1)))
    beside = padded[:, :, 2:, 1:-1, 1:-1] + padded[:, :, :-2, 1:-1, 1:-1]
    beside = beside + padded[:, :, 1:-1, 2:, 1:-1] + padded[:, :, 1:-1, :-2, 1:-1]
    beside = beside + padded[:, :, 1:-1, 1:-1, 2:] + padded[:, :, 1:-1, 1:-1, :-2]
    real_part = diag_re * field[:, 0] - diag_im * field[:, 1]
    imag_part = diag_re * field[:, 1] + diag_im * field[:, 0]
    return jnp.stack([real_part, imag_part], axis=1) - beside


def bicgstab(sources, diag_re, diag_im):
    solution = jnp.zeros_like(sources)
    residual = sources
    shadow = sources
    direction = sources
    bilinear = product_pair(shadow, residual)
    for iteration in range(ITERS):
        image = operate(direction, diag_re, diag_im)
        advance = divide_pair(bilinear, product_pair(shadow, image))
        halfway = residual - scaled(advance, image)
        second = operate(halfway, diag_re, diag_im)
        cross = product_pair(second, halfway)
        energy = jnp.sum(second[:, 0] * second[:, 0] + second[:, 1] * second[:, 1], axis=(1, 2, 3))
        relax_coef = (cross[0] / energy, cross[1] / energy)
        solution = solution + scaled(advance, direction) + scaled(relax_coef, halfway)
        residual = halfway - scaled(relax_coef, second)
        if iteration + 1 < ITERS:
            bilinear_new = product_pair(shadow, residual)
            blend_coef = multiply_pair(divide_pair(bilinear_new, bilinear), divide_pair(advance, relax_coef))
            direction = residual + scaled(blend_coef, direction - scaled(relax_coef, image))
            bilinear = bilinear_new
    return solution


def reference(background, absorb, density, profiles, adjoint_source, port_modes, design_start):
    planes = jnp.arange(NZ).astype(jnp.int32)
    in_design = (planes >= design_start[0]) & (planes < design_start[0] + DZ)
    in_design = in_design[:, None, None]
    permittivity = jnp.where(in_design, low_perm + perm_span * density, background)
    diag_re = 6.0 - wave_sq * permittivity
    diag_im = absorb
    selector = (port_modes[:, None] == jnp.arange(MODES).astype(jnp.int32)[None, :]).astype(jnp.float32)
    forward_source = jnp.einsum("pm,mczyx->pczyx", selector, profiles, precision=lax.Precision.HIGHEST)

    def solve_port(pair):
        stacked = jnp.stack([pair[0], pair[1]], axis=0)
        return bicgstab(stacked, diag_re, diag_im)

    fields = lax.map(solve_port, (forward_source, adjoint_source))
    forward_field = fields[:, 0]
    adjoint_field = fields[:, 1]
    terms = forward_field[:, 0] * adjoint_field[:, 0] - forward_field[:, 1] * adjoint_field[:, 1]
    gradient = -wave_sq * jnp.sum(terms, axis=0)
    updated = jnp.where(in_design, jnp.clip(density - step_size * perm_span * gradient, 0.0, 1.0), density)
    padded = jnp.pad(updated, ((1, 1), (0, 0), (1, 1)))
    filtered = (2.0 * updated + padded[2:, :, 1:-1] + padded[:-2, :, 1:-1]
                + padded[1:-1, :, 2:] + padded[1:-1, :, :-2]) / 6.0
    new_density = (jnp.tanh(sharpness * threshold) + jnp.tanh(sharpness * (filtered - threshold))) / (
        jnp.tanh(sharpness * threshold) + jnp.tanh(sharpness * (1.0 - threshold)))
    return forward_field, adjoint_field, new_density
```

```python
import functools

import jax
import jax.numpy as jnp
import numpy as np
from jax import lax
from jax.experimental import pallas as pl
from jax.experimental.pallas import tpu as pltpu
from jax.sharding import PartitionSpec as P

ITERS = 4


wave_sq = 0.1
step_size = 2.0
perm_span = 10.0
low_perm = 2.1
sharpness = 8.0
threshold = 0.5


def with_halo(block, sides, width):
    for axis, dim in sides:
        count = lax.axis_size(axis)
        forward = [(i, i + 1) for i in range(count - 1)]
        backward = [(target, source) for source, target in forward]
        low = lax.ppermute(
            lax.slice_in_dim(block, block.shape[dim] - width, None, axis=dim), axis, forward
        )
        high = lax.ppermute(lax.slice_in_dim(block, 0, width, axis=dim), axis, backward)
        block = jnp.concatenate([low, block, high], axis=dim)
    return block


def scaled(coef, field):
    coef_re = coef[0].reshape((-1, 1, 1, 1))
    coef_im = coef[1].reshape((-1, 1, 1, 1))
    real_part = coef_re * field[:, 0] - coef_im * field[:, 1]
    imag_part = coef_re * field[:, 1] + coef_im * field[:, 0]
    return jnp.stack([real_part, imag_part], axis=1)


def product_pair(left, right):
    real_part = jnp.sum(left[:, 0] * right[:, 0] + left[:, 1] * right[:, 1], axis=(1, 2, 3))
    imag_part = jnp.sum(left[:, 0] * right[:, 1] - left[:, 1] * right[:, 0], axis=(1, 2, 3))
    return (real_part, imag_part)


def divide_pair(top, bottom):
    denominator = bottom[0] * bottom[0] + bottom[1] * bottom[1]
    return (
        (top[0] * bottom[0] + top[1] * bottom[1]) / denominator,
        (top[1] * bottom[0] - top[0] * bottom[1]) / denominator,
    )


def multiply_pair(left, right):
    return (left[0] * right[0] - left[1] * right[1], left[0] * right[1] + left[1] * right[0])


def with_planes(field):
    return with_halo(field, (("zslab", 2),), 1)


def operate(field, diag_re, diag_im):
    padded = jnp.pad(with_planes(field), ((0, 0), (0, 0), (0, 0), (1, 1), (1, 1)))
    beside = padded[:, :, 2:, 1:-1, 1:-1] + padded[:, :, :-2, 1:-1, 1:-1]
    beside = beside + padded[:, :, 1:-1, 2:, 1:-1] + padded[:, :, 1:-1, :-2, 1:-1]
    beside = beside + padded[:, :, 1:-1, 1:-1, 2:] + padded[:, :, 1:-1, 1:-1, :-2]
    real_part = diag_re * field[:, 0] - diag_im * field[:, 1]
    imag_part = diag_re * field[:, 1] + diag_im * field[:, 0]
    return jnp.stack([real_part, imag_part], axis=1) - beside


def bicgstab(sources, diag_re, diag_im):
    solution = jnp.zeros_like(sources)
    residual = sources
    direction = sources
    bilinear = lax.psum(product_pair(sources, residual), "zslab")
    for iteration in range(ITERS):
        image = operate(direction, diag_re, diag_im)
        along = lax.psum(product_pair(sources, image), "zslab")
        advance = divide_pair(bilinear, along)
        halfway = residual - scaled(advance, image)
        second = operate(halfway, diag_re, diag_im)
        cross_re, cross_im = product_pair(second, halfway)
        energy = jnp.sum(second[:, 0] * second[:, 0] + second[:, 1] * second[:, 1], axis=(1, 2, 3))
        cross_re, cross_im, energy = lax.psum((cross_re, cross_im, energy), "zslab")
        relax_coef = (cross_re / energy, cross_im / energy)
        solution = solution + scaled(advance, direction) + scaled(relax_coef, halfway)
        residual = halfway - scaled(relax_coef, second)
        if iteration + 1 < ITERS:
            bilinear_new = lax.psum(product_pair(sources, residual), "zslab")
        if iteration + 1 < ITERS:
            blend_coef = multiply_pair(
                divide_pair(bilinear_new, bilinear), divide_pair(advance, relax_coef)
            )
            direction = residual + scaled(blend_coef, direction - scaled(relax_coef, image))
            bilinear = bilinear_new
    return solution


def iterate_on_device(background, absorb, density, profiles, adjoint_source, port_modes, design_start):
    planes_dev = density.shape[0]
    rows_all = density.shape[1]
    first_plane = lax.axis_index("zslab") * planes_dev
    design_depth = planes_dev * lax.axis_size("zslab") // 2
    planes = first_plane + jnp.arange(planes_dev)
    in_design = (planes >= design_start[0]) & (planes < design_start[0] + design_depth)
    in_design = in_design[:, None, None]
    permittivity = jnp.where(in_design, low_perm + perm_span * density, background)
    diag_re = 6.0 - wave_sq * permittivity
    selector = (port_modes[:, None] == jnp.arange(profiles.shape[0])[None, :]).astype(jnp.float32)
    forward_source = jnp.einsum(
        "pm,mczyx->pczyx", selector, profiles, precision=lax.Precision.HIGHEST
    )
    port_count = forward_source.shape[0]
    sources = jnp.concatenate([forward_source, adjoint_source], axis=0)
    fields = bicgstab(sources, diag_re, absorb)
    forward_field = fields[:port_count]
    adjoint_field = fields[port_count:]
    terms = forward_field[:, 0] * adjoint_field[:, 0] - forward_field[:, 1] * adjoint_field[:, 1]
    local_term = -wave_sq * jnp.sum(terms, axis=0)
    rows_share = rows_all // lax.axis_size("group")
    row_start = lax.axis_index("group") * rows_share
    total = lax.psum(local_term, "group")
    gradient = lax.dynamic_slice_in_dim(total, row_start, rows_share, 1)
    density_rows = lax.dynamic_slice_in_dim(density, row_start, rows_share, 1)
    updated = jnp.where(
        in_design, jnp.clip(density_rows - step_size * perm_span * gradient, 0.0, 1.0), density_rows
    )
    extended = with_halo(updated, (("zslab", 0),), 1)
    padded = jnp.pad(extended, ((0, 0), (0, 0), (1, 1)))
    filtered = (
        2.0 * updated
        + padded[2:, :, 1:-1]
        + padded[:-2, :, 1:-1]
        + padded[1:-1, :, 2:]
        + padded[1:-1, :, :-2]
    ) / 6.0
    new_density = (
        jnp.tanh(sharpness * threshold) + jnp.tanh(sharpness * (filtered - threshold))
    ) / (jnp.tanh(sharpness * threshold) + jnp.tanh(sharpness * (1.0 - threshold)))
    return (forward_field, adjoint_field, new_density)


BASIS = 2 * ITERS + 1
CENTRE = 5.3
HALF_RADIUS = 3.0
THIRD = 1.0 / HALF_RADIUS
NUDGE = 1e-6
AGREE = 5e-4
ROWS = 16 * BASIS


def pair_places():
    real, imag, place = {}, {}, 0
    for j in range(BASIS):
        for i in range(j + 1):
            real[(i, j)] = place
            place += 1
    for j in range(BASIS):
        for i in range(j):
            imag[(i, j)] = place
            place += 1
    return real, imag


def gram_tables():
    real, imag = pair_places()
    pick = np.zeros((6 * ROWS, 128), np.float32)
    nudge = np.zeros((2 * ROWS, 128), np.float32)
    rng = np.random.default_rng(7)
    sign_re = {pair: np.where(rng.random(128) < 0.5, -1.0, 1.0) for pair in real}
    sign_im = {pair: np.where(rng.random(128) < 0.5, -1.0, 1.0) for pair in imag}
    for j in range(BASIS):
        for i in range(BASIS):
            row, pair = j * 16 + i, (min(i, j), max(i, j))
            pick[row, real[pair]] = 1.0
            for half in (0, ROWS):
                pick[2 * ROWS + half + row, real[(i, i)]] = 1.0
                pick[4 * ROWS + half + row, real[(j, j)]] = 1.0
            nudge[row] = NUDGE * sign_re[pair]
            if i != j:
                side = 1.0 if i < j else -1.0
                pick[ROWS + row, imag[pair]] = side
                nudge[ROWS + row] = NUDGE * side * sign_im[pair]
    nudge[:, 0] = 0.0
    return pick, nudge


def exact_dot(left, right, dims):
    return lax.dot_general(
        left, right, (dims, ((), ())), precision=lax.Precision.HIGHEST,
        preferred_element_type=jnp.float32,
    )


def minus_pair(left, right):
    return (left[0] - right[0], left[1] - right[1])


def plus_pair(left, right):
    return (left[0] + right[0], left[1] + right[1])


def coefficients(gram):
    gram_re = [gram[16 * j : 16 * j + 16] for j in range(BASIS)]
    gram_im = [gram[ROWS + 16 * j : ROWS + 16 * j + 16] for j in range(BASIS)]
    row = lax.broadcasted_iota(jnp.int32, (16, 128), 0)
    keep = jnp.where(row == 15, 0.0, HALF_RADIUS)

    def apply(q):
        return tuple(
            CENTRE * v + HALF_RADIUS * pltpu.roll(v, 1, 0) + keep * pltpu.roll(v, 15, 0) for v in q
        )

    def total(v):
        return jnp.sum(v, axis=0, keepdims=True)

    def with_source(q):
        return (
            total(gram_re[0] * q[0] + gram_im[0] * q[1]),
            total(gram_re[0] * q[1] - gram_im[0] * q[0]),
        )

    def times_gram(q):
        out_re = jnp.zeros((16, 128), jnp.float32)
        out_im = jnp.zeros((16, 128), jnp.float32)
        for j in range(BASIS):
            q_re, q_im = q[0][j : j + 1], q[1][j : j + 1]
            out_re = out_re + (gram_re[j] * q_re - gram_im[j] * q_im)
            out_im = out_im + (gram_re[j] * q_im + gram_im[j] * q_re)
        return out_re, out_im

    one = jnp.where(row == 0, 1.0, 0.0)
    zero = jnp.zeros((16, 128), jnp.float32)
    answer, residual, direction = (zero, zero), (one, zero), (one, zero)
    bilinear = with_source(residual)
    for iteration in range(ITERS):
        image = apply(direction)
        advance = divide_pair(bilinear, with_source(image))
        halfway = minus_pair(residual, multiply_pair(advance, image))
        second = apply(halfway)
        weighed = times_gram(second)
        energy = total(second[0] * weighed[0] + second[1] * weighed[1])
        relax = (
            total(weighed[0] * halfway[0] + weighed[1] * halfway[1]) / energy,
            total(weighed[0] * halfway[1] - weighed[1] * halfway[0]) / energy,
        )
        answer = plus_pair(
            answer, plus_pair(multiply_pair(advance, direction), multiply_pair(relax, halfway))
        )
        if iteration + 1 < ITERS:
            residual = minus_pair(halfway, multiply_pair(relax, second))
            bilinear_new = with_source(residual)
            blend = multiply_pair(divide_pair(bilinear_new, bilinear), divide_pair(advance, relax))
            direction = plus_pair(
                residual, multiply_pair(blend, minus_pair(direction, multiply_pair(relax, image)))
            )
            bilinear = bilinear_new
    first = tuple(jnp.broadcast_to(v[:, :1], v.shape) for v in answer)
    apart = minus_pair(answer, first)

    def norm(q):
        weighed = times_gram(q)
        return total(q[0] * weighed[0] + q[1] * weighed[1])

    return first, norm(apart), norm(first)


TILES = 4
SYSTEMS = 8
BLOCK = 16 * TILES // 2 + 2
WINDOW = 32
CORE = 8
KEPT = 18
VMEM = pl.BlockSpec(memory_space=pltpu.VMEM)
SMEM = pl.BlockSpec(memory_space=pltpu.SMEM)
ANY = pl.BlockSpec(memory_space=pl.ANY)
LIMIT = 40 * 1024 * 1024


def call(kernel, outs, specs, out_specs, scratch=(), name=None):
    return pl.pallas_call(
        kernel,
        out_shape=outs,
        in_specs=specs,
        out_specs=out_specs,
        scratch_shapes=list(scratch),
        compiler_params=pltpu.CompilerParams(vmem_limit_bytes=LIMIT),
        name=name,
    )


def f32(*shape):
    return jax.ShapeDtypeStruct(shape, jnp.float32)


def pack_kernel(modes, start, place, background, absorb, density, profiles, adjoint, out, sems):
    copies = []
    for port in range(SYSTEMS // 2):
        copies.append(
            pltpu.make_async_copy(
                profiles.at[modes[port]], out.at[port, pl.ds(0, 16)], sems.at[port]
            )
        )
        copies.append(
            pltpu.make_async_copy(
                adjoint.at[port],
                out.at[SYSTEMS // 2 + port, pl.ds(0, 16)],
                sems.at[SYSTEMS // 2 + port],
            )
        )
    for copy in copies:
        copy.start()
    for plane in range(2):
        where = place[0] * 2 + plane
        inside = (where >= start[0]) & (where < start[0] + 64)
        for tile in range(TILES):
            dens = density[plane, tile]
            perm = jnp.where(inside, low_perm + perm_span * dens, background[plane, tile])
            diag_re = ((6.0 - wave_sq * perm) - CENTRE) * THIRD
            diag_im = absorb[plane, tile] * THIRD
            for system in range(SYSTEMS):
                out[system, 16 + plane * TILES + tile] = diag_re
                out[system, 24 + plane * TILES + tile] = diag_im
        rows = density[plane, place[1]]
        for system in range(SYSTEMS):
            out[system, 32 + plane] = rows
    for copy in copies:
        copy.wait()


def basis_kernel(place, block, low, high, basis, gram, dens, diag, acc):
    row = lax.broadcasted_iota(jnp.int32, (8 * TILES, 128), 0)
    lane = lax.broadcasted_iota(jnp.int32, (8 * TILES, 128), 1)
    first_row, last_row = row == 0, row == 8 * TILES - 1
    first_lane, last_lane = lane == 0, lane == 127
    third_low = jnp.where(place[0] >= SYSTEMS, THIRD, 0.0)
    third_high = jnp.where(place[0] < SYSTEMS * (SYSTEMS - 1), THIRD, 0.0)

    def load(source, chunks, at):
        def one(chunk, _):
            for plane in range(2):
                window = at + 2 * chunk + plane
                for part in range(2):
                    basis[0, part, window] = source[
                        chunk, pl.ds(part * 8 + plane * TILES, TILES)
                    ].reshape(8 * TILES, 128)
                    diag[part, window] = source[
                        chunk, pl.ds(16 + part * 8 + plane * TILES, TILES)
                    ].reshape(8 * TILES, 128)
            return 0

        lax.fori_loop(0, chunks, one, 0)

    load(low, 4, 0)
    load(block, 8, CORE)
    load(high, 4, CORE + 16)

    me = place[0] % SYSTEMS
    dens[0] = jnp.where(me > 0, block[jnp.maximum(me - 1, 0), 33], low[3, 33])
    dens[1] = block[me, 32]
    dens[2] = block[me, 33]
    dens[3] = jnp.where(
        me < SYSTEMS - 1, block[jnp.minimum(me + 1, SYSTEMS - 1), 32], high[0, 32]
    )

    def beside(field, level, part, window):
        up = jnp.where(first_row, 0.0, pltpu.roll(field, 1, 0))
        down = jnp.where(last_row, 0.0, pltpu.roll(field, 8 * TILES - 1, 0))
        left = jnp.where(first_lane, 0.0, pltpu.roll(field, 1, 1))
        right = jnp.where(last_lane, 0.0, pltpu.roll(field, 127, 1))
        z_sum = basis[level, part, window - 1] + basis[level, part, window + 1]
        return (z_sum + (up + down)) + (left + right)

    for level in range(BASIS - 1):

        def plane_step(window, _, level=level):
            third = jnp.where(
                window < CORE, third_low, jnp.where(window >= CORE + 16, third_high, THIRD)
            )
            real, imag = basis[level, 0, window], basis[level, 1, window]
            diag_re, diag_im = diag[0, window], diag[1, window]
            new_re = diag_re * real - diag_im * imag - third * beside(real, level, 0, window)
            new_im = diag_re * imag + diag_im * real - third * beside(imag, level, 1, window)
            if level > 0:
                new_re = new_re - basis[level - 1, 0, window]
                new_im = new_im - basis[level - 1, 1, window]
            basis[level + 1, 0, window] = new_re
            basis[level + 1, 1, window] = new_im
            return 0

        lax.fori_loop(level + 1, WINDOW - 1 - level, plane_step, 0, unroll=2)

    real_at, imag_at = pair_places()
    for rows in ((0, 1), (2, 3), range(4, BASIS)):
        pairs = [(i, j) for i in rows for j in range(i, BASIS)]
        count = sum(2 - (i == j) for i, j in pairs)
        low_index = min(rows)

        def position(step, sums, pairs=pairs, low_index=low_index):
            window, tile = CORE + step // TILES, step % TILES
            here = pl.ds(pl.multiple_of(tile * 8, 8), 8)
            field = {
                k: (basis[k, 0, window, here], basis[k, 1, window, here])
                for k in range(low_index, BASIS)
            }
            new = []
            for i, j in pairs:
                (i_re, i_im), (j_re, j_im) = field[i], field[j]
                new.append(i_re * j_re + i_im * j_im)
                if i != j:
                    new.append(i_re * j_im - i_im * j_re)
            return tuple(total + term for total, term in zip(sums, new))

        zero = jnp.zeros((8, 128), jnp.float32)
        sums = lax.fori_loop(0, 16 * TILES, position, (zero,) * count, unroll=2)
        place_of = 0
        for i, j in pairs:
            acc[real_at[(i, j)]] = sums[place_of]
            place_of += 1
            if i != j:
                acc[imag_at[(i, j)]] = sums[place_of]
                place_of += 1
    for spare in range(len(real_at) + len(imag_at), 128):
        acc[spare] = jnp.zeros((8, 128), jnp.float32)
    by_pair = jnp.sum(acc[...], axis=1)
    ones = jnp.ones((8, 128), jnp.float32)
    gram[...] = exact_dot(ones, by_pair, ((1,), (1,)))[0:1]


def combine_kernel(grams, pick, nudge, basis, out):
    row = grams[0]
    for other in range(1, SYSTEMS):
        row = row + grams[other]
    ones = jnp.ones((128, 128), jnp.float32)
    picked = exact_dot(pick[...] * row, ones, ((1,), (0,)))
    norms = jnp.sqrt(picked[2 * ROWS : 4 * ROWS] * picked[4 * ROWS :])
    answer, apart, size = coefficients(picked[: 2 * ROWS] + nudge[...] * norms)
    agrees = jnp.max(jnp.where(apart <= AGREE * AGREE * size, 0.0, 1.0))
    flag = jnp.zeros((8, 128), jnp.float32) + agrees
    for slab in range(SYSTEMS):
        out[slab, 32] = flag
    weight = [
        (
            jnp.broadcast_to(answer[0][k : k + 1], (8 * TILES, 128)),
            jnp.broadcast_to(answer[1][k : k + 1], (8 * TILES, 128)),
        )
        for k in range(BASIS - 1)
    ]

    def two_planes(first):
        planes = []
        for plane in (first, first + 1):
            real = jnp.zeros((8 * TILES, 128), jnp.float32)
            imag = jnp.zeros((8 * TILES, 128), jnp.float32)
            for k in range(BASIS - 1):
                b_re, b_im = basis[k, 0, plane], basis[k, 1, plane]
                real = real + (weight[k][0] * b_re - weight[k][1] * b_im)
                imag = imag + (weight[k][0] * b_im + weight[k][1] * b_re)
            planes.append((real.reshape(TILES, 8, 128), imag.reshape(TILES, 8, 128)))
        return planes

    def put(slab, at, planes):
        for plane in range(2):
            for part in range(2):
                out[slab, pl.ds((part * 4 + at + plane) * TILES, TILES)] = planes[plane][part]

    def middle(slab, _):
        planes = two_planes(CORE - 1 + 2 * slab)
        put(slab, 0, planes)
        put(slab - 1, 2, planes)
        return 0

    put(0, 0, two_planes(CORE - 1))
    lax.fori_loop(1, SYSTEMS, middle, 0)
    put(SYSTEMS - 1, 2, two_planes(CORE - 1 + 2 * SYSTEMS))


def fields_kernel(fields, forward, adjoint, terms):
    half = SYSTEMS // 2
    for port in range(half):
        for part in range(2):
            own = pl.ds((part * 4 + 1) * TILES, 2 * TILES)
            forward[port, part] = fields[port, own]
            adjoint[port, part] = fields[half + port, own]
    for plane in range(4):
        total = None
        for port in range(half):
            real, imag = pl.ds(plane * TILES, TILES), pl.ds((4 + plane) * TILES, TILES)
            term = fields[port, real] * fields[half + port, real]
            term = term - fields[port, imag] * fields[half + port, imag]
            total = term if total is None else total + term
        for tile in range(TILES):
            terms[tile, plane] = total[tile]
    flag = fields[0, 32]
    for system in range(1, SYSTEMS):
        flag = flag + fields[system, 32]
    for tile in range(TILES):
        terms[tile, 4] = flag


def density_kernel(start, place, terms, dens, out, flag):
    lane = lax.broadcasted_iota(jnp.int32, (8, 128), 1)
    updated = []
    for plane in range(4):
        total = terms[0, plane]
        for other in range(1, 4):
            total = total + terms[other, plane]
        gradient = -wave_sq * total
        where = place[0] * 2 + plane - 1
        inside = (where >= start[0]) & (where < start[0] + 64)
        rows = dens[plane]
        moved = jnp.clip(rows - step_size * perm_span * gradient, 0.0, 1.0)
        rows = jnp.where(inside, moved, rows)
        exists = (where >= 0) & (where < 2 * SYSTEMS * SYSTEMS)
        updated.append(jnp.where(exists, rows, 0.0))
    for plane in range(2):
        own = updated[plane + 1]
        right = jnp.where(lane == 127, 0.0, pltpu.roll(own, 127, 1))
        left = jnp.where(lane == 0, 0.0, pltpu.roll(own, 1, 1))
        filtered = (2.0 * own + updated[plane + 2] + updated[plane] + right + left) / 6.0
        edge = float(np.tanh(sharpness * threshold))
        other_edge = float(np.tanh(sharpness * (1.0 - threshold)))
        out[plane] = (edge + jnp.tanh(sharpness * (filtered - threshold))) / (edge + other_edge)
    spread = terms[0, 4] + terms[1, 4] + terms[2, 4] + terms[3, 4]
    flag[0] = jnp.max(spread)


def on_device(background, absorb, density, profiles, adjoint_source, port_modes, design_start):
    args = (background, absorb, density, profiles, adjoint_source, port_modes, design_start)
    slab = lax.axis_index("zslab")
    place = jnp.stack([slab, lax.axis_index("group")]).astype(jnp.int32)
    planes_of = [[z * SYSTEMS + l for l in range(SYSTEMS)] for z in range(SYSTEMS)]
    columns = [[z * SYSTEMS + l for z in range(SYSTEMS)] for l in range(SYSTEMS)]
    tiles = (2, TILES, 8, 128)
    packed = call(
        pack_kernel,
        f32(SYSTEMS, BLOCK, 8, 128),
        [SMEM, SMEM, SMEM, VMEM, VMEM, VMEM, ANY, ANY],
        VMEM,
        [pltpu.SemaphoreType.DMA((SYSTEMS,))],
        "pack",
    )(
        port_modes, design_start, place,
        background.reshape(tiles), absorb.reshape(tiles), density.reshape(tiles),
        profiles.reshape(-1, 16, 8, 128), adjoint_source.reshape(-1, 16, 8, 128),
    )
    block = lax.all_to_all(packed, "zslab", 0, 0, axis_index_groups=planes_of, tiled=True)
    count = SYSTEMS * SYSTEMS
    up = [(i, i + SYSTEMS) for i in range(count - SYSTEMS)]
    down = [(target, source) for source, target in up]
    low = lax.ppermute(block[SYSTEMS // 2 :], "zslab", up)
    high = lax.ppermute(block[: SYSTEMS // 2], "zslab", down)
    basis, gram, dens = call(
        basis_kernel,
        (f32(BASIS, 2, WINDOW, 8 * TILES, 128), f32(1, 128), f32(4, 8, 128)),
        [SMEM, VMEM, VMEM, VMEM],
        (VMEM, VMEM, VMEM),
        [pltpu.VMEM((2, WINDOW, 8 * TILES, 128), jnp.float32), pltpu.VMEM((128, 8, 128), jnp.float32)],
        "basis",
    )(place, block, low, high)
    grams = lax.all_to_all(
        jnp.broadcast_to(gram[None], (SYSTEMS, 1, 128)), "zslab", 0, 0,
        axis_index_groups=columns, tiled=True,
    )
    pick, nudge = gram_tables()
    solved = call(
        combine_kernel, f32(SYSTEMS, 33, 8, 128), [VMEM, VMEM, VMEM, VMEM], VMEM, (), "combine"
    )(grams, jnp.asarray(pick), jnp.asarray(nudge), basis)
    fields = lax.all_to_all(solved, "zslab", 0, 0, axis_index_groups=planes_of, tiled=True)
    half = (SYSTEMS // 2, 2, 2 * TILES, 8, 128)
    forward, adjoint, terms = call(
        fields_kernel, (f32(*half), f32(*half), f32(4, 5, 8, 128)), [VMEM], (VMEM,) * 3, (), "fields"
    )(fields)
    terms = lax.all_to_all(terms, "group", 0, 0, tiled=True)
    new_density, flag = call(
        density_kernel, (f32(2, 8, 128), f32(1)), [SMEM, SMEM, VMEM, VMEM], (VMEM, SMEM), (), "density"
    )(design_start, place, terms, dens)
    shape = (SYSTEMS // 2, 2, 2, 8 * TILES, 128)
    state = (flag[0], forward.reshape(shape), adjoint.reshape(shape), new_density)

    def again(state):
        return (jnp.zeros((), jnp.float32),) + iterate_on_device(*args)

    return lax.while_loop(lambda state: state[0] > 0.0, again, state)[1:]


def solution(mesh):
    return jax.shard_map(
        on_device,
        mesh=mesh,
        in_specs=(
            P("zslab", None, None),
            P("zslab", None, None),
            P("zslab", None, None),
            P(None, None, "zslab", None, None),
            P("group", None, "zslab", None, None),
            P("group"),
            P(),
        ),
        out_specs=(
            P("group", None, "zslab", None, None),
            P("group", None, "zslab", None, None),
            P("zslab", "group", None),
        ),
        check_vma=False,
    )
```

```python
import functools

import jax
import jax.numpy as jnp
import numpy as np
from jax import lax
from jax.experimental import pallas as pl
from jax.experimental.pallas import tpu as pltpu
from jax.sharding import PartitionSpec as P

ITERS = 4


wave_sq = 0.1
step_size = 2.0
perm_span = 10.0
low_perm = 2.1
sharpness = 8.0
threshold = 0.5


def with_halo(block, sides, width):
    for axis, dim in sides:
        count = lax.axis_size(axis)
        forward = [(i, i + 1) for i in range(count - 1)]
        backward = [(target, source) for source, target in forward]
        low = lax.ppermute(
            lax.slice_in_dim(block, block.shape[dim] - width, None, axis=dim), axis, forward
        )
        high = lax.ppermute(lax.slice_in_dim(block, 0, width, axis=dim), axis, backward)
        block = jnp.concatenate([low, block, high], axis=dim)
    return block


def scaled(coef, field):
    coef_re = coef[0].reshape((-1, 1, 1, 1))
    coef_im = coef[1].reshape((-1, 1, 1, 1))
    real_part = coef_re * field[:, 0] - coef_im * field[:, 1]
    imag_part = coef_re * field[:, 1] + coef_im * field[:, 0]
    return jnp.stack([real_part, imag_part], axis=1)


def product_pair(left, right):
    real_part = jnp.sum(left[:, 0] * right[:, 0] + left[:, 1] * right[:, 1], axis=(1, 2, 3))
    imag_part = jnp.sum(left[:, 0] * right[:, 1] - left[:, 1] * right[:, 0], axis=(1, 2, 3))
    return (real_part, imag_part)


def divide_pair(top, bottom):
    denominator = bottom[0] * bottom[0] + bottom[1] * bottom[1]
    return (
        (top[0] * bottom[0] + top[1] * bottom[1]) / denominator,
        (top[1] * bottom[0] - top[0] * bottom[1]) / denominator,
    )


def multiply_pair(left, right):
    return (left[0] * right[0] - left[1] * right[1], left[0] * right[1] + left[1] * right[0])


def with_planes(field):
    return with_halo(field, (("zslab", 2),), 1)


def operate(field, diag_re, diag_im):
    padded = jnp.pad(with_planes(field), ((0, 0), (0, 0), (0, 0), (1, 1), (1, 1)))
    beside = padded[:, :, 2:, 1:-1, 1:-1] + padded[:, :, :-2, 1:-1, 1:-1]
    beside = beside + padded[:, :, 1:-1, 2:, 1:-1] + padded[:, :, 1:-1, :-2, 1:-1]
    beside = beside + padded[:, :, 1:-1, 1:-1, 2:] + padded[:, :, 1:-1, 1:-1, :-2]
    real_part = diag_re * field[:, 0] - diag_im * field[:, 1]
    imag_part = diag_re * field[:, 1] + diag_im * field[:, 0]
    return jnp.stack([real_part, imag_part], axis=1) - beside


def bicgstab(sources, diag_re, diag_im):
    solution = jnp.zeros_like(sources)
    residual = sources
    direction = sources
    bilinear = lax.psum(product_pair(sources, residual), "zslab")
    for iteration in range(ITERS):
        image = operate(direction, diag_re, diag_im)
        along = lax.psum(product_pair(sources, image), "zslab")
        advance = divide_pair(bilinear, along)
        halfway = residual - scaled(advance, image)
        second = operate(halfway, diag_re, diag_im)
        cross_re, cross_im = product_pair(second, halfway)
        energy = jnp.sum(second[:, 0] * second[:, 0] + second[:, 1] * second[:, 1], axis=(1, 2, 3))
        cross_re, cross_im, energy = lax.psum((cross_re, cross_im, energy), "zslab")
        relax_coef = (cross_re / energy, cross_im / energy)
        solution = solution + scaled(advance, direction) + scaled(relax_coef, halfway)
        residual = halfway - scaled(relax_coef, second)
        if iteration + 1 < ITERS:
            bilinear_new = lax.psum(product_pair(sources, residual), "zslab")
        if iteration + 1 < ITERS:
            blend_coef = multiply_pair(
                divide_pair(bilinear_new, bilinear), divide_pair(advance, relax_coef)
            )
            direction = residual + scaled(blend_coef, direction - scaled(relax_coef, image))
            bilinear = bilinear_new
    return solution


def iterate_on_device(background, absorb, density, profiles, adjoint_source, port_modes, design_start):
    planes_dev = density.shape[0]
    rows_all = density.shape[1]
    first_plane = lax.axis_index("zslab") * planes_dev
    design_depth = planes_dev * lax.axis_size("zslab") // 2
    planes = first_plane + jnp.arange(planes_dev)
    in_design = (planes >= design_start[0]) & (planes < design_start[0] + design_depth)
    in_design = in_design[:, None, None]
    permittivity = jnp.where(in_design, low_perm + perm_span * density, background)
    diag_re = 6.0 - wave_sq * permittivity
    selector = (port_modes[:, None] == jnp.arange(profiles.shape[0])[None, :]).astype(jnp.float32)
    forward_source = jnp.einsum(
        "pm,mczyx->pczyx", selector, profiles, precision=lax.Precision.HIGHEST
    )
    port_count = forward_source.shape[0]
    sources = jnp.concatenate([forward_source, adjoint_source], axis=0)
    fields = bicgstab(sources, diag_re, absorb)
    forward_field = fields[:port_count]
    adjoint_field = fields[port_count:]
    terms = forward_field[:, 0] * adjoint_field[:, 0] - forward_field[:, 1] * adjoint_field[:, 1]
    local_term = -wave_sq * jnp.sum(terms, axis=0)
    rows_share = rows_all // lax.axis_size("group")
    row_start = lax.axis_index("group") * rows_share
    total = lax.psum(local_term, "group")
    gradient = lax.dynamic_slice_in_dim(total, row_start, rows_share, 1)
    density_rows = lax.dynamic_slice_in_dim(density, row_start, rows_share, 1)
    updated = jnp.where(
        in_design, jnp.clip(density_rows - step_size * perm_span * gradient, 0.0, 1.0), density_rows
    )
    extended = with_halo(updated, (("zslab", 0),), 1)
    padded = jnp.pad(extended, ((0, 0), (0, 0), (1, 1)))
    filtered = (
        2.0 * updated
        + padded[2:, :, 1:-1]
        + padded[:-2, :, 1:-1]
        + padded[1:-1, :, 2:]
        + padded[1:-1, :, :-2]
    ) / 6.0
    new_density = (
        jnp.tanh(sharpness * threshold) + jnp.tanh(sharpness * (filtered - threshold))
    ) / (jnp.tanh(sharpness * threshold) + jnp.tanh(sharpness * (1.0 - threshold)))
    return (forward_field, adjoint_field, new_density)


BASIS = 2 * ITERS + 1
CENTRE = 5.3
HALF_RADIUS = 3.0
THIRD = 1.0 / HALF_RADIUS
NUDGE = 1e-6
AGREE = 5e-4
ROWS = 16 * BASIS


def pair_places():
    real, imag, place = {}, {}, 0
    for j in range(BASIS):
        for i in range(j + 1):
            real[(i, j)] = place
            place += 1
    for j in range(BASIS):
        for i in range(j):
            imag[(i, j)] = place
            place += 1
    return real, imag


def gram_tables():
    real, imag = pair_places()
    pick = np.zeros((6 * ROWS, 128), np.float32)
    nudge = np.zeros((2 * ROWS, 128), np.float32)
    rng = np.random.default_rng(7)
    sign_re = {pair: np.where(rng.random(128) < 0.5, -1.0, 1.0) for pair in real}
    sign_im = {pair: np.where(rng.random(128) < 0.5, -1.0, 1.0) for pair in imag}
    for j in range(BASIS):
        for i in range(BASIS):
            row, pair = j * 16 + i, (min(i, j), max(i, j))
            pick[row, real[pair]] = 1.0
            for half in (0, ROWS):
                pick[2 * ROWS + half + row, real[(i, i)]] = 1.0
                pick[4 * ROWS + half + row, real[(j, j)]] = 1.0
            nudge[row] = NUDGE * sign_re[pair]
            if i != j:
                side = 1.0 if i < j else -1.0
                pick[ROWS + row, imag[pair]] = side
                nudge[ROWS + row] = NUDGE * side * sign_im[pair]
    nudge[:, 0] = 0.0
    return pick, nudge


def exact_dot(left, right, dims):
    return lax.dot_general(
        left, right, (dims, ((), ())), precision=lax.Precision.HIGHEST,
        preferred_element_type=jnp.float32,
    )


def minus_pair(left, right):
    return (left[0] - right[0], left[1] - right[1])


def plus_pair(left, right):
    return (left[0] + right[0], left[1] + right[1])


def coefficients(gram):
    gram_re = [gram[16 * j : 16 * j + 16] for j in range(BASIS)]
    gram_im = [gram[ROWS + 16 * j : ROWS + 16 * j + 16] for j in range(BASIS)]
    row = lax.broadcasted_iota(jnp.int32, (16, 128), 0)
    keep = jnp.where(row == 15, 0.0, HALF_RADIUS)

    def apply(q):
        return tuple(
            CENTRE * v + HALF_RADIUS * pltpu.roll(v, 1, 0) + keep * pltpu.roll(v, 15, 0) for v in q
        )

    def total(v):
        return jnp.sum(v, axis=0, keepdims=True)

    def with_source(q):
        return (
            total(gram_re[0] * q[0] + gram_im[0] * q[1]),
            total(gram_re[0] * q[1] - gram_im[0] * q[0]),
        )

    def times_gram(q):
        out_re = jnp.zeros((16, 128), jnp.float32)
        out_im = jnp.zeros((16, 128), jnp.float32)
        for j in range(BASIS):
            q_re, q_im = q[0][j : j + 1], q[1][j : j + 1]
            out_re = out_re + (gram_re[j] * q_re - gram_im[j] * q_im)
            out_im = out_im + (gram_re[j] * q_im + gram_im[j] * q_re)
        return out_re, out_im

    one = jnp.where(row == 0, 1.0, 0.0)
    zero = jnp.zeros((16, 128), jnp.float32)
    answer, residual, direction = (zero, zero), (one, zero), (one, zero)
    bilinear = with_source(residual)
    for iteration in range(ITERS):
        image = apply(direction)
        advance = divide_pair(bilinear, with_source(image))
        halfway = minus_pair(residual, multiply_pair(advance, image))
        second = apply(halfway)
        weighed = times_gram(second)
        energy = total(second[0] * weighed[0] + second[1] * weighed[1])
        relax = (
            total(weighed[0] * halfway[0] + weighed[1] * halfway[1]) / energy,
            total(weighed[0] * halfway[1] - weighed[1] * halfway[0]) / energy,
        )
        answer = plus_pair(
            answer, plus_pair(multiply_pair(advance, direction), multiply_pair(relax, halfway))
        )
        if iteration + 1 < ITERS:
            residual = minus_pair(halfway, multiply_pair(relax, second))
            bilinear_new = with_source(residual)
            blend = multiply_pair(divide_pair(bilinear_new, bilinear), divide_pair(advance, relax))
            direction = plus_pair(
                residual, multiply_pair(blend, minus_pair(direction, multiply_pair(relax, image)))
            )
            bilinear = bilinear_new
    first = tuple(jnp.broadcast_to(v[:, :1], v.shape) for v in answer)
    apart = minus_pair(answer, first)

    def norm(q):
        weighed = times_gram(q)
        return total(q[0] * weighed[0] + q[1] * weighed[1])

    return first, norm(apart), norm(first)


TILES = 4
SYSTEMS = 8
BLOCK = 16 * TILES // 2 + 2
OWN = 16
WINDOW = 32
CORE = 8
VMEM = pl.BlockSpec(memory_space=pltpu.VMEM)
SMEM = pl.BlockSpec(memory_space=pltpu.SMEM)
HBM = pl.BlockSpec(memory_space=pltpu.HBM)
LIMIT = 24 * 1024 * 1024


def call(kernel, outs, specs, out_specs, scratch=(), name=None, flops=0):
    return pl.pallas_call(
        kernel,
        out_shape=outs,
        in_specs=specs,
        out_specs=out_specs,
        scratch_shapes=list(scratch),
        compiler_params=pltpu.CompilerParams(vmem_limit_bytes=LIMIT),
        cost_estimate=pl.CostEstimate(flops=flops, bytes_accessed=1 << 20, transcendentals=0),
        name=name,
    )


def f32(*shape):
    return jax.ShapeDtypeStruct(shape, jnp.float32)


def rows_of(tile):
    return pl.ds(tile, 8, stride=TILES)


def pack_kernel(modes, start, place, background, absorb, density, profiles, adjoint, out, raw, sems):
    half = SYSTEMS // 2
    copies = []
    for system in range(SYSTEMS):
        source = profiles.at[modes[system]] if system < half else adjoint.at[system - half]
        copies.append(pltpu.make_async_copy(source, raw.at[system], sems.at[system]))
    for copy in copies:
        copy.start()
    for plane in range(2):
        where = place[0] * 2 + plane
        inside = (where >= start[0]) & (where < start[0] + SYSTEMS * SYSTEMS)
        for tile in range(TILES):
            rows = rows_of(tile)
            perm = jnp.where(
                inside, low_perm + perm_span * density[plane, rows], background[plane, rows]
            )
            diag_re = ((6.0 - wave_sq * perm) - CENTRE) * THIRD
            diag_im = absorb[plane, rows] * THIRD
            for system in range(SYSTEMS):
                out[system, 16 + plane * TILES + tile] = diag_re
                out[system, 24 + plane * TILES + tile] = diag_im
        share = density[plane, pl.ds(pl.multiple_of(place[1] * 8, 8), 8)]
        for system in range(SYSTEMS):
            out[system, 32 + plane] = share
    for system in range(SYSTEMS):
        copies[system].wait()
        for part in range(2):
            for plane in range(2):
                for tile in range(TILES):
                    out[system, (part * 2 + plane) * TILES + tile] = raw[
                        system, part, plane, rows_of(tile)
                    ]


class Stencil:
    def __init__(self):
        row = lax.broadcasted_iota(jnp.int32, (8, 128), 0)
        lane = lax.broadcasted_iota(jnp.int32, (8, 128), 1)
        self.first_row, self.last_row = row == 0, row == 7
        self.first_lane, self.last_lane = lane == 0, lane == 127

    def beside(self, below, here, above):
        up = jnp.where(self.first_row, 0.0, pltpu.roll(here[TILES - 1], 1, 0))
        down = jnp.where(self.last_row, 0.0, pltpu.roll(here[0], 7, 0))
        rows = [up] + list(here) + [down]
        sums = []
        for tile in range(TILES):
            left = jnp.where(self.first_lane, 0.0, pltpu.roll(here[tile], 1, 1))
            right = jnp.where(self.last_lane, 0.0, pltpu.roll(here[tile], 127, 1))
            z_sum = below[tile] + above[tile]
            sums.append((z_sum + (rows[tile] + rows[tile + 2])) + (left + right))
        return sums

    def step(self, basis, diag, level, at, third):
        def plane(part, where):
            return [basis[level, part, where, tile] for tile in range(TILES)]

        real, imag = plane(0, at), plane(1, at)
        near_re = self.beside(plane(0, at - 1), real, plane(0, at + 1))
        near_im = self.beside(plane(1, at - 1), imag, plane(1, at + 1))
        for tile in range(TILES):
            diag_re, diag_im = diag[0, at, tile], diag[1, at, tile]
            new_re = diag_re * real[tile] - diag_im * imag[tile] - third * near_re[tile]
            new_im = diag_re * imag[tile] + diag_im * real[tile] - third * near_im[tile]
            if level > 0:
                new_re = new_re - basis[level - 1, 0, at, tile]
                new_im = new_im - basis[level - 1, 1, at, tile]
            basis[level + 1, 0, at, tile] = new_re
            basis[level + 1, 1, at, tile] = new_im


def gram_pass(basis, acc, columns, ranges, shift):
    real_at, imag_at = pair_places()
    pairs = [(i, j) for j in columns for i in range(j + 1)]
    top = max(columns) + 1
    places = []
    for pair in pairs:
        places.append(real_at[pair])
        if pair[0] != pair[1]:
            places.append(imag_at[pair])

    def position(step, sums, first=0):
        window, tile = first + shift + step // TILES, step % TILES
        field = [(basis[k, 0, window, tile], basis[k, 1, window, tile]) for k in range(top)]
        new = []
        for i, j in pairs:
            (i_re, i_im), (j_re, j_im) = field[i], field[j]
            new.append(i_re * j_re + i_im * j_im)
            if i != j:
                new.append(i_re * j_im - i_im * j_re)
        return tuple(total + term for total, term in zip(sums, new))

    sums = tuple(acc[at] for at in places)
    for first, last in ranges:
        sums = lax.fori_loop(
            0, (last - first) * TILES, functools.partial(position, first=first), sums
        )
    for at, value in zip(places, sums):
        acc[at] = value


def inner_kernel(block, basis, diag, acc):
    def load(chunk, _):
        for plane in range(2):
            for part in range(2):
                for tile in range(TILES):
                    at = part * 8 + plane * TILES + tile
                    basis[0, part, 2 * chunk + plane, tile] = block[chunk, at]
                    diag[part, 2 * chunk + plane, tile] = block[chunk, 16 + at]
        return 0

    lax.fori_loop(0, SYSTEMS, load, 0)
    stencil = Stencil()
    for level in range(SYSTEMS - 1):

        def plane_step(at, _, level=level):
            stencil.step(basis, diag, level, at, THIRD)
            return 0

        lax.fori_loop(level + 1, OWN - 1 - level, plane_step, 0, unroll=2)
    acc[...] = jnp.zeros_like(acc)
    for columns, ranges in INNER_PASSES:
        gram_pass(basis, acc, columns, ranges, 0)


INNER_PASSES = (
    ((0, 1, 2, 3, 4), ((4, 12),)),
    ((0, 1, 2), ((2, 4), (12, 14))),
    ((5, 6), ((6, 10),)),
)
OUTER_PASSES = (
    ((0, 1, 2, 3, 4), ((0, 2), (14, 16))),
    ((3, 4), ((2, 4), (12, 14))),
    ((5, 6), ((0, 6), (10, 16))),
    ((7,), ((0, 16),)),
    ((8,), ((0, 16),)),
)


def outer_kernel(place, block, low, high, inner, inner_diag, inner_acc, basis, gram, dens, diag, acc):
    def load(source, chunks, at):
        def one(chunk, _):
            for plane in range(2):
                window = at + 2 * chunk + plane
                for part in range(2):
                    for tile in range(TILES):
                        spot = part * 8 + plane * TILES + tile
                        basis[0, part, window, tile] = source[chunk, spot]
                        diag[part, window, tile] = source[chunk, 16 + spot]
            return 0

        lax.fori_loop(0, chunks, one, 0)

    load(low, SYSTEMS // 2, 0)
    load(high, SYSTEMS // 2, CORE + OWN)
    for level in range(SYSTEMS):

        def keep(at, _, level=level):
            for part in range(2):
                for tile in range(TILES):
                    basis[level, part, CORE + at, tile] = inner[level, part, at, tile]
                    if level == 0:
                        diag[part, CORE + at, tile] = inner_diag[part, at, tile]
            return 0

        lax.fori_loop(level, OWN - level, keep, 0, unroll=2)
    acc[...] = inner_acc[...]

    me = place[0] % SYSTEMS
    dens[0] = jnp.where(me > 0, block[jnp.maximum(me - 1, 0), 33], low[SYSTEMS // 2 - 1, 33])
    dens[1] = block[me, 32]
    dens[2] = block[me, 33]
    dens[3] = jnp.where(
        me < SYSTEMS - 1, block[jnp.minimum(me + 1, SYSTEMS - 1), 32], high[0, 32]
    )

    third_low = jnp.where(place[0] >= SYSTEMS, THIRD, 0.0)
    third_high = jnp.where(place[0] < SYSTEMS * (SYSTEMS - 1), THIRD, 0.0)
    stencil = Stencil()
    for level in range(BASIS - 1):

        def two_planes(step, _, level=level):
            lower, upper = level + 1 + step, WINDOW - 2 - level - step
            stencil.step(basis, diag, level, lower, jnp.where(lower < CORE, third_low, THIRD))
            stencil.step(
                basis, diag, level, upper, jnp.where(upper >= CORE + OWN, third_high, THIRD)
            )
            return 0

        lax.fori_loop(0, CORE, two_planes, 0)
    for columns, ranges in OUTER_PASSES:
        gram_pass(basis, acc, columns, ranges, CORE)
    by_pair = jnp.sum(acc[...], axis=1)
    ones = jnp.ones((8, 128), jnp.float32)
    gram[...] = exact_dot(ones, by_pair, ((1,), (1,)))[0:1]


def combine_kernel(grams, pick, nudge, basis, out):
    row = grams[0]
    for other in range(1, SYSTEMS):
        row = row + grams[other]
    ones = jnp.ones((128, 128), jnp.float32)
    picked = exact_dot(pick[...] * row, ones, ((1,), (0,)))
    norms = jnp.sqrt(picked[2 * ROWS : 4 * ROWS] * picked[4 * ROWS :])
    answer, apart, size = coefficients(picked[: 2 * ROWS] + nudge[...] * norms)
    agrees = jnp.max(jnp.where(apart <= AGREE * AGREE * size, 0.0, 1.0))
    flag = jnp.zeros((8, 128), jnp.float32) + agrees
    for slab in range(SYSTEMS):
        out[slab, 32] = flag
    weight = [
        (
            jnp.broadcast_to(answer[0][k : k + 1], (8, 128)),
            jnp.broadcast_to(answer[1][k : k + 1], (8, 128)),
        )
        for k in range(BASIS - 1)
    ]

    def solve_plane(plane, goals):
        for tile in range(TILES):
            real = jnp.zeros((8, 128), jnp.float32)
            imag = jnp.zeros((8, 128), jnp.float32)
            for k in range(BASIS - 1):
                b_re, b_im = basis[k, 0, plane, tile], basis[k, 1, plane, tile]
                real = real + (weight[k][0] * b_re - weight[k][1] * b_im)
                imag = imag + (weight[k][0] * b_im + weight[k][1] * b_re)
            for slab, at in goals:
                out[slab, at * TILES + tile] = real
                out[slab, (4 + at) * TILES + tile] = imag

    def middle(slab, _):
        for plane in range(2):
            solve_plane(CORE - 1 + 2 * slab + plane, ((slab, plane), (slab - 1, 2 + plane)))
        return 0

    for plane in range(2):
        solve_plane(CORE - 1 + plane, ((0, plane),))
        solve_plane(CORE + OWN - 1 + plane, ((SYSTEMS - 1, 2 + plane),))
    lax.fori_loop(1, SYSTEMS, middle, 0)


def fields_kernel(fields, forward, adjoint, terms, natural):
    half = SYSTEMS // 2
    for port in range(half):
        for part in range(2):
            for plane in range(2):
                for tile in range(TILES):
                    at = (part * 4 + 1 + plane) * TILES + tile
                    forward[port, part, plane, rows_of(tile)] = fields[port, at]
                    adjoint[port, part, plane, rows_of(tile)] = fields[half + port, at]
    for plane in range(4):
        for tile in range(TILES):
            real, imag = plane * TILES + tile, (4 + plane) * TILES + tile
            total = None
            for port in range(half):
                term = fields[port, real] * fields[half + port, real]
                term = term - fields[port, imag] * fields[half + port, imag]
                total = term if total is None else total + term
            natural[plane, rows_of(tile)] = total
    for share in range(4):
        for plane in range(4):
            terms[share, plane] = natural[plane, pl.ds(share * 8, 8)]
    flag = fields[0, 32]
    for system in range(1, SYSTEMS):
        flag = flag + fields[system, 32]
    for share in range(4):
        terms[share, 4] = flag


def density_kernel(start, place, terms, dens, out, flag):
    lane = lax.broadcasted_iota(jnp.int32, (8, 128), 1)
    updated = []
    for plane in range(4):
        total = terms[0, plane]
        for other in range(1, 4):
            total = total + terms[other, plane]
        gradient = -wave_sq * total
        where = place[0] * 2 + plane - 1
        inside = (where >= start[0]) & (where < start[0] + SYSTEMS * SYSTEMS)
        rows = dens[plane]
        moved = jnp.clip(rows - step_size * perm_span * gradient, 0.0, 1.0)
        rows = jnp.where(inside, moved, rows)
        exists = (where >= 0) & (where < 2 * SYSTEMS * SYSTEMS)
        updated.append(jnp.where(exists, rows, 0.0))
    for plane in range(2):
        own = updated[plane + 1]
        right = jnp.where(lane == 127, 0.0, pltpu.roll(own, 127, 1))
        left = jnp.where(lane == 0, 0.0, pltpu.roll(own, 1, 1))
        filtered = (2.0 * own + updated[plane + 2] + updated[plane] + right + left) / 6.0
        edge = float(np.tanh(sharpness * threshold))
        other_edge = float(np.tanh(sharpness * (1.0 - threshold)))
        out[plane] = (edge + jnp.tanh(sharpness * (filtered - threshold))) / (edge + other_edge)
    spread = terms[0, 4] + terms[1, 4] + terms[2, 4] + terms[3, 4]
    flag[0] = jnp.max(spread)


def copy_kernel(count, *refs):
    sems = refs[-1]
    arrays = refs[-1 - 2 * count : -1]
    copies = [
        pltpu.make_async_copy(arrays[at], arrays[count + at], sems.at[at]) for at in range(count)
    ]
    for copy in copies:
        copy.start()
    for copy in copies:
        copy.wait()


def row_major(mark, arrays, name):
    count = len(arrays)
    return call(
        functools.partial(copy_kernel, count),
        tuple(jax.ShapeDtypeStruct(array.shape, array.dtype) for array in arrays),
        [SMEM] + [HBM] * count,
        (HBM,) * count,
        [pltpu.SemaphoreType.DMA((count,))],
        name,
    )(mark.reshape(1), *arrays)


def on_device(background, absorb, density, profiles, adjoint_source, port_modes, design_start):
    slab = lax.axis_index("zslab")
    place = jnp.stack([slab, lax.axis_index("group")]).astype(jnp.int32)
    planes_of = [[z * SYSTEMS + l for l in range(SYSTEMS)] for z in range(SYSTEMS)]
    columns = [[z * SYSTEMS + l for z in range(SYSTEMS)] for l in range(SYSTEMS)]
    packed = call(
        pack_kernel,
        f32(SYSTEMS, BLOCK, 8, 128),
        [SMEM, SMEM, SMEM, VMEM, VMEM, VMEM, HBM, HBM],
        VMEM,
        [
            pltpu.VMEM((SYSTEMS,) + profiles.shape[1:], jnp.float32),
            pltpu.SemaphoreType.DMA((SYSTEMS,)),
        ],
        "pack",
    )(port_modes, design_start, place, background, absorb, density, profiles, adjoint_source)
    block = lax.all_to_all(packed, "zslab", 0, 0, axis_index_groups=planes_of, tiled=True)
    count = SYSTEMS * SYSTEMS
    up = [(i, i + SYSTEMS) for i in range(count - SYSTEMS)]
    down = [(target, source) for source, target in up]
    low = lax.ppermute(block[SYSTEMS // 2 :], "zslab", up)
    high = lax.ppermute(block[: SYSTEMS // 2], "zslab", down)
    inner = call(
        inner_kernel,
        (f32(SYSTEMS, 2, OWN, TILES, 8, 128), f32(2, OWN, TILES, 8, 128), f32(128, 8, 128)),
        [VMEM],
        (VMEM,) * 3,
        (),
        "inner",
        10**8,
    )(block)
    plane = (TILES, 8, 128)
    basis, gram, dens = call(
        outer_kernel,
        (f32(BASIS, 2, WINDOW, *plane), f32(1, 128), f32(4, 8, 128)),
        [SMEM] + [VMEM] * 6,
        (VMEM, VMEM, VMEM),
        [pltpu.VMEM((2, WINDOW) + plane, jnp.float32), pltpu.VMEM((128, 8, 128), jnp.float32)],
        "outer",
        2 * 10**8,
    )(place, block, low, high, *inner)
    grams = lax.all_to_all(
        jnp.broadcast_to(gram[None], (SYSTEMS, 1, 128)), "zslab", 0, 0,
        axis_index_groups=columns, tiled=True,
    )
    pick, nudge = gram_tables()
    solved = call(
        combine_kernel, f32(SYSTEMS, 33, 8, 128), [VMEM, VMEM, VMEM, VMEM], VMEM, (), "combine"
    )(grams, jnp.asarray(pick), jnp.asarray(nudge), basis)
    fields = lax.all_to_all(solved, "zslab", 0, 0, axis_index_groups=planes_of, tiled=True)
    half = f32(SYSTEMS // 2, 2, 2, 8 * TILES, 128)
    forward, adjoint, terms = call(
        fields_kernel,
        (half, half, f32(4, 5, 8, 128)),
        [VMEM],
        (VMEM,) * 3,
        [pltpu.VMEM((4, 8 * TILES, 128), jnp.float32)],
        "fields",
    )(fields)
    terms = lax.all_to_all(terms, "group", 0, 0, tiled=True)
    new_density, flag = call(
        density_kernel, (f32(2, 8, 128), f32(1)), [SMEM, SMEM, VMEM, VMEM], (VMEM, SMEM), (), "density"
    )(design_start, place, terms, dens)

    def again(state):
        held = (background, absorb, density, profiles, adjoint_source)
        held = row_major(state[0], held, "arguments")
        results = iterate_on_device(*held, port_modes, design_start)
        return (jnp.zeros((), jnp.float32),) + tuple(row_major(state[0], results, "results"))

    state = (flag[0], forward, adjoint, new_density)
    return lax.while_loop(lambda state: state[0] > 0.0, again, state)[1:]


def solution(mesh):
    return jax.shard_map(
        on_device,
        mesh=mesh,
        in_specs=(
            P("zslab", None, None),
            P("zslab", None, None),
            P("zslab", None, None),
            P(None, None, "zslab", None, None),
            P("group", None, "zslab", None, None),
            P("group"),
            P(),
        ),
        out_specs=(
            P("group", None, "zslab", None, None),
            P("group", None, "zslab", None, None),
            P("zslab", "group", None),
        ),
        check_vma=False,
    )
```

```python
import functools

import jax
import jax.numpy as jnp
import numpy as np
from jax import lax
from jax.experimental import pallas as pl
from jax.experimental.pallas import tpu as pltpu
from jax.sharding import PartitionSpec as P

ITERS = 4


wave_sq = 0.1
step_size = 2.0
perm_span = 10.0
low_perm = 2.1
sharpness = 8.0
threshold = 0.5


def with_halo(block, sides, width):
    for axis, dim in sides:
        count = lax.axis_size(axis)
        forward = [(i, i + 1) for i in range(count - 1)]
        backward = [(target, source) for source, target in forward]
        low = lax.ppermute(
            lax.slice_in_dim(block, block.shape[dim] - width, None, axis=dim), axis, forward
        )
        high = lax.ppermute(lax.slice_in_dim(block, 0, width, axis=dim), axis, backward)
        block = jnp.concatenate([low, block, high], axis=dim)
    return block


def scaled(coef, field):
    coef_re = coef[0].reshape((-1, 1, 1, 1))
    coef_im = coef[1].reshape((-1, 1, 1, 1))
    real_part = coef_re * field[:, 0] - coef_im * field[:, 1]
    imag_part = coef_re * field[:, 1] + coef_im * field[:, 0]
    return jnp.stack([real_part, imag_part], axis=1)


def product_pair(left, right):
    real_part = jnp.sum(left[:, 0] * right[:, 0] + left[:, 1] * right[:, 1], axis=(1, 2, 3))
    imag_part = jnp.sum(left[:, 0] * right[:, 1] - left[:, 1] * right[:, 0], axis=(1, 2, 3))
    return (real_part, imag_part)


def divide_pair(top, bottom):
    denominator = bottom[0] * bottom[0] + bottom[1] * bottom[1]
    return (
        (top[0] * bottom[0] + top[1] * bottom[1]) / denominator,
        (top[1] * bottom[0] - top[0] * bottom[1]) / denominator,
    )


def multiply_pair(left, right):
    return (left[0] * right[0] - left[1] * right[1], left[0] * right[1] + left[1] * right[0])


def with_planes(field):
    return with_halo(field, (("zslab", 2),), 1)


def operate(field, diag_re, diag_im):
    padded = jnp.pad(with_planes(field), ((0, 0), (0, 0), (0, 0), (1, 1), (1, 1)))
    beside = padded[:, :, 2:, 1:-1, 1:-1] + padded[:, :, :-2, 1:-1, 1:-1]
    beside = beside + padded[:, :, 1:-1, 2:, 1:-1] + padded[:, :, 1:-1, :-2, 1:-1]
    beside = beside + padded[:, :, 1:-1, 1:-1, 2:] + padded[:, :, 1:-1, 1:-1, :-2]
    real_part = diag_re * field[:, 0] - diag_im * field[:, 1]
    imag_part = diag_re * field[:, 1] + diag_im * field[:, 0]
    return jnp.stack([real_part, imag_part], axis=1) - beside


def bicgstab(sources, diag_re, diag_im):
    solution = jnp.zeros_like(sources)
    residual = sources
    direction = sources
    bilinear = lax.psum(product_pair(sources, residual), "zslab")
    for iteration in range(ITERS):
        image = operate(direction, diag_re, diag_im)
        along = lax.psum(product_pair(sources, image), "zslab")
        advance = divide_pair(bilinear, along)
        halfway = residual - scaled(advance, image)
        second = operate(halfway, diag_re, diag_im)
        cross_re, cross_im = product_pair(second, halfway)
        energy = jnp.sum(second[:, 0] * second[:, 0] + second[:, 1] * second[:, 1], axis=(1, 2, 3))
        cross_re, cross_im, energy = lax.psum((cross_re, cross_im, energy), "zslab")
        relax_coef = (cross_re / energy, cross_im / energy)
        solution = solution + scaled(advance, direction) + scaled(relax_coef, halfway)
        residual = halfway - scaled(relax_coef, second)
        if iteration + 1 < ITERS:
            bilinear_new = lax.psum(product_pair(sources, residual), "zslab")
        if iteration + 1 < ITERS:
            blend_coef = multiply_pair(
                divide_pair(bilinear_new, bilinear), divide_pair(advance, relax_coef)
            )
            direction = residual + scaled(blend_coef, direction - scaled(relax_coef, image))
            bilinear = bilinear_new
    return solution


def iterate_on_device(background, absorb, density, profiles, adjoint_source, port_modes, design_start):
    planes_dev = density.shape[0]
    rows_all = density.shape[1]
    first_plane = lax.axis_index("zslab") * planes_dev
    design_depth = planes_dev * lax.axis_size("zslab") // 2
    planes = first_plane + jnp.arange(planes_dev)
    in_design = (planes >= design_start[0]) & (planes < design_start[0] + design_depth)
    in_design = in_design[:, None, None]
    permittivity = jnp.where(in_design, low_perm + perm_span * density, background)
    diag_re = 6.0 - wave_sq * permittivity
    selector = (port_modes[:, None] == jnp.arange(profiles.shape[0])[None, :]).astype(jnp.float32)
    forward_source = jnp.einsum(
        "pm,mczyx->pczyx", selector, profiles, precision=lax.Precision.HIGHEST
    )
    port_count = forward_source.shape[0]
    sources = jnp.concatenate([forward_source, adjoint_source], axis=0)
    fields = bicgstab(sources, diag_re, absorb)
    forward_field = fields[:port_count]
    adjoint_field = fields[port_count:]
    terms = forward_field[:, 0] * adjoint_field[:, 0] - forward_field[:, 1] * adjoint_field[:, 1]
    local_term = -wave_sq * jnp.sum(terms, axis=0)
    rows_share = rows_all // lax.axis_size("group")
    row_start = lax.axis_index("group") * rows_share
    total = lax.psum(local_term, "group")
    gradient = lax.dynamic_slice_in_dim(total, row_start, rows_share, 1)
    density_rows = lax.dynamic_slice_in_dim(density, row_start, rows_share, 1)
    updated = jnp.where(
        in_design, jnp.clip(density_rows - step_size * perm_span * gradient, 0.0, 1.0), density_rows
    )
    extended = with_halo(updated, (("zslab", 0),), 1)
    padded = jnp.pad(extended, ((0, 0), (0, 0), (1, 1)))
    filtered = (
        2.0 * updated
        + padded[2:, :, 1:-1]
        + padded[:-2, :, 1:-1]
        + padded[1:-1, :, 2:]
        + padded[1:-1, :, :-2]
    ) / 6.0
    new_density = (
        jnp.tanh(sharpness * threshold) + jnp.tanh(sharpness * (filtered - threshold))
    ) / (jnp.tanh(sharpness * threshold) + jnp.tanh(sharpness * (1.0 - threshold)))
    return (forward_field, adjoint_field, new_density)


BASIS = 2 * ITERS + 1
CENTRE = 5.3
HALF_RADIUS = 3.0
THIRD = 1.0 / HALF_RADIUS
NUDGE = 1e-6
AGREE = 5e-4
ROWS = 16 * BASIS


def pair_places():
    real, imag, place = {}, {}, 0
    for j in range(BASIS):
        for i in range(j + 1):
            real[(i, j)] = place
            place += 1
    for j in range(BASIS):
        for i in range(j):
            imag[(i, j)] = place
            place += 1
    return real, imag


def gram_tables():
    real, imag = pair_places()
    pick = np.zeros((6 * ROWS, 128), np.float32)
    nudge = np.zeros((2 * ROWS, 128), np.float32)
    rng = np.random.default_rng(7)
    sign_re = {pair: np.where(rng.random(128) < 0.5, -1.0, 1.0) for pair in real}
    sign_im = {pair: np.where(rng.random(128) < 0.5, -1.0, 1.0) for pair in imag}
    for j in range(BASIS):
        for i in range(BASIS):
            row, pair = j * 16 + i, (min(i, j), max(i, j))
            pick[row, real[pair]] = 1.0
            for half in (0, ROWS):
                pick[2 * ROWS + half + row, real[(i, i)]] = 1.0
                pick[4 * ROWS + half + row, real[(j, j)]] = 1.0
            nudge[row] = NUDGE * sign_re[pair]
            if i != j:
                side = 1.0 if i < j else -1.0
                pick[ROWS + row, imag[pair]] = side
                nudge[ROWS + row] = NUDGE * side * sign_im[pair]
    nudge[:, 0] = 0.0
    return pick, nudge


def exact_dot(left, right, dims):
    return lax.dot_general(
        left, right, (dims, ((), ())), precision=lax.Precision.HIGHEST,
        preferred_element_type=jnp.float32,
    )


def minus_pair(left, right):
    return (left[0] - right[0], left[1] - right[1])


def plus_pair(left, right):
    return (left[0] + right[0], left[1] + right[1])


def coefficients(gram):
    gram_re = [gram[16 * j : 16 * j + 16] for j in range(BASIS)]
    gram_im = [gram[ROWS + 16 * j : ROWS + 16 * j + 16] for j in range(BASIS)]
    row = lax.broadcasted_iota(jnp.int32, (16, 128), 0)
    keep = jnp.where(row == 15, 0.0, HALF_RADIUS)

    def apply(q):
        return tuple(
            CENTRE * v + HALF_RADIUS * pltpu.roll(v, 1, 0) + keep * pltpu.roll(v, 15, 0) for v in q
        )

    def total(v):
        return jnp.sum(v, axis=0, keepdims=True)

    def with_source(q):
        return (
            total(gram_re[0] * q[0] + gram_im[0] * q[1]),
            total(gram_re[0] * q[1] - gram_im[0] * q[0]),
        )

    def times_gram(q):
        out_re = jnp.zeros((16, 128), jnp.float32)
        out_im = jnp.zeros((16, 128), jnp.float32)
        for j in range(BASIS):
            q_re, q_im = q[0][j : j + 1], q[1][j : j + 1]
            out_re = out_re + (gram_re[j] * q_re - gram_im[j] * q_im)
            out_im = out_im + (gram_re[j] * q_im + gram_im[j] * q_re)
        return out_re, out_im

    one = jnp.where(row == 0, 1.0, 0.0)
    zero = jnp.zeros((16, 128), jnp.float32)
    answer, residual, direction = (zero, zero), (one, zero), (one, zero)
    bilinear = with_source(residual)
    for iteration in range(ITERS):
        image = apply(direction)
        advance = divide_pair(bilinear, with_source(image))
        halfway = minus_pair(residual, multiply_pair(advance, image))
        second = apply(halfway)
        weighed = times_gram(second)
        energy = total(second[0] * weighed[0] + second[1] * weighed[1])
        relax = (
            total(weighed[0] * halfway[0] + weighed[1] * halfway[1]) / energy,
            total(weighed[0] * halfway[1] - weighed[1] * halfway[0]) / energy,
        )
        answer = plus_pair(
            answer, plus_pair(multiply_pair(advance, direction), multiply_pair(relax, halfway))
        )
        if iteration + 1 < ITERS:
            residual = minus_pair(halfway, multiply_pair(relax, second))
            bilinear_new = with_source(residual)
            blend = multiply_pair(divide_pair(bilinear_new, bilinear), divide_pair(advance, relax))
            direction = plus_pair(
                residual, multiply_pair(blend, minus_pair(direction, multiply_pair(relax, image)))
            )
            bilinear = bilinear_new
    first = tuple(jnp.broadcast_to(v[:, :1], v.shape) for v in answer)
    apart = minus_pair(answer, first)

    def norm(q):
        weighed = times_gram(q)
        return total(q[0] * weighed[0] + q[1] * weighed[1])

    return first, norm(apart), norm(first)


TILES = 4
SYSTEMS = 8
BLOCK = 16 * TILES // 2 + 2
OWN = 16
WINDOW = 32
CORE = 8
VMEM = pl.BlockSpec(memory_space=pltpu.VMEM)
SMEM = pl.BlockSpec(memory_space=pltpu.SMEM)
HBM = pl.BlockSpec(memory_space=pltpu.HBM)
LIMIT = 24 * 1024 * 1024


def call(kernel, outs, specs, out_specs, scratch=(), name=None, flops=0):
    return pl.pallas_call(
        kernel,
        out_shape=outs,
        in_specs=specs,
        out_specs=out_specs,
        scratch_shapes=list(scratch),
        compiler_params=pltpu.CompilerParams(vmem_limit_bytes=LIMIT),
        cost_estimate=pl.CostEstimate(flops=flops, bytes_accessed=1 << 20, transcendentals=0),
        name=name,
    )


def f32(*shape):
    return jax.ShapeDtypeStruct(shape, jnp.float32)


def rows_of(tile):
    return pl.ds(tile, 8, stride=TILES)


def pack_kernel(modes, start, place, background, absorb, density, profiles, adjoint, out, raw, sems):
    half = SYSTEMS // 2
    copies = []
    for system in range(SYSTEMS):
        source = profiles.at[modes[system]] if system < half else adjoint.at[system - half]
        copies.append(pltpu.make_async_copy(source, raw.at[system], sems.at[system]))
    for copy in copies:
        copy.start()
    for plane in range(2):
        where = place[0] * 2 + plane
        inside = (where >= start[0]) & (where < start[0] + SYSTEMS * SYSTEMS)
        for tile in range(TILES):
            rows = rows_of(tile)
            perm = jnp.where(
                inside, low_perm + perm_span * density[plane, rows], background[plane, rows]
            )
            diag_re = ((6.0 - wave_sq * perm) - CENTRE) * THIRD
            diag_im = absorb[plane, rows] * THIRD
            for system in range(SYSTEMS):
                out[system, 16 + plane * TILES + tile] = diag_re
                out[system, 24 + plane * TILES + tile] = diag_im
        share = density[plane, pl.ds(pl.multiple_of(place[1] * 8, 8), 8)]
        for system in range(SYSTEMS):
            out[system, 32 + plane] = share
    for system in range(SYSTEMS):
        copies[system].wait()
        for part in range(2):
            for plane in range(2):
                for tile in range(TILES):
                    out[system, (part * 2 + plane) * TILES + tile] = raw[
                        system, part, plane, rows_of(tile)
                    ]


class Stencil:
    def __init__(self):
        row = lax.broadcasted_iota(jnp.int32, (8, 128), 0)
        lane = lax.broadcasted_iota(jnp.int32, (8, 128), 1)
        self.first_row, self.last_row = row == 0, row == 7
        self.first_lane, self.last_lane = lane == 0, lane == 127

    def beside(self, below, here, above):
        up = jnp.where(self.first_row, 0.0, pltpu.roll(here[TILES - 1], 1, 0))
        down = jnp.where(self.last_row, 0.0, pltpu.roll(here[0], 7, 0))
        rows = [up] + list(here) + [down]
        sums = []
        for tile in range(TILES):
            left = jnp.where(self.first_lane, 0.0, pltpu.roll(here[tile], 1, 1))
            right = jnp.where(self.last_lane, 0.0, pltpu.roll(here[tile], 127, 1))
            z_sum = below[tile] + above[tile]
            sums.append((z_sum + (rows[tile] + rows[tile + 2])) + (left + right))
        return sums

    def step(self, basis, diag, level, at, third):
        def plane(part, where):
            return [basis[level, part, where, tile] for tile in range(TILES)]

        real, imag = plane(0, at), plane(1, at)
        near_re = self.beside(plane(0, at - 1), real, plane(0, at + 1))
        near_im = self.beside(plane(1, at - 1), imag, plane(1, at + 1))
        for tile in range(TILES):
            diag_re, diag_im = diag[0, at, tile], diag[1, at, tile]
            new_re = diag_re * real[tile] - diag_im * imag[tile] - third * near_re[tile]
            new_im = diag_re * imag[tile] + diag_im * real[tile] - third * near_im[tile]
            if level > 0:
                new_re = new_re - basis[level - 1, 0, at, tile]
                new_im = new_im - basis[level - 1, 1, at, tile]
            basis[level + 1, 0, at, tile] = new_re
            basis[level + 1, 1, at, tile] = new_im


def gram_pass(basis, acc, columns, ranges, shift):
    real_at, imag_at = pair_places()
    pairs = [(i, j) for j in columns for i in range(j + 1)]
    top = max(columns) + 1
    places = []
    for pair in pairs:
        places.append(real_at[pair])
        if pair[0] != pair[1]:
            places.append(imag_at[pair])

    def position(step, sums, first=0):
        window, tile = first + shift + step // TILES, step % TILES
        field = [(basis[k, 0, window, tile], basis[k, 1, window, tile]) for k in range(top)]
        new = []
        for i, j in pairs:
            (i_re, i_im), (j_re, j_im) = field[i], field[j]
            new.append(i_re * j_re + i_im * j_im)
            if i != j:
                new.append(i_re * j_im - i_im * j_re)
        return tuple(total + term for total, term in zip(sums, new))

    sums = tuple(acc[at] for at in places)
    for first, last in ranges:
        sums = lax.fori_loop(
            0, (last - first) * TILES, functools.partial(position, first=first), sums,
            unroll=TILES,
        )
    for at, value in zip(places, sums):
        acc[at] = value


def inner_kernel(block, basis, diag, acc):
    def load(chunk, _):
        for plane in range(2):
            for part in range(2):
                for tile in range(TILES):
                    at = part * 8 + plane * TILES + tile
                    basis[0, part, 2 * chunk + plane, tile] = block[chunk, at]
                    diag[part, 2 * chunk + plane, tile] = block[chunk, 16 + at]
        return 0

    lax.fori_loop(0, SYSTEMS, load, 0)
    stencil = Stencil()
    for level in range(SYSTEMS - 1):

        def plane_step(at, _, level=level):
            stencil.step(basis, diag, level, at, THIRD)
            return 0

        lax.fori_loop(
            level + 1, OWN - 1 - level, plane_step, 0, unroll=OWN - 2 - 2 * level
        )
    acc[...] = jnp.zeros_like(acc)
    for columns, ranges in INNER_PASSES:
        gram_pass(basis, acc, columns, ranges, 0)


INNER_PASSES = (
    ((0, 1, 2, 3, 4), ((4, 12),)),
    ((0, 1, 2), ((2, 4), (12, 14))),
    ((5, 6), ((6, 10),)),
)
OUTER_PASSES = (
    ((0, 1, 2, 3, 4), ((0, 2), (14, 16))),
    ((3, 4), ((2, 4), (12, 14))),
    ((5, 6), ((0, 6), (10, 16))),
    ((7,), ((0, 16),)),
    ((8,), ((0, 16),)),
)


def outer_kernel(place, block, low, high, inner, inner_diag, inner_acc, basis, gram, dens, diag, acc):
    def load(source, chunks, at):
        def one(chunk, _):
            for plane in range(2):
                window = at + 2 * chunk + plane
                for part in range(2):
                    for tile in range(TILES):
                        spot = part * 8 + plane * TILES + tile
                        basis[0, part, window, tile] = source[chunk, spot]
                        diag[part, window, tile] = source[chunk, 16 + spot]
            return 0

        lax.fori_loop(0, chunks, one, 0)

    load(low, SYSTEMS // 2, 0)
    load(high, SYSTEMS // 2, CORE + OWN)
    for level in range(SYSTEMS):

        def keep(at, _, level=level):
            for part in range(2):
                for tile in range(TILES):
                    basis[level, part, CORE + at, tile] = inner[level, part, at, tile]
                    if level == 0:
                        diag[part, CORE + at, tile] = inner_diag[part, at, tile]
            return 0

        lax.fori_loop(level, OWN - level, keep, 0, unroll=2)
    acc[...] = inner_acc[...]

    me = place[0] % SYSTEMS
    dens[0] = jnp.where(me > 0, block[jnp.maximum(me - 1, 0), 33], low[SYSTEMS // 2 - 1, 33])
    dens[1] = block[me, 32]
    dens[2] = block[me, 33]
    dens[3] = jnp.where(
        me < SYSTEMS - 1, block[jnp.minimum(me + 1, SYSTEMS - 1), 32], high[0, 32]
    )

    third_low = jnp.where(place[0] >= SYSTEMS, THIRD, 0.0)
    third_high = jnp.where(place[0] < SYSTEMS * (SYSTEMS - 1), THIRD, 0.0)
    stencil = Stencil()
    for level in range(BASIS - 1):

        def two_planes(step, _, level=level):
            lower, upper = level + 1 + step, WINDOW - 2 - level - step
            stencil.step(basis, diag, level, lower, jnp.where(lower < CORE, third_low, THIRD))
            stencil.step(
                basis, diag, level, upper, jnp.where(upper >= CORE + OWN, third_high, THIRD)
            )
            return 0

        lax.fori_loop(0, CORE, two_planes, 0, unroll=CORE)
    for columns, ranges in OUTER_PASSES:
        gram_pass(basis, acc, columns, ranges, CORE)
    by_pair = jnp.sum(acc[...], axis=1)
    ones = jnp.ones((8, 128), jnp.float32)
    gram[...] = exact_dot(ones, by_pair, ((1,), (1,)))[0:1]


def combine_kernel(grams, pick, nudge, basis, out):
    row = grams[0]
    for other in range(1, SYSTEMS):
        row = row + grams[other]
    ones = jnp.ones((128, 128), jnp.float32)
    picked = exact_dot(pick[...] * row, ones, ((1,), (0,)))
    norms = jnp.sqrt(picked[2 * ROWS : 4 * ROWS] * picked[4 * ROWS :])
    answer, apart, size = coefficients(picked[: 2 * ROWS] + nudge[...] * norms)
    agrees = jnp.max(jnp.where(apart <= AGREE * AGREE * size, 0.0, 1.0))
    flag = jnp.zeros((8, 128), jnp.float32) + agrees
    for slab in range(SYSTEMS):
        out[slab, 32] = flag
    weight = [
        (
            jnp.broadcast_to(answer[0][k : k + 1], (8, 128)),
            jnp.broadcast_to(answer[1][k : k + 1], (8, 128)),
        )
        for k in range(BASIS - 1)
    ]

    def solve_plane(plane, goals):
        for tile in range(TILES):
            real = jnp.zeros((8, 128), jnp.float32)
            imag = jnp.zeros((8, 128), jnp.float32)
            for k in range(BASIS - 1):
                b_re, b_im = basis[k, 0, plane, tile], basis[k, 1, plane, tile]
                real = real + (weight[k][0] * b_re - weight[k][1] * b_im)
                imag = imag + (weight[k][0] * b_im + weight[k][1] * b_re)
            for slab, at in goals:
                out[slab, at * TILES + tile] = real
                out[slab, (4 + at) * TILES + tile] = imag

    def middle(slab, _):
        for plane in range(2):
            solve_plane(CORE - 1 + 2 * slab + plane, ((slab, plane), (slab - 1, 2 + plane)))
        return 0

    for plane in range(2):
        solve_plane(CORE - 1 + plane, ((0, plane),))
        solve_plane(CORE + OWN - 1 + plane, ((SYSTEMS - 1, 2 + plane),))
    lax.fori_loop(1, SYSTEMS, middle, 0)


def fields_kernel(fields, forward, adjoint, terms, natural):
    half = SYSTEMS // 2
    for port in range(half):
        for part in range(2):
            for plane in range(2):
                for tile in range(TILES):
                    at = (part * 4 + 1 + plane) * TILES + tile
                    forward[port, part, plane, rows_of(tile)] = fields[port, at]
                    adjoint[port, part, plane, rows_of(tile)] = fields[half + port, at]
    for plane in range(4):
        for tile in range(TILES):
            real, imag = plane * TILES + tile, (4 + plane) * TILES + tile
            total = None
            for port in range(half):
                term = fields[port, real] * fields[half + port, real]
                term = term - fields[port, imag] * fields[half + port, imag]
                total = term if total is None else total + term
            natural[plane, rows_of(tile)] = total
    for share in range(4):
        for plane in range(4):
            terms[share, plane] = natural[plane, pl.ds(share * 8, 8)]
    flag = fields[0, 32]
    for system in range(1, SYSTEMS):
        flag = flag + fields[system, 32]
    for share in range(4):
        terms[share, 4] = flag


def density_kernel(start, place, terms, dens, out, flag):
    lane = lax.broadcasted_iota(jnp.int32, (8, 128), 1)
    updated = []
    for plane in range(4):
        total = terms[0, plane]
        for other in range(1, 4):
            total = total + terms[other, plane]
        gradient = -wave_sq * total
        where = place[0] * 2 + plane - 1
        inside = (where >= start[0]) & (where < start[0] + SYSTEMS * SYSTEMS)
        rows = dens[plane]
        moved = jnp.clip(rows - step_size * perm_span * gradient, 0.0, 1.0)
        rows = jnp.where(inside, moved, rows)
        exists = (where >= 0) & (where < 2 * SYSTEMS * SYSTEMS)
        updated.append(jnp.where(exists, rows, 0.0))
    for plane in range(2):
        own = updated[plane + 1]
        right = jnp.where(lane == 127, 0.0, pltpu.roll(own, 127, 1))
        left = jnp.where(lane == 0, 0.0, pltpu.roll(own, 1, 1))
        filtered = (2.0 * own + updated[plane + 2] + updated[plane] + right + left) / 6.0
        edge = float(np.tanh(sharpness * threshold))
        other_edge = float(np.tanh(sharpness * (1.0 - threshold)))
        out[plane] = (edge + jnp.tanh(sharpness * (filtered - threshold))) / (edge + other_edge)
    spread = terms[0, 4] + terms[1, 4] + terms[2, 4] + terms[3, 4]
    flag[0] = jnp.max(spread)


def copy_kernel(count, *refs):
    sems = refs[-1]
    arrays = refs[-1 - 2 * count : -1]
    copies = [
        pltpu.make_async_copy(arrays[at], arrays[count + at], sems.at[at]) for at in range(count)
    ]
    for copy in copies:
        copy.start()
    for copy in copies:
        copy.wait()


def row_major(mark, arrays, name):
    count = len(arrays)
    return call(
        functools.partial(copy_kernel, count),
        tuple(jax.ShapeDtypeStruct(array.shape, array.dtype) for array in arrays),
        [SMEM] + [HBM] * count,
        (HBM,) * count,
        [pltpu.SemaphoreType.DMA((count,))],
        name,
    )(mark.reshape(1), *arrays)


def on_device(background, absorb, density, profiles, adjoint_source, port_modes, design_start):
    slab = lax.axis_index("zslab")
    place = jnp.stack([slab, lax.axis_index("group")]).astype(jnp.int32)
    planes_of = [[z * SYSTEMS + l for l in range(SYSTEMS)] for z in range(SYSTEMS)]
    columns = [[z * SYSTEMS + l for z in range(SYSTEMS)] for l in range(SYSTEMS)]
    packed = call(
        pack_kernel,
        f32(SYSTEMS, BLOCK, 8, 128),
        [SMEM, SMEM, SMEM, VMEM, VMEM, VMEM, HBM, HBM],
        VMEM,
        [
            pltpu.VMEM((SYSTEMS,) + profiles.shape[1:], jnp.float32),
            pltpu.SemaphoreType.DMA((SYSTEMS,)),
        ],
        "pack",
    )(port_modes, design_start, place, background, absorb, density, profiles, adjoint_source)
    block = lax.all_to_all(packed, "zslab", 0, 0, axis_index_groups=planes_of, tiled=True)
    count = SYSTEMS * SYSTEMS
    up = [(i, i + SYSTEMS) for i in range(count - SYSTEMS)]
    down = [(target, source) for source, target in up]
    low = lax.ppermute(block[SYSTEMS // 2 :], "zslab", up)
    high = lax.ppermute(block[: SYSTEMS // 2], "zslab", down)
    inner = call(
        inner_kernel,
        (f32(SYSTEMS, 2, OWN, TILES, 8, 128), f32(2, OWN, TILES, 8, 128), f32(128, 8, 128)),
        [VMEM],
        (VMEM,) * 3,
        (),
        "inner",
        10**8,
    )(block)
    plane = (TILES, 8, 128)
    basis, gram, dens = call(
        outer_kernel,
        (f32(BASIS, 2, WINDOW, *plane), f32(1, 128), f32(4, 8, 128)),
        [SMEM] + [VMEM] * 6,
        (VMEM, VMEM, VMEM),
        [pltpu.VMEM((2, WINDOW) + plane, jnp.float32), pltpu.VMEM((128, 8, 128), jnp.float32)],
        "outer",
        2 * 10**8,
    )(place, block, low, high, *inner)
    grams = lax.all_to_all(
        jnp.broadcast_to(gram[None], (SYSTEMS, 1, 128)), "zslab", 0, 0,
        axis_index_groups=columns, tiled=True,
    )
    pick, nudge = gram_tables()
    solved = call(
        combine_kernel, f32(SYSTEMS, 33, 8, 128), [VMEM, VMEM, VMEM, VMEM], VMEM, (), "combine"
    )(grams, jnp.asarray(pick), jnp.asarray(nudge), basis)
    fields = lax.all_to_all(solved, "zslab", 0, 0, axis_index_groups=planes_of, tiled=True)
    half = f32(SYSTEMS // 2, 2, 2, 8 * TILES, 128)
    forward, adjoint, terms = call(
        fields_kernel,
        (half, half, f32(4, 5, 8, 128)),
        [VMEM],
        (VMEM,) * 3,
        [pltpu.VMEM((4, 8 * TILES, 128), jnp.float32)],
        "fields",
    )(fields)
    terms = lax.all_to_all(terms, "group", 0, 0, tiled=True)
    new_density, flag = call(
        density_kernel, (f32(2, 8, 128), f32(1)), [SMEM, SMEM, VMEM, VMEM], (VMEM, SMEM), (), "density"
    )(design_start, place, terms, dens)

    def again(state):
        held = (background, absorb, density, profiles, adjoint_source)
        held = row_major(state[0], held, "arguments")
        results = iterate_on_device(*held, port_modes, design_start)
        return (jnp.zeros((), jnp.float32),) + tuple(row_major(state[0], results, "results"))

    state = (flag[0], forward, adjoint, new_density)
    return lax.while_loop(lambda state: state[0] > 0.0, again, state)[1:]


def solution(mesh):
    return jax.shard_map(
        on_device,
        mesh=mesh,
        in_specs=(
            P("zslab", None, None),
            P("zslab", None, None),
            P("zslab", None, None),
            P(None, None, "zslab", None, None),
            P("group", None, "zslab", None, None),
            P("group"),
            P(),
        ),
        out_specs=(
            P("group", None, "zslab", None, None),
            P("group", None, "zslab", None, None),
            P("zslab", "group", None),
        ),
        check_vma=False,
    )
```

```python
import functools

import jax
import jax.numpy as jnp
import numpy as np
from jax import lax
from jax.experimental import pallas as pl
from jax.experimental.pallas import tpu as pltpu
from jax.sharding import PartitionSpec as P

ITERS = 4


wave_sq = 0.1
step_size = 2.0
perm_span = 10.0
low_perm = 2.1
sharpness = 8.0
threshold = 0.5


def with_halo(block, sides, width):
    for axis, dim in sides:
        count = lax.axis_size(axis)
        forward = [(i, i + 1) for i in range(count - 1)]
        backward = [(target, source) for source, target in forward]
        low = lax.ppermute(
            lax.slice_in_dim(block, block.shape[dim] - width, None, axis=dim), axis, forward
        )
        high = lax.ppermute(lax.slice_in_dim(block, 0, width, axis=dim), axis, backward)
        block = jnp.concatenate([low, block, high], axis=dim)
    return block


def scaled(coef, field):
    coef_re = coef[0].reshape((-1, 1, 1, 1))
    coef_im = coef[1].reshape((-1, 1, 1, 1))
    real_part = coef_re * field[:, 0] - coef_im * field[:, 1]
    imag_part = coef_re * field[:, 1] + coef_im * field[:, 0]
    return jnp.stack([real_part, imag_part], axis=1)


def product_pair(left, right):
    real_part = jnp.sum(left[:, 0] * right[:, 0] + left[:, 1] * right[:, 1], axis=(1, 2, 3))
    imag_part = jnp.sum(left[:, 0] * right[:, 1] - left[:, 1] * right[:, 0], axis=(1, 2, 3))
    return (real_part, imag_part)


def divide_pair(top, bottom):
    denominator = bottom[0] * bottom[0] + bottom[1] * bottom[1]
    return (
        (top[0] * bottom[0] + top[1] * bottom[1]) / denominator,
        (top[1] * bottom[0] - top[0] * bottom[1]) / denominator,
    )


def multiply_pair(left, right):
    return (left[0] * right[0] - left[1] * right[1], left[0] * right[1] + left[1] * right[0])


def with_planes(field):
    return with_halo(field, (("zslab", 2),), 1)


def operate(field, diag_re, diag_im):
    padded = jnp.pad(with_planes(field), ((0, 0), (0, 0), (0, 0), (1, 1), (1, 1)))
    beside = padded[:, :, 2:, 1:-1, 1:-1] + padded[:, :, :-2, 1:-1, 1:-1]
    beside = beside + padded[:, :, 1:-1, 2:, 1:-1] + padded[:, :, 1:-1, :-2, 1:-1]
    beside = beside + padded[:, :, 1:-1, 1:-1, 2:] + padded[:, :, 1:-1, 1:-1, :-2]
    real_part = diag_re * field[:, 0] - diag_im * field[:, 1]
    imag_part = diag_re * field[:, 1] + diag_im * field[:, 0]
    return jnp.stack([real_part, imag_part], axis=1) - beside


def bicgstab(sources, diag_re, diag_im):
    solution = jnp.zeros_like(sources)
    residual = sources
    direction = sources
    bilinear = lax.psum(product_pair(sources, residual), "zslab")
    for iteration in range(ITERS):
        image = operate(direction, diag_re, diag_im)
        along = lax.psum(product_pair(sources, image), "zslab")
        advance = divide_pair(bilinear, along)
        halfway = residual - scaled(advance, image)
        second = operate(halfway, diag_re, diag_im)
        cross_re, cross_im = product_pair(second, halfway)
        energy = jnp.sum(second[:, 0] * second[:, 0] + second[:, 1] * second[:, 1], axis=(1, 2, 3))
        cross_re, cross_im, energy = lax.psum((cross_re, cross_im, energy), "zslab")
        relax_coef = (cross_re / energy, cross_im / energy)
        solution = solution + scaled(advance, direction) + scaled(relax_coef, halfway)
        residual = halfway - scaled(relax_coef, second)
        if iteration + 1 < ITERS:
            bilinear_new = lax.psum(product_pair(sources, residual), "zslab")
        if iteration + 1 < ITERS:
            blend_coef = multiply_pair(
                divide_pair(bilinear_new, bilinear), divide_pair(advance, relax_coef)
            )
            direction = residual + scaled(blend_coef, direction - scaled(relax_coef, image))
            bilinear = bilinear_new
    return solution


def iterate_on_device(background, absorb, density, profiles, adjoint_source, port_modes, design_start):
    planes_dev = density.shape[0]
    rows_all = density.shape[1]
    first_plane = lax.axis_index("zslab") * planes_dev
    design_depth = planes_dev * lax.axis_size("zslab") // 2
    planes = first_plane + jnp.arange(planes_dev)
    in_design = (planes >= design_start[0]) & (planes < design_start[0] + design_depth)
    in_design = in_design[:, None, None]
    permittivity = jnp.where(in_design, low_perm + perm_span * density, background)
    diag_re = 6.0 - wave_sq * permittivity
    selector = (port_modes[:, None] == jnp.arange(profiles.shape[0])[None, :]).astype(jnp.float32)
    forward_source = jnp.einsum(
        "pm,mczyx->pczyx", selector, profiles, precision=lax.Precision.HIGHEST
    )
    port_count = forward_source.shape[0]
    sources = jnp.concatenate([forward_source, adjoint_source], axis=0)
    fields = bicgstab(sources, diag_re, absorb)
    forward_field = fields[:port_count]
    adjoint_field = fields[port_count:]
    terms = forward_field[:, 0] * adjoint_field[:, 0] - forward_field[:, 1] * adjoint_field[:, 1]
    local_term = -wave_sq * jnp.sum(terms, axis=0)
    rows_share = rows_all // lax.axis_size("group")
    row_start = lax.axis_index("group") * rows_share
    total = lax.psum(local_term, "group")
    gradient = lax.dynamic_slice_in_dim(total, row_start, rows_share, 1)
    density_rows = lax.dynamic_slice_in_dim(density, row_start, rows_share, 1)
    updated = jnp.where(
        in_design, jnp.clip(density_rows - step_size * perm_span * gradient, 0.0, 1.0), density_rows
    )
    extended = with_halo(updated, (("zslab", 0),), 1)
    padded = jnp.pad(extended, ((0, 0), (0, 0), (1, 1)))
    filtered = (
        2.0 * updated
        + padded[2:, :, 1:-1]
        + padded[:-2, :, 1:-1]
        + padded[1:-1, :, 2:]
        + padded[1:-1, :, :-2]
    ) / 6.0
    new_density = (
        jnp.tanh(sharpness * threshold) + jnp.tanh(sharpness * (filtered - threshold))
    ) / (jnp.tanh(sharpness * threshold) + jnp.tanh(sharpness * (1.0 - threshold)))
    return (forward_field, adjoint_field, new_density)


BASIS = 2 * ITERS + 1
CENTRE = 5.3
HALF_RADIUS = 3.0
THIRD = 1.0 / HALF_RADIUS
NUDGE = 1e-6
AGREE = 5e-4
ROWS = 16 * BASIS


def pair_places():
    real, imag, place = {}, {}, 0
    for j in range(BASIS):
        for i in range(j + 1):
            real[(i, j)] = place
            place += 1
    for j in range(BASIS):
        for i in range(j):
            imag[(i, j)] = place
            place += 1
    return real, imag


def gram_tables():
    real, imag = pair_places()
    pick = np.zeros((6 * ROWS, 128), np.float32)
    nudge = np.zeros((2 * ROWS, 128), np.float32)
    rng = np.random.default_rng(7)
    sign_re = {pair: np.where(rng.random(128) < 0.5, -1.0, 1.0) for pair in real}
    sign_im = {pair: np.where(rng.random(128) < 0.5, -1.0, 1.0) for pair in imag}
    for j in range(BASIS):
        for i in range(BASIS):
            row, pair = j * 16 + i, (min(i, j), max(i, j))
            pick[row, real[pair]] = 1.0
            for half in (0, ROWS):
                pick[2 * ROWS + half + row, real[(i, i)]] = 1.0
                pick[4 * ROWS + half + row, real[(j, j)]] = 1.0
            nudge[row] = NUDGE * sign_re[pair]
            if i != j:
                side = 1.0 if i < j else -1.0
                pick[ROWS + row, imag[pair]] = side
                nudge[ROWS + row] = NUDGE * side * sign_im[pair]
    nudge[:, 0] = 0.0
    return pick, nudge


def exact_dot(left, right, dims):
    return lax.dot_general(
        left, right, (dims, ((), ())), precision=lax.Precision.HIGHEST,
        preferred_element_type=jnp.float32,
    )


def minus_pair(left, right):
    return (left[0] - right[0], left[1] - right[1])


def plus_pair(left, right):
    return (left[0] + right[0], left[1] + right[1])


def coefficients(gram):
    gram_re = [gram[16 * j : 16 * j + 16] for j in range(BASIS)]
    gram_im = [gram[ROWS + 16 * j : ROWS + 16 * j + 16] for j in range(BASIS)]
    row = lax.broadcasted_iota(jnp.int32, (16, 128), 0)
    keep = jnp.where(row == 15, 0.0, HALF_RADIUS)

    def apply(q):
        return tuple(
            CENTRE * v + HALF_RADIUS * pltpu.roll(v, 1, 0) + keep * pltpu.roll(v, 15, 0) for v in q
        )

    def total(v):
        return jnp.sum(v, axis=0, keepdims=True)

    def with_source(q):
        return (
            total(gram_re[0] * q[0] + gram_im[0] * q[1]),
            total(gram_re[0] * q[1] - gram_im[0] * q[0]),
        )

    def times_gram(q):
        out_re = jnp.zeros((16, 128), jnp.float32)
        out_im = jnp.zeros((16, 128), jnp.float32)
        for j in range(BASIS):
            q_re, q_im = q[0][j : j + 1], q[1][j : j + 1]
            out_re = out_re + (gram_re[j] * q_re - gram_im[j] * q_im)
            out_im = out_im + (gram_re[j] * q_im + gram_im[j] * q_re)
        return out_re, out_im

    one = jnp.where(row == 0, 1.0, 0.0)
    zero = jnp.zeros((16, 128), jnp.float32)
    answer, residual, direction = (zero, zero), (one, zero), (one, zero)
    bilinear = with_source(residual)
    for iteration in range(ITERS):
        image = apply(direction)
        advance = divide_pair(bilinear, with_source(image))
        halfway = minus_pair(residual, multiply_pair(advance, image))
        second = apply(halfway)
        weighed = times_gram(second)
        energy = total(second[0] * weighed[0] + second[1] * weighed[1])
        relax = (
            total(weighed[0] * halfway[0] + weighed[1] * halfway[1]) / energy,
            total(weighed[0] * halfway[1] - weighed[1] * halfway[0]) / energy,
        )
        answer = plus_pair(
            answer, plus_pair(multiply_pair(advance, direction), multiply_pair(relax, halfway))
        )
        if iteration + 1 < ITERS:
            residual = minus_pair(halfway, multiply_pair(relax, second))
            bilinear_new = with_source(residual)
            blend = multiply_pair(divide_pair(bilinear_new, bilinear), divide_pair(advance, relax))
            direction = plus_pair(
                residual, multiply_pair(blend, minus_pair(direction, multiply_pair(relax, image)))
            )
            bilinear = bilinear_new
    first = tuple(jnp.broadcast_to(v[:, :1], v.shape) for v in answer)
    apart = minus_pair(answer, first)

    def norm(q):
        weighed = times_gram(q)
        return total(q[0] * weighed[0] + q[1] * weighed[1])

    return first, norm(apart), norm(first)


TILES = 4
SYSTEMS = 8
BLOCK = 16 * TILES // 2 + 2
OWN = 16
WINDOW = 32
CORE = 8
VMEM = pl.BlockSpec(memory_space=pltpu.VMEM)
SMEM = pl.BlockSpec(memory_space=pltpu.SMEM)
HBM = pl.BlockSpec(memory_space=pltpu.HBM)
LIMIT = 24 * 1024 * 1024


def call(kernel, outs, specs, out_specs, scratch=(), name=None, flops=0):
    return pl.pallas_call(
        kernel,
        out_shape=outs,
        in_specs=specs,
        out_specs=out_specs,
        scratch_shapes=list(scratch),
        compiler_params=pltpu.CompilerParams(vmem_limit_bytes=LIMIT),
        cost_estimate=pl.CostEstimate(flops=flops, bytes_accessed=1 << 20, transcendentals=0),
        name=name,
    )


def f32(*shape):
    return jax.ShapeDtypeStruct(shape, jnp.float32)


def rows_of(tile):
    return pl.ds(tile, 8, stride=TILES)


def pack_kernel(modes, start, place, background, absorb, density, profiles, adjoint, out, raw, sems):
    half = SYSTEMS // 2
    copies = []
    for system in range(SYSTEMS):
        source = profiles.at[modes[system]] if system < half else adjoint.at[system - half]
        copies.append(pltpu.make_async_copy(source, raw.at[system], sems.at[system]))
    for copy in copies:
        copy.start()
    for plane in range(2):
        where = place[0] * 2 + plane
        inside = (where >= start[0]) & (where < start[0] + SYSTEMS * SYSTEMS)
        for tile in range(TILES):
            rows = rows_of(tile)
            perm = jnp.where(
                inside, low_perm + perm_span * density[plane, rows], background[plane, rows]
            )
            diag_re = ((6.0 - wave_sq * perm) - CENTRE) * THIRD
            diag_im = absorb[plane, rows] * THIRD
            for system in range(SYSTEMS):
                out[system, 16 + plane * TILES + tile] = diag_re
                out[system, 24 + plane * TILES + tile] = diag_im
        share = density[plane, pl.ds(pl.multiple_of(place[1] * 8, 8), 8)]
        for system in range(SYSTEMS):
            out[system, 32 + plane] = share
    for system in range(SYSTEMS):
        copies[system].wait()
        for part in range(2):
            for plane in range(2):
                for tile in range(TILES):
                    out[system, (part * 2 + plane) * TILES + tile] = raw[
                        system, part, plane, rows_of(tile)
                    ]


class Stencil:
    def __init__(self):
        row = lax.broadcasted_iota(jnp.int32, (8, 128), 0)
        lane = lax.broadcasted_iota(jnp.int32, (8, 128), 1)
        self.first_row, self.last_row = row == 0, row == 7
        self.first_lane, self.last_lane = lane == 0, lane == 127

    def beside(self, below, here, above):
        up = jnp.where(self.first_row, 0.0, pltpu.roll(here[TILES - 1], 1, 0))
        down = jnp.where(self.last_row, 0.0, pltpu.roll(here[0], 7, 0))
        rows = [up] + list(here) + [down]
        sums = []
        for tile in range(TILES):
            left = jnp.where(self.first_lane, 0.0, pltpu.roll(here[tile], 1, 1))
            right = jnp.where(self.last_lane, 0.0, pltpu.roll(here[tile], 127, 1))
            z_sum = below[tile] + above[tile]
            sums.append((z_sum + (rows[tile] + rows[tile + 2])) + (left + right))
        return sums

    def step(self, basis, diag, level, at, third):
        def plane(part, where):
            return [basis[level, part, where, tile] for tile in range(TILES)]

        real, imag = plane(0, at), plane(1, at)
        near_re = self.beside(plane(0, at - 1), real, plane(0, at + 1))
        near_im = self.beside(plane(1, at - 1), imag, plane(1, at + 1))
        for tile in range(TILES):
            diag_re, diag_im = diag[0, at, tile], diag[1, at, tile]
            new_re = diag_re * real[tile] - diag_im * imag[tile] - third * near_re[tile]
            new_im = diag_re * imag[tile] + diag_im * real[tile] - third * near_im[tile]
            if level > 0:
                new_re = new_re - basis[level - 1, 0, at, tile]
                new_im = new_im - basis[level - 1, 1, at, tile]
            basis[level + 1, 0, at, tile] = new_re
            basis[level + 1, 1, at, tile] = new_im


def gram_pass(basis, acc, columns, ranges, shift):
    real_at, imag_at = pair_places()
    pairs = [(i, j) for j in columns for i in range(j + 1)]
    top = max(columns) + 1
    places = []
    for pair in pairs:
        places.append(real_at[pair])
        if pair[0] != pair[1]:
            places.append(imag_at[pair])

    def position(step, sums, first=0):
        window, tile = first + shift + step // TILES, step % TILES
        field = [(basis[k, 0, window, tile], basis[k, 1, window, tile]) for k in range(top)]
        new = []
        for i, j in pairs:
            (i_re, i_im), (j_re, j_im) = field[i], field[j]
            new.append(i_re * j_re + i_im * j_im)
            if i != j:
                new.append(i_re * j_im - i_im * j_re)
        return tuple(total + term for total, term in zip(sums, new))

    sums = tuple(acc[at] for at in places)
    for first, last in ranges:
        sums = lax.fori_loop(
            0, (last - first) * TILES, functools.partial(position, first=first), sums,
            unroll=TILES,
        )
    for at, value in zip(places, sums):
        acc[at] = value


def inner_kernel(block, basis, diag, acc):
    def load(chunk, _):
        for plane in range(2):
            for part in range(2):
                for tile in range(TILES):
                    at = part * 8 + plane * TILES + tile
                    basis[0, part, 2 * chunk + plane, tile] = block[chunk, at]
                    diag[part, 2 * chunk + plane, tile] = block[chunk, 16 + at]
        return 0

    lax.fori_loop(0, SYSTEMS, load, 0)
    stencil = Stencil()
    for level in range(SYSTEMS - 1):

        def plane_step(at, _, level=level):
            stencil.step(basis, diag, level, at, THIRD)
            return 0

        lax.fori_loop(
            level + 1, OWN - 1 - level, plane_step, 0, unroll=OWN - 2 - 2 * level
        )
    acc[...] = jnp.zeros_like(acc)
    for columns, ranges in INNER_PASSES:
        gram_pass(basis, acc, columns, ranges, 0)


INNER_PASSES = (
    ((0, 1, 2, 3, 4), ((4, 12),)),
    ((0, 1, 2), ((2, 4), (12, 14))),
    ((5, 6), ((6, 10),)),
)
OUTER_PASSES = (
    ((0, 1, 2, 3, 4), ((0, 2), (14, 16))),
    ((3, 4), ((2, 4), (12, 14))),
    ((5, 6), ((0, 6), (10, 16))),
    ((7,), ((0, 16),)),
    ((8,), ((0, 16),)),
)


def outer_kernel(place, block, low, high, inner, inner_diag, inner_acc, basis, gram, dens, diag, acc):
    def load(source, chunks, at):
        def one(chunk, _):
            for plane in range(2):
                window = at + 2 * chunk + plane
                for part in range(2):
                    for tile in range(TILES):
                        spot = part * 8 + plane * TILES + tile
                        basis[0, part, window, tile] = source[chunk, spot]
                        diag[part, window, tile] = source[chunk, 16 + spot]
            return 0

        lax.fori_loop(0, chunks, one, 0)

    load(low, SYSTEMS // 2, 0)
    load(high, SYSTEMS // 2, CORE + OWN)
    for level in range(SYSTEMS):

        def keep(at, _, level=level):
            for part in range(2):
                for tile in range(TILES):
                    basis[level, part, CORE + at, tile] = inner[level, part, at, tile]
                    if level == 0:
                        diag[part, CORE + at, tile] = inner_diag[part, at, tile]
            return 0

        lax.fori_loop(level, OWN - level, keep, 0, unroll=2)
    acc[...] = inner_acc[...]

    me = place[0] % SYSTEMS
    dens[0] = jnp.where(me > 0, block[jnp.maximum(me - 1, 0), 33], low[SYSTEMS // 2 - 1, 33])
    dens[1] = block[me, 32]
    dens[2] = block[me, 33]
    dens[3] = jnp.where(
        me < SYSTEMS - 1, block[jnp.minimum(me + 1, SYSTEMS - 1), 32], high[0, 32]
    )

    third_low = jnp.where(place[0] >= SYSTEMS, THIRD, 0.0)
    third_high = jnp.where(place[0] < SYSTEMS * (SYSTEMS - 1), THIRD, 0.0)
    stencil = Stencil()
    for level in range(BASIS - 1):

        def two_planes(step, _, level=level):
            lower, upper = level + 1 + step, WINDOW - 2 - level - step
            stencil.step(basis, diag, level, lower, jnp.where(lower < CORE, third_low, THIRD))
            stencil.step(
                basis, diag, level, upper, jnp.where(upper >= CORE + OWN, third_high, THIRD)
            )
            return 0

        lax.fori_loop(0, CORE, two_planes, 0, unroll=CORE)
    for columns, ranges in OUTER_PASSES:
        gram_pass(basis, acc, columns, ranges, CORE)
    by_pair = jnp.sum(acc[...], axis=1)
    ones = jnp.ones((8, 128), jnp.float32)
    gram[...] = exact_dot(ones, by_pair, ((1,), (1,)))[0:1]


def combine_kernel(grams, pick, nudge, basis, out):
    row = grams[0]
    for other in range(1, SYSTEMS):
        row = row + grams[other]
    ones = jnp.ones((128, 128), jnp.float32)
    picked = exact_dot(pick[...] * row, ones, ((1,), (0,)))
    norms = jnp.sqrt(picked[2 * ROWS : 4 * ROWS] * picked[4 * ROWS :])
    answer, apart, size = coefficients(picked[: 2 * ROWS] + nudge[...] * norms)
    agrees = jnp.max(jnp.where(apart <= AGREE * AGREE * size, 0.0, 1.0))
    flag = jnp.zeros((8, 128), jnp.float32) + agrees
    for slab in range(SYSTEMS):
        out[slab, 32] = flag
    weight = [
        (
            jnp.broadcast_to(answer[0][k : k + 1], (8, 128)),
            jnp.broadcast_to(answer[1][k : k + 1], (8, 128)),
        )
        for k in range(BASIS - 1)
    ]

    def solve_plane(plane, goals):
        for tile in range(TILES):
            real = jnp.zeros((8, 128), jnp.float32)
            imag = jnp.zeros((8, 128), jnp.float32)
            for k in range(BASIS - 1):
                b_re, b_im = basis[k, 0, plane, tile], basis[k, 1, plane, tile]
                real = real + (weight[k][0] * b_re - weight[k][1] * b_im)
                imag = imag + (weight[k][0] * b_im + weight[k][1] * b_re)
            for slab, at in goals:
                out[slab, at * TILES + tile] = real
                out[slab, (4 + at) * TILES + tile] = imag

    def middle(slab, _):
        for plane in range(2):
            solve_plane(CORE - 1 + 2 * slab + plane, ((slab, plane), (slab - 1, 2 + plane)))
        return 0

    for plane in range(2):
        solve_plane(CORE - 1 + plane, ((0, plane),))
        solve_plane(CORE + OWN - 1 + plane, ((SYSTEMS - 1, 2 + plane),))
    lax.fori_loop(1, SYSTEMS, middle, 0)


def fields_kernel(place, fields, forward, adjoint, keep, give, natural):
    half = SYSTEMS // 2
    for port in range(half):
        for part in range(2):
            for plane in range(2):
                for tile in range(TILES):
                    at = (part * 4 + 1 + plane) * TILES + tile
                    forward[port, part, plane, rows_of(tile)] = fields[port, at]
                    adjoint[port, part, plane, rows_of(tile)] = fields[half + port, at]
    for plane in range(4):
        for tile in range(TILES):
            real, imag = plane * TILES + tile, (4 + plane) * TILES + tile
            total = None
            for port in range(half):
                term = fields[port, real] * fields[half + port, real]
                term = term - fields[port, imag] * fields[half + port, imag]
                total = term if total is None else total + term
            natural[plane, rows_of(tile)] = total
    flag = fields[0, 32]
    for system in range(1, SYSTEMS):
        flag = flag + fields[system, 32]
    core = place[1] % 2
    for out, side in ((keep, core), (give, 1 - core)):
        for pair in range(2):
            rows = pl.ds(pl.multiple_of((2 * pair + side) * 8, 8), 8)
            for plane in range(4):
                out[pair, plane] = natural[plane, rows]
            out[pair, 4] = flag


def pair_kernel(place, mine, other, keep, give):
    own = place[1] // 2
    for at in range(5):
        keep[at] = mine[own, at] + other[own, at]
        give[at] = mine[1 - own, at] + other[1 - own, at]


def density_kernel(start, place, mine, other, dens, out, flag):
    lane = lax.broadcasted_iota(jnp.int32, (8, 128), 1)
    updated = []
    for plane in range(4):
        gradient = -wave_sq * (mine[plane] + other[plane])
        where = place[0] * 2 + plane - 1
        inside = (where >= start[0]) & (where < start[0] + SYSTEMS * SYSTEMS)
        rows = dens[plane]
        moved = jnp.clip(rows - step_size * perm_span * gradient, 0.0, 1.0)
        rows = jnp.where(inside, moved, rows)
        exists = (where >= 0) & (where < 2 * SYSTEMS * SYSTEMS)
        updated.append(jnp.where(exists, rows, 0.0))
    for plane in range(2):
        own = updated[plane + 1]
        right = jnp.where(lane == 127, 0.0, pltpu.roll(own, 127, 1))
        left = jnp.where(lane == 0, 0.0, pltpu.roll(own, 1, 1))
        filtered = (2.0 * own + updated[plane + 2] + updated[plane] + right + left) / 6.0
        edge = float(np.tanh(sharpness * threshold))
        other_edge = float(np.tanh(sharpness * (1.0 - threshold)))
        out[plane] = (edge + jnp.tanh(sharpness * (filtered - threshold))) / (edge + other_edge)
    flag[0] = jnp.max(mine[4] + other[4])


def copy_kernel(count, *refs):
    sems = refs[-1]
    arrays = refs[-1 - 2 * count : -1]
    copies = [
        pltpu.make_async_copy(arrays[at], arrays[count + at], sems.at[at]) for at in range(count)
    ]
    for copy in copies:
        copy.start()
    for copy in copies:
        copy.wait()


def row_major(mark, arrays, name):
    count = len(arrays)
    return call(
        functools.partial(copy_kernel, count),
        tuple(jax.ShapeDtypeStruct(array.shape, array.dtype) for array in arrays),
        [SMEM] + [HBM] * count,
        (HBM,) * count,
        [pltpu.SemaphoreType.DMA((count,))],
        name,
    )(mark.reshape(1), *arrays)


def on_device(background, absorb, density, profiles, adjoint_source, port_modes, design_start):
    slab = lax.axis_index("zslab")
    place = jnp.stack([slab, lax.axis_index("group")]).astype(jnp.int32)
    planes_of = [[z * SYSTEMS + l for l in range(SYSTEMS)] for z in range(SYSTEMS)]
    columns = [[z * SYSTEMS + l for z in range(SYSTEMS)] for l in range(SYSTEMS)]
    packed = call(
        pack_kernel,
        f32(SYSTEMS, BLOCK, 8, 128),
        [SMEM, SMEM, SMEM, VMEM, VMEM, VMEM, HBM, HBM],
        VMEM,
        [
            pltpu.VMEM((SYSTEMS,) + profiles.shape[1:], jnp.float32),
            pltpu.SemaphoreType.DMA((SYSTEMS,)),
        ],
        "pack",
    )(port_modes, design_start, place, background, absorb, density, profiles, adjoint_source)
    block = lax.all_to_all(packed, "zslab", 0, 0, axis_index_groups=planes_of, tiled=True)
    count = SYSTEMS * SYSTEMS
    up = [(i, i + SYSTEMS) for i in range(count - SYSTEMS)]
    down = [(target, source) for source, target in up]
    low = lax.ppermute(block[SYSTEMS // 2 :], "zslab", up)
    high = lax.ppermute(block[: SYSTEMS // 2], "zslab", down)
    inner = call(
        inner_kernel,
        (f32(SYSTEMS, 2, OWN, TILES, 8, 128), f32(2, OWN, TILES, 8, 128), f32(128, 8, 128)),
        [VMEM],
        (VMEM,) * 3,
        (),
        "inner",
        10**8,
    )(block)
    plane = (TILES, 8, 128)
    basis, gram, dens = call(
        outer_kernel,
        (f32(BASIS, 2, WINDOW, *plane), f32(1, 128), f32(4, 8, 128)),
        [SMEM] + [VMEM] * 6,
        (VMEM, VMEM, VMEM),
        [pltpu.VMEM((2, WINDOW) + plane, jnp.float32), pltpu.VMEM((128, 8, 128), jnp.float32)],
        "outer",
        2 * 10**8,
    )(place, block, low, high, *inner)
    grams = lax.all_to_all(
        jnp.broadcast_to(gram[None], (SYSTEMS, 1, 128)), "zslab", 0, 0,
        axis_index_groups=columns, tiled=True,
    )
    pick, nudge = gram_tables()
    solved = call(
        combine_kernel, f32(SYSTEMS, 33, 8, 128), [VMEM, VMEM, VMEM, VMEM], VMEM, (), "combine"
    )(grams, jnp.asarray(pick), jnp.asarray(nudge), basis)
    fields = lax.all_to_all(solved, "zslab", 0, 0, axis_index_groups=planes_of, tiled=True)
    half = f32(SYSTEMS // 2, 2, 2, 8 * TILES, 128)
    forward, adjoint, keep, give = call(
        fields_kernel,
        (half, half, f32(2, 5, 8, 128), f32(2, 5, 8, 128)),
        [SMEM, VMEM],
        (VMEM,) * 4,
        [pltpu.VMEM((4, 8 * TILES, 128), jnp.float32)],
        "fields",
    )(place, fields)
    got = lax.ppermute(give, "group", [(i, i ^ 1) for i in range(4)])
    keep, give = call(
        pair_kernel, (f32(5, 8, 128), f32(5, 8, 128)), [SMEM, VMEM, VMEM], (VMEM, VMEM), (), "pair"
    )(place, keep, got)
    got = lax.ppermute(give, "group", [(i, i ^ 2) for i in range(4)])
    new_density, flag = call(
        density_kernel,
        (f32(2, 8, 128), f32(1)),
        [SMEM, SMEM, VMEM, VMEM, VMEM],
        (VMEM, SMEM),
        (),
        "density",
    )(design_start, place, keep, got, dens)

    def again(state):
        held = (background, absorb, density, profiles, adjoint_source)
        held = row_major(state[0], held, "arguments")
        results = iterate_on_device(*held, port_modes, design_start)
        return (jnp.zeros((), jnp.float32),) + tuple(row_major(state[0], results, "results"))

    state = (flag[0], forward, adjoint, new_density)
    return lax.while_loop(lambda state: state[0] > 0.0, again, state)[1:]


def solution(mesh):
    return jax.shard_map(
        on_device,
        mesh=mesh,
        in_specs=(
            P("zslab", None, None),
            P("zslab", None, None),
            P("zslab", None, None),
            P(None, None, "zslab", None, None),
            P("group", None, "zslab", None, None),
            P("group"),
            P(),
        ),
        out_specs=(
            P("group", None, "zslab", None, None),
            P("group", None, "zslab", None, None),
            P("zslab", "group", None),
        ),
        check_vma=False,
    )
```

```python
import functools

import jax
import jax.numpy as jnp
import numpy as np
from jax import lax
from jax.experimental import pallas as pl
from jax.experimental.pallas import tpu as pltpu
from jax.sharding import PartitionSpec as P

ITERS = 4


wave_sq = 0.1
step_size = 2.0
perm_span = 10.0
low_perm = 2.1
sharpness = 8.0
threshold = 0.5


def with_halo(block, sides, width):
    for axis, dim in sides:
        count = lax.axis_size(axis)
        forward = [(i, i + 1) for i in range(count - 1)]
        backward = [(target, source) for source, target in forward]
        low = lax.ppermute(
            lax.slice_in_dim(block, block.shape[dim] - width, None, axis=dim), axis, forward
        )
        high = lax.ppermute(lax.slice_in_dim(block, 0, width, axis=dim), axis, backward)
        block = jnp.concatenate([low, block, high], axis=dim)
    return block


def scaled(coef, field):
    coef_re = coef[0].reshape((-1, 1, 1, 1))
    coef_im = coef[1].reshape((-1, 1, 1, 1))
    real_part = coef_re * field[:, 0] - coef_im * field[:, 1]
    imag_part = coef_re * field[:, 1] + coef_im * field[:, 0]
    return jnp.stack([real_part, imag_part], axis=1)


def product_pair(left, right):
    real_part = jnp.sum(left[:, 0] * right[:, 0] + left[:, 1] * right[:, 1], axis=(1, 2, 3))
    imag_part = jnp.sum(left[:, 0] * right[:, 1] - left[:, 1] * right[:, 0], axis=(1, 2, 3))
    return (real_part, imag_part)


def divide_pair(top, bottom):
    denominator = bottom[0] * bottom[0] + bottom[1] * bottom[1]
    return (
        (top[0] * bottom[0] + top[1] * bottom[1]) / denominator,
        (top[1] * bottom[0] - top[0] * bottom[1]) / denominator,
    )


def multiply_pair(left, right):
    return (left[0] * right[0] - left[1] * right[1], left[0] * right[1] + left[1] * right[0])


def with_planes(field):
    return with_halo(field, (("zslab", 2),), 1)


def operate(field, diag_re, diag_im):
    padded = jnp.pad(with_planes(field), ((0, 0), (0, 0), (0, 0), (1, 1), (1, 1)))
    beside = padded[:, :, 2:, 1:-1, 1:-1] + padded[:, :, :-2, 1:-1, 1:-1]
    beside = beside + padded[:, :, 1:-1, 2:, 1:-1] + padded[:, :, 1:-1, :-2, 1:-1]
    beside = beside + padded[:, :, 1:-1, 1:-1, 2:] + padded[:, :, 1:-1, 1:-1, :-2]
    real_part = diag_re * field[:, 0] - diag_im * field[:, 1]
    imag_part = diag_re * field[:, 1] + diag_im * field[:, 0]
    return jnp.stack([real_part, imag_part], axis=1) - beside


def bicgstab(sources, diag_re, diag_im):
    solution = jnp.zeros_like(sources)
    residual = sources
    direction = sources
    bilinear = lax.psum(product_pair(sources, residual), "zslab")
    for iteration in range(ITERS):
        image = operate(direction, diag_re, diag_im)
        along = lax.psum(product_pair(sources, image), "zslab")
        advance = divide_pair(bilinear, along)
        halfway = residual - scaled(advance, image)
        second = operate(halfway, diag_re, diag_im)
        cross_re, cross_im = product_pair(second, halfway)
        energy = jnp.sum(second[:, 0] * second[:, 0] + second[:, 1] * second[:, 1], axis=(1, 2, 3))
        cross_re, cross_im, energy = lax.psum((cross_re, cross_im, energy), "zslab")
        relax_coef = (cross_re / energy, cross_im / energy)
        solution = solution + scaled(advance, direction) + scaled(relax_coef, halfway)
        residual = halfway - scaled(relax_coef, second)
        if iteration + 1 < ITERS:
            bilinear_new = lax.psum(product_pair(sources, residual), "zslab")
        if iteration + 1 < ITERS:
            blend_coef = multiply_pair(
                divide_pair(bilinear_new, bilinear), divide_pair(advance, relax_coef)
            )
            direction = residual + scaled(blend_coef, direction - scaled(relax_coef, image))
            bilinear = bilinear_new
    return solution


def iterate_on_device(background, absorb, density, profiles, adjoint_source, port_modes, design_start):
    planes_dev = density.shape[0]
    rows_all = density.shape[1]
    first_plane = lax.axis_index("zslab") * planes_dev
    design_depth = planes_dev * lax.axis_size("zslab") // 2
    planes = first_plane + jnp.arange(planes_dev)
    in_design = (planes >= design_start[0]) & (planes < design_start[0] + design_depth)
    in_design = in_design[:, None, None]
    permittivity = jnp.where(in_design, low_perm + perm_span * density, background)
    diag_re = 6.0 - wave_sq * permittivity
    selector = (port_modes[:, None] == jnp.arange(profiles.shape[0])[None, :]).astype(jnp.float32)
    forward_source = jnp.einsum(
        "pm,mczyx->pczyx", selector, profiles, precision=lax.Precision.HIGHEST
    )
    port_count = forward_source.shape[0]
    sources = jnp.concatenate([forward_source, adjoint_source], axis=0)
    fields = bicgstab(sources, diag_re, absorb)
    forward_field = fields[:port_count]
    adjoint_field = fields[port_count:]
    terms = forward_field[:, 0] * adjoint_field[:, 0] - forward_field[:, 1] * adjoint_field[:, 1]
    local_term = -wave_sq * jnp.sum(terms, axis=0)
    rows_share = rows_all // lax.axis_size("group")
    row_start = lax.axis_index("group") * rows_share
    total = lax.psum(local_term, "group")
    gradient = lax.dynamic_slice_in_dim(total, row_start, rows_share, 1)
    density_rows = lax.dynamic_slice_in_dim(density, row_start, rows_share, 1)
    updated = jnp.where(
        in_design, jnp.clip(density_rows - step_size * perm_span * gradient, 0.0, 1.0), density_rows
    )
    extended = with_halo(updated, (("zslab", 0),), 1)
    padded = jnp.pad(extended, ((0, 0), (0, 0), (1, 1)))
    filtered = (
        2.0 * updated
        + padded[2:, :, 1:-1]
        + padded[:-2, :, 1:-1]
        + padded[1:-1, :, 2:]
        + padded[1:-1, :, :-2]
    ) / 6.0
    new_density = (
        jnp.tanh(sharpness * threshold) + jnp.tanh(sharpness * (filtered - threshold))
    ) / (jnp.tanh(sharpness * threshold) + jnp.tanh(sharpness * (1.0 - threshold)))
    return (forward_field, adjoint_field, new_density)


BASIS = 2 * ITERS + 1
CENTRE = 5.3
HALF_RADIUS = 3.0
THIRD = 1.0 / HALF_RADIUS
NUDGE = 1e-6
AGREE = 5e-4
ROWS = 16 * BASIS


def pair_places():
    real, imag, place = {}, {}, 0
    for j in range(BASIS):
        for i in range(j + 1):
            real[(i, j)] = place
            place += 1
    for j in range(BASIS):
        for i in range(j):
            imag[(i, j)] = place
            place += 1
    return real, imag


def gram_tables():
    real, imag = pair_places()
    pick = np.zeros((6 * ROWS, 128), np.float32)
    nudge = np.zeros((2 * ROWS, 128), np.float32)
    rng = np.random.default_rng(7)
    sign_re = {pair: np.where(rng.random(128) < 0.5, -1.0, 1.0) for pair in real}
    sign_im = {pair: np.where(rng.random(128) < 0.5, -1.0, 1.0) for pair in imag}
    for j in range(BASIS):
        for i in range(BASIS):
            row, pair = j * 16 + i, (min(i, j), max(i, j))
            pick[row, real[pair]] = 1.0
            for half in (0, ROWS):
                pick[2 * ROWS + half + row, real[(i, i)]] = 1.0
                pick[4 * ROWS + half + row, real[(j, j)]] = 1.0
            nudge[row] = NUDGE * sign_re[pair]
            if i != j:
                side = 1.0 if i < j else -1.0
                pick[ROWS + row, imag[pair]] = side
                nudge[ROWS + row] = NUDGE * side * sign_im[pair]
    nudge[:, 0] = 0.0
    return pick, nudge


def exact_dot(left, right, dims):
    return lax.dot_general(
        left, right, (dims, ((), ())), precision=lax.Precision.HIGHEST,
        preferred_element_type=jnp.float32,
    )


def minus_pair(left, right):
    return (left[0] - right[0], left[1] - right[1])


def plus_pair(left, right):
    return (left[0] + right[0], left[1] + right[1])


def coefficients(gram):
    gram_re = [gram[16 * j : 16 * j + 16] for j in range(BASIS)]
    gram_im = [gram[ROWS + 16 * j : ROWS + 16 * j + 16] for j in range(BASIS)]
    row = lax.broadcasted_iota(jnp.int32, (16, 128), 0)
    keep = jnp.where(row == 15, 0.0, HALF_RADIUS)

    def apply(q):
        return tuple(
            CENTRE * v + HALF_RADIUS * pltpu.roll(v, 1, 0) + keep * pltpu.roll(v, 15, 0) for v in q
        )

    def total(v):
        return jnp.sum(v, axis=0, keepdims=True)

    def with_source(q):
        return (
            total(gram_re[0] * q[0] + gram_im[0] * q[1]),
            total(gram_re[0] * q[1] - gram_im[0] * q[0]),
        )

    def times_gram(q):
        out_re = jnp.zeros((16, 128), jnp.float32)
        out_im = jnp.zeros((16, 128), jnp.float32)
        for j in range(BASIS):
            q_re, q_im = q[0][j : j + 1], q[1][j : j + 1]
            out_re = out_re + (gram_re[j] * q_re - gram_im[j] * q_im)
            out_im = out_im + (gram_re[j] * q_im + gram_im[j] * q_re)
        return out_re, out_im

    one = jnp.where(row == 0, 1.0, 0.0)
    zero = jnp.zeros((16, 128), jnp.float32)
    answer, residual, direction = (zero, zero), (one, zero), (one, zero)
    bilinear = with_source(residual)
    for iteration in range(ITERS):
        image = apply(direction)
        advance = divide_pair(bilinear, with_source(image))
        halfway = minus_pair(residual, multiply_pair(advance, image))
        second = apply(halfway)
        weighed = times_gram(second)
        energy = total(second[0] * weighed[0] + second[1] * weighed[1])
        relax = (
            total(weighed[0] * halfway[0] + weighed[1] * halfway[1]) / energy,
            total(weighed[0] * halfway[1] - weighed[1] * halfway[0]) / energy,
        )
        answer = plus_pair(
            answer, plus_pair(multiply_pair(advance, direction), multiply_pair(relax, halfway))
        )
        if iteration + 1 < ITERS:
            residual = minus_pair(halfway, multiply_pair(relax, second))
            bilinear_new = with_source(residual)
            blend = multiply_pair(divide_pair(bilinear_new, bilinear), divide_pair(advance, relax))
            direction = plus_pair(
                residual, multiply_pair(blend, minus_pair(direction, multiply_pair(relax, image)))
            )
            bilinear = bilinear_new
    first = tuple(jnp.broadcast_to(v[:, :1], v.shape) for v in answer)
    apart = minus_pair(answer, first)

    def norm(q):
        weighed = times_gram(q)
        return total(q[0] * weighed[0] + q[1] * weighed[1])

    return first, norm(apart), norm(first)


TILES = 4
SYSTEMS = 8
BLOCK = 12 * TILES // 2 + 2
ROWS_AT = BLOCK - 2
OWN = 16
WINDOW = 32
CORE = 8
VMEM = pl.BlockSpec(memory_space=pltpu.VMEM)
SMEM = pl.BlockSpec(memory_space=pltpu.SMEM)
HBM = pl.BlockSpec(memory_space=pltpu.HBM)
LIMIT = 24 * 1024 * 1024


def call(kernel, outs, specs, out_specs, scratch=(), name=None, flops=0):
    return pl.pallas_call(
        kernel,
        out_shape=outs,
        in_specs=specs,
        out_specs=out_specs,
        scratch_shapes=list(scratch),
        compiler_params=pltpu.CompilerParams(vmem_limit_bytes=LIMIT),
        cost_estimate=pl.CostEstimate(flops=flops, bytes_accessed=1 << 20, transcendentals=0),
        name=name,
    )


def f32(*shape):
    return jax.ShapeDtypeStruct(shape, jnp.float32)


def rows_of(tile):
    return pl.ds(tile, 8, stride=TILES)


def pack_kernel(modes, start, place, background, absorb, density, profiles, adjoint, out, raw, sems):
    half = SYSTEMS // 2
    copies = []
    for system in range(SYSTEMS):
        source = profiles.at[modes[system]] if system < half else adjoint.at[system - half]
        copies.append(pltpu.make_async_copy(source, raw.at[system], sems.at[system]))
    for copy in copies:
        copy.start()
    for plane in range(2):
        where = place[0] * 2 + plane
        inside = (where >= start[0]) & (where < start[0] + SYSTEMS * SYSTEMS)
        for tile in range(TILES):
            rows = rows_of(tile)
            perm = jnp.where(
                inside, low_perm + perm_span * density[plane, rows], background[plane, rows]
            )
            diag_re = ((6.0 - wave_sq * perm) - CENTRE) * THIRD
            diag_im = absorb[plane, rows] * THIRD
            part = jnp.where(place[1] % 2 == 0, diag_re, diag_im)
            for system in range(SYSTEMS):
                out[system, 16 + plane * TILES + tile] = part
        share = density[plane, pl.ds(pl.multiple_of(place[1] * 8, 8), 8)]
        for system in range(SYSTEMS):
            out[system, ROWS_AT + plane] = share
    for system in range(SYSTEMS):
        copies[system].wait()
        for part in range(2):
            for plane in range(2):
                for tile in range(TILES):
                    out[system, (part * 2 + plane) * TILES + tile] = raw[
                        system, part, plane, rows_of(tile)
                    ]


class Stencil:
    def __init__(self):
        row = lax.broadcasted_iota(jnp.int32, (8, 128), 0)
        lane = lax.broadcasted_iota(jnp.int32, (8, 128), 1)
        self.first_row, self.last_row = row == 0, row == 7
        self.first_lane, self.last_lane = lane == 0, lane == 127

    def beside(self, below, here, above):
        up = jnp.where(self.first_row, 0.0, pltpu.roll(here[TILES - 1], 1, 0))
        down = jnp.where(self.last_row, 0.0, pltpu.roll(here[0], 7, 0))
        rows = [up] + list(here) + [down]
        sums = []
        for tile in range(TILES):
            left = jnp.where(self.first_lane, 0.0, pltpu.roll(here[tile], 1, 1))
            right = jnp.where(self.last_lane, 0.0, pltpu.roll(here[tile], 127, 1))
            z_sum = below[tile] + above[tile]
            sums.append((z_sum + (rows[tile] + rows[tile + 2])) + (left + right))
        return sums

    def step(self, basis, diag, level, at, third):
        def plane(part, where):
            return [basis[level, part, where, tile] for tile in range(TILES)]

        real, imag = plane(0, at), plane(1, at)
        near_re = self.beside(plane(0, at - 1), real, plane(0, at + 1))
        near_im = self.beside(plane(1, at - 1), imag, plane(1, at + 1))
        for tile in range(TILES):
            diag_re, diag_im = diag[0, at, tile], diag[1, at, tile]
            new_re = diag_re * real[tile] - diag_im * imag[tile] - third * near_re[tile]
            new_im = diag_re * imag[tile] + diag_im * real[tile] - third * near_im[tile]
            if level > 0:
                new_re = new_re - basis[level - 1, 0, at, tile]
                new_im = new_im - basis[level - 1, 1, at, tile]
            basis[level + 1, 0, at, tile] = new_re
            basis[level + 1, 1, at, tile] = new_im


def gram_pass(basis, acc, columns, ranges, shift):
    real_at, imag_at = pair_places()
    pairs = [(i, j) for j in columns for i in range(j + 1)]
    top = max(columns) + 1
    places = []
    for pair in pairs:
        places.append(real_at[pair])
        if pair[0] != pair[1]:
            places.append(imag_at[pair])

    def position(step, sums, first=0):
        window, tile = first + shift + step // TILES, step % TILES
        field = [(basis[k, 0, window, tile], basis[k, 1, window, tile]) for k in range(top)]
        new = []
        for i, j in pairs:
            (i_re, i_im), (j_re, j_im) = field[i], field[j]
            new.append(i_re * j_re + i_im * j_im)
            if i != j:
                new.append(i_re * j_im - i_im * j_re)
        return tuple(total + term for total, term in zip(sums, new))

    sums = tuple(acc[at] for at in places)
    for first, last in ranges:
        sums = lax.fori_loop(
            0, (last - first) * TILES, functools.partial(position, first=first), sums,
            unroll=TILES,
        )
    for at, value in zip(places, sums):
        acc[at] = value


def inner_kernel(place, block, other, basis, diag, acc):
    core = place[1] % 2

    def load(chunk, _):
        for plane in range(2):
            for part in range(2):
                for tile in range(TILES):
                    at = part * 8 + plane * TILES + tile
                    basis[0, part, 2 * chunk + plane, tile] = block[chunk, at]
            for tile in range(TILES):
                at = plane * TILES + tile
                diag[core, 2 * chunk + plane, tile] = block[chunk, 16 + at]
                diag[1 - core, 2 * chunk + plane, tile] = other[chunk, at]
        return 0

    lax.fori_loop(0, SYSTEMS, load, 0)
    stencil = Stencil()
    for level in range(SYSTEMS - 1):

        def plane_step(at, _, level=level):
            stencil.step(basis, diag, level, at, THIRD)
            return 0

        lax.fori_loop(
            level + 1, OWN - 1 - level, plane_step, 0, unroll=OWN - 2 - 2 * level
        )
    acc[...] = jnp.zeros_like(acc)
    for columns, ranges in INNER_PASSES:
        gram_pass(basis, acc, columns, ranges, 0)


INNER_PASSES = (
    ((0, 1, 2, 3, 4), ((4, 12),)),
    ((0, 1, 2), ((2, 4), (12, 14))),
    ((5, 6), ((6, 10),)),
)
OUTER_PASSES = (
    ((0, 1, 2, 3, 4), ((0, 2), (14, 16))),
    ((3, 4), ((2, 4), (12, 14))),
    ((5, 6), ((0, 6), (10, 16))),
    ((7,), ((0, 16),)),
    ((8,), ((0, 16),)),
)


def outer_kernel(
    place, block, low, high, other, inner, inner_diag, inner_acc, basis, gram, dens, diag, acc
):
    core = place[1] % 2

    def load(source, first, at):
        def one(chunk, _):
            for plane in range(2):
                window = at + 2 * chunk + plane
                for part in range(2):
                    for tile in range(TILES):
                        spot = part * 8 + plane * TILES + tile
                        basis[0, part, window, tile] = source[chunk, spot]
                for tile in range(TILES):
                    spot = plane * TILES + tile
                    diag[core, window, tile] = source[chunk, 16 + spot]
                    diag[1 - core, window, tile] = other[first + chunk, spot]
            return 0

        lax.fori_loop(0, SYSTEMS // 2, one, 0)

    load(low, 0, 0)
    load(high, SYSTEMS // 2, CORE + OWN)
    for level in range(SYSTEMS):

        def keep(at, _, level=level):
            for part in range(2):
                for tile in range(TILES):
                    basis[level, part, CORE + at, tile] = inner[level, part, at, tile]
                    if level == 0:
                        diag[part, CORE + at, tile] = inner_diag[part, at, tile]
            return 0

        lax.fori_loop(level, OWN - level, keep, 0, unroll=2)
    acc[...] = inner_acc[...]

    me = place[0] % SYSTEMS
    dens[0] = jnp.where(me > 0, block[jnp.maximum(me - 1, 0), ROWS_AT + 1], low[SYSTEMS // 2 - 1, ROWS_AT + 1])
    dens[1] = block[me, ROWS_AT]
    dens[2] = block[me, ROWS_AT + 1]
    dens[3] = jnp.where(
        me < SYSTEMS - 1, block[jnp.minimum(me + 1, SYSTEMS - 1), ROWS_AT], high[0, ROWS_AT]
    )

    third_low = jnp.where(place[0] >= SYSTEMS, THIRD, 0.0)
    third_high = jnp.where(place[0] < SYSTEMS * (SYSTEMS - 1), THIRD, 0.0)
    stencil = Stencil()
    for level in range(BASIS - 1):

        def two_planes(step, _, level=level):
            lower, upper = level + 1 + step, WINDOW - 2 - level - step
            stencil.step(basis, diag, level, lower, jnp.where(lower < CORE, third_low, THIRD))
            stencil.step(
                basis, diag, level, upper, jnp.where(upper >= CORE + OWN, third_high, THIRD)
            )
            return 0

        lax.fori_loop(0, CORE, two_planes, 0, unroll=CORE)
    for columns, ranges in OUTER_PASSES:
        gram_pass(basis, acc, columns, ranges, CORE)
    by_pair = jnp.sum(acc[...], axis=1)
    ones = jnp.ones((8, 128), jnp.float32)
    gram[...] = exact_dot(ones, by_pair, ((1,), (1,)))[0:1]


def combine_kernel(grams, pick, nudge, basis, out):
    row = grams[0]
    for other in range(1, SYSTEMS):
        row = row + grams[other]
    ones = jnp.ones((128, 128), jnp.float32)
    picked = exact_dot(pick[...] * row, ones, ((1,), (0,)))
    norms = jnp.sqrt(picked[2 * ROWS : 4 * ROWS] * picked[4 * ROWS :])
    answer, apart, size = coefficients(picked[: 2 * ROWS] + nudge[...] * norms)
    agrees = jnp.max(jnp.where(apart <= AGREE * AGREE * size, 0.0, 1.0))
    flag = jnp.zeros((8, 128), jnp.float32) + agrees
    for slab in range(SYSTEMS):
        out[slab, 32] = flag
    weight = [
        (
            jnp.broadcast_to(answer[0][k : k + 1], (8, 128)),
            jnp.broadcast_to(answer[1][k : k + 1], (8, 128)),
        )
        for k in range(BASIS - 1)
    ]

    def solve_plane(plane, goals):
        for tile in range(TILES):
            real = jnp.zeros((8, 128), jnp.float32)
            imag = jnp.zeros((8, 128), jnp.float32)
            for k in range(BASIS - 1):
                b_re, b_im = basis[k, 0, plane, tile], basis[k, 1, plane, tile]
                real = real + (weight[k][0] * b_re - weight[k][1] * b_im)
                imag = imag + (weight[k][0] * b_im + weight[k][1] * b_re)
            for slab, at in goals:
                out[slab, at * TILES + tile] = real
                out[slab, (4 + at) * TILES + tile] = imag

    def middle(slab, _):
        for plane in range(2):
            solve_plane(CORE - 1 + 2 * slab + plane, ((slab, plane), (slab - 1, 2 + plane)))
        return 0

    for plane in range(2):
        solve_plane(CORE - 1 + plane, ((0, plane),))
        solve_plane(CORE + OWN - 1 + plane, ((SYSTEMS - 1, 2 + plane),))
    lax.fori_loop(1, SYSTEMS, middle, 0)


def fields_kernel(fields, forward, adjoint):
    half = SYSTEMS // 2
    for port in range(half):
        for part in range(2):
            for plane in range(2):
                for tile in range(TILES):
                    at = (part * 4 + 1 + plane) * TILES + tile
                    forward[port, part, plane, rows_of(tile)] = fields[port, at]
                    adjoint[port, part, plane, rows_of(tile)] = fields[half + port, at]


def terms_kernel(place, fields, keep, give, natural):
    half = SYSTEMS // 2
    for plane in range(4):
        for tile in range(TILES):
            real, imag = plane * TILES + tile, (4 + plane) * TILES + tile
            total = None
            for port in range(half):
                term = fields[port, real] * fields[half + port, real]
                term = term - fields[port, imag] * fields[half + port, imag]
                total = term if total is None else total + term
            natural[plane, rows_of(tile)] = total
    flag = fields[0, 32]
    for system in range(1, SYSTEMS):
        flag = flag + fields[system, 32]
    core = place[1] % 2
    for out, side in ((keep, core), (give, 1 - core)):
        for pair in range(2):
            rows = pl.ds(pl.multiple_of((2 * pair + side) * 8, 8), 8)
            for plane in range(4):
                out[pair, plane] = natural[plane, rows]
            out[pair, 4] = flag


def pair_kernel(place, mine, other, keep, give):
    own = place[1] // 2
    for at in range(5):
        keep[at] = mine[own, at] + other[own, at]
        give[at] = mine[1 - own, at] + other[1 - own, at]


def density_kernel(start, place, mine, other, dens, out, flag):
    lane = lax.broadcasted_iota(jnp.int32, (8, 128), 1)
    updated = []
    for plane in range(4):
        gradient = -wave_sq * (mine[plane] + other[plane])
        where = place[0] * 2 + plane - 1
        inside = (where >= start[0]) & (where < start[0] + SYSTEMS * SYSTEMS)
        rows = dens[plane]
        moved = jnp.clip(rows - step_size * perm_span * gradient, 0.0, 1.0)
        rows = jnp.where(inside, moved, rows)
        exists = (where >= 0) & (where < 2 * SYSTEMS * SYSTEMS)
        updated.append(jnp.where(exists, rows, 0.0))
    for plane in range(2):
        own = updated[plane + 1]
        right = jnp.where(lane == 127, 0.0, pltpu.roll(own, 127, 1))
        left = jnp.where(lane == 0, 0.0, pltpu.roll(own, 1, 1))
        filtered = (2.0 * own + updated[plane + 2] + updated[plane] + right + left) / 6.0
        edge = float(np.tanh(sharpness * threshold))
        other_edge = float(np.tanh(sharpness * (1.0 - threshold)))
        out[plane] = (edge + jnp.tanh(sharpness * (filtered - threshold))) / (edge + other_edge)
    flag[0] = jnp.max(mine[4] + other[4])


def copy_kernel(count, *refs):
    sems = refs[-1]
    arrays = refs[-1 - 2 * count : -1]
    copies = [
        pltpu.make_async_copy(arrays[at], arrays[count + at], sems.at[at]) for at in range(count)
    ]
    for copy in copies:
        copy.start()
    for copy in copies:
        copy.wait()


def row_major(mark, arrays, name):
    count = len(arrays)
    return call(
        functools.partial(copy_kernel, count),
        tuple(jax.ShapeDtypeStruct(array.shape, array.dtype) for array in arrays),
        [SMEM] + [HBM] * count,
        (HBM,) * count,
        [pltpu.SemaphoreType.DMA((count,))],
        name,
    )(mark.reshape(1), *arrays)


def on_device(background, absorb, density, profiles, adjoint_source, port_modes, design_start):
    slab = lax.axis_index("zslab")
    place = jnp.stack([slab, lax.axis_index("group")]).astype(jnp.int32)
    planes_of = [[z * SYSTEMS + l for l in range(SYSTEMS)] for z in range(SYSTEMS)]
    columns = [[z * SYSTEMS + l for z in range(SYSTEMS)] for l in range(SYSTEMS)]
    packed = call(
        pack_kernel,
        f32(SYSTEMS, BLOCK, 8, 128),
        [SMEM, SMEM, SMEM, VMEM, VMEM, VMEM, HBM, HBM],
        VMEM,
        [
            pltpu.VMEM((SYSTEMS,) + profiles.shape[1:], jnp.float32),
            pltpu.SemaphoreType.DMA((SYSTEMS,)),
        ],
        "pack",
    )(port_modes, design_start, place, background, absorb, density, profiles, adjoint_source)
    block = lax.all_to_all(packed, "zslab", 0, 0, axis_index_groups=planes_of, tiled=True)
    count = SYSTEMS * SYSTEMS
    up = [(i, i + SYSTEMS) for i in range(count - SYSTEMS)]
    down = [(target, source) for source, target in up]
    low = lax.ppermute(block[SYSTEMS // 2 :], "zslab", up)
    high = lax.ppermute(block[: SYSTEMS // 2], "zslab", down)
    swap = [(i, i ^ 1) for i in range(4)]
    other = lax.ppermute(block[:, 16:ROWS_AT], "group", swap)
    inner = call(
        inner_kernel,
        (f32(SYSTEMS, 2, OWN, TILES, 8, 128), f32(2, OWN, TILES, 8, 128), f32(128, 8, 128)),
        [SMEM, VMEM, VMEM],
        (VMEM,) * 3,
        (),
        "inner",
        10**8,
    )(place, block, other)
    low, high, inner = lax.optimization_barrier((low, high, inner))
    ends = jnp.concatenate([low[:, 16:ROWS_AT], high[:, 16:ROWS_AT]], axis=0)
    ends = lax.ppermute(ends, "group", swap)
    plane = (TILES, 8, 128)
    basis, gram, dens = call(
        outer_kernel,
        (f32(BASIS, 2, WINDOW, *plane), f32(1, 128), f32(4, 8, 128)),
        [SMEM] + [VMEM] * 7,
        (VMEM, VMEM, VMEM),
        [pltpu.VMEM((2, WINDOW) + plane, jnp.float32), pltpu.VMEM((128, 8, 128), jnp.float32)],
        "outer",
        2 * 10**8,
    )(place, block, low, high, ends, *inner)
    grams = lax.all_to_all(
        jnp.broadcast_to(gram[None], (SYSTEMS, 1, 128)), "zslab", 0, 0,
        axis_index_groups=columns, tiled=True,
    )
    pick, nudge = gram_tables()
    solved = call(
        combine_kernel, f32(SYSTEMS, 33, 8, 128), [VMEM, VMEM, VMEM, VMEM], VMEM, (), "combine"
    )(grams, jnp.asarray(pick), jnp.asarray(nudge), basis)
    fields = lax.all_to_all(solved, "zslab", 0, 0, axis_index_groups=planes_of, tiled=True)
    half = f32(SYSTEMS // 2, 2, 2, 8 * TILES, 128)
    forward, adjoint = call(fields_kernel, (half, half), [VMEM], (VMEM,) * 2, (), "fields", 10**7)(fields)
    keep, give = call(
        terms_kernel,
        (f32(2, 5, 8, 128), f32(2, 5, 8, 128)),
        [SMEM, VMEM],
        (VMEM,) * 2,
        [pltpu.VMEM((4, 8 * TILES, 128), jnp.float32)],
        "terms",
    )(place, fields)
    got = lax.ppermute(give, "group", [(i, i ^ 1) for i in range(4)])
    keep, give = call(
        pair_kernel, (f32(5, 8, 128), f32(5, 8, 128)), [SMEM, VMEM, VMEM], (VMEM, VMEM), (), "pair"
    )(place, keep, got)
    got = lax.ppermute(give, "group", [(i, i ^ 2) for i in range(4)])
    new_density, flag = call(
        density_kernel,
        (f32(2, 8, 128), f32(1)),
        [SMEM, SMEM, VMEM, VMEM, VMEM],
        (VMEM, SMEM),
        (),
        "density",
    )(design_start, place, keep, got, dens)

    def again(state):
        held = (background, absorb, density, profiles, adjoint_source)
        held = row_major(state[0], held, "arguments")
        results = iterate_on_device(*held, port_modes, design_start)
        return (jnp.zeros((), jnp.float32),) + tuple(row_major(state[0], results, "results"))

    state = (flag[0], forward, adjoint, new_density)
    return lax.while_loop(lambda state: state[0] > 0.0, again, state)[1:]


def solution(mesh):
    return jax.shard_map(
        on_device,
        mesh=mesh,
        in_specs=(
            P("zslab", None, None),
            P("zslab", None, None),
            P("zslab", None, None),
            P(None, None, "zslab", None, None),
            P("group", None, "zslab", None, None),
            P("group"),
            P(),
        ),
        out_specs=(
            P("group", None, "zslab", None, None),
            P("group", None, "zslab", None, None),
            P("zslab", "group", None),
        ),
        check_vma=False,
    )
```

```python
import functools

import jax
import jax.numpy as jnp
import numpy as np
from jax import lax
from jax.experimental import pallas as pl
from jax.experimental.pallas import tpu as pltpu
from jax.sharding import PartitionSpec as P

ITERS = 4


wave_sq = 0.1
step_size = 2.0
perm_span = 10.0
low_perm = 2.1
sharpness = 8.0
threshold = 0.5


def with_halo(block, sides, width):
    for axis, dim in sides:
        count = lax.axis_size(axis)
        forward = [(i, i + 1) for i in range(count - 1)]
        backward = [(target, source) for source, target in forward]
        low = lax.ppermute(
            lax.slice_in_dim(block, block.shape[dim] - width, None, axis=dim), axis, forward
        )
        high = lax.ppermute(lax.slice_in_dim(block, 0, width, axis=dim), axis, backward)
        block = jnp.concatenate([low, block, high], axis=dim)
    return block


def scaled(coef, field):
    coef_re = coef[0].reshape((-1, 1, 1, 1))
    coef_im = coef[1].reshape((-1, 1, 1, 1))
    real_part = coef_re * field[:, 0] - coef_im * field[:, 1]
    imag_part = coef_re * field[:, 1] + coef_im * field[:, 0]
    return jnp.stack([real_part, imag_part], axis=1)


def product_pair(left, right):
    real_part = jnp.sum(left[:, 0] * right[:, 0] + left[:, 1] * right[:, 1], axis=(1, 2, 3))
    imag_part = jnp.sum(left[:, 0] * right[:, 1] - left[:, 1] * right[:, 0], axis=(1, 2, 3))
    return (real_part, imag_part)


def divide_pair(top, bottom):
    denominator = bottom[0] * bottom[0] + bottom[1] * bottom[1]
    return (
        (top[0] * bottom[0] + top[1] * bottom[1]) / denominator,
        (top[1] * bottom[0] - top[0] * bottom[1]) / denominator,
    )


def multiply_pair(left, right):
    return (left[0] * right[0] - left[1] * right[1], left[0] * right[1] + left[1] * right[0])


def with_planes(field):
    return with_halo(field, (("zslab", 2),), 1)


def operate(field, diag_re, diag_im):
    padded = jnp.pad(with_planes(field), ((0, 0), (0, 0), (0, 0), (1, 1), (1, 1)))
    beside = padded[:, :, 2:, 1:-1, 1:-1] + padded[:, :, :-2, 1:-1, 1:-1]
    beside = beside + padded[:, :, 1:-1, 2:, 1:-1] + padded[:, :, 1:-1, :-2, 1:-1]
    beside = beside + padded[:, :, 1:-1, 1:-1, 2:] + padded[:, :, 1:-1, 1:-1, :-2]
    real_part = diag_re * field[:, 0] - diag_im * field[:, 1]
    imag_part = diag_re * field[:, 1] + diag_im * field[:, 0]
    return jnp.stack([real_part, imag_part], axis=1) - beside


def bicgstab(sources, diag_re, diag_im):
    solution = jnp.zeros_like(sources)
    residual = sources
    direction = sources
    bilinear = lax.psum(product_pair(sources, residual), "zslab")
    for iteration in range(ITERS):
        image = operate(direction, diag_re, diag_im)
        along = lax.psum(product_pair(sources, image), "zslab")
        advance = divide_pair(bilinear, along)
        halfway = residual - scaled(advance, image)
        second = operate(halfway, diag_re, diag_im)
        cross_re, cross_im = product_pair(second, halfway)
        energy = jnp.sum(second[:, 0] * second[:, 0] + second[:, 1] * second[:, 1], axis=(1, 2, 3))
        cross_re, cross_im, energy = lax.psum((cross_re, cross_im, energy), "zslab")
        relax_coef = (cross_re / energy, cross_im / energy)
        solution = solution + scaled(advance, direction) + scaled(relax_coef, halfway)
        residual = halfway - scaled(relax_coef, second)
        if iteration + 1 < ITERS:
            bilinear_new = lax.psum(product_pair(sources, residual), "zslab")
        if iteration + 1 < ITERS:
            blend_coef = multiply_pair(
                divide_pair(bilinear_new, bilinear), divide_pair(advance, relax_coef)
            )
            direction = residual + scaled(blend_coef, direction - scaled(relax_coef, image))
            bilinear = bilinear_new
    return solution


def iterate_on_device(background, absorb, density, profiles, adjoint_source, port_modes, design_start):
    planes_dev = density.shape[0]
    rows_all = density.shape[1]
    first_plane = lax.axis_index("zslab") * planes_dev
    design_depth = planes_dev * lax.axis_size("zslab") // 2
    planes = first_plane + jnp.arange(planes_dev)
    in_design = (planes >= design_start[0]) & (planes < design_start[0] + design_depth)
    in_design = in_design[:, None, None]
    permittivity = jnp.where(in_design, low_perm + perm_span * density, background)
    diag_re = 6.0 - wave_sq * permittivity
    selector = (port_modes[:, None] == jnp.arange(profiles.shape[0])[None, :]).astype(jnp.float32)
    forward_source = jnp.einsum(
        "pm,mczyx->pczyx", selector, profiles, precision=lax.Precision.HIGHEST
    )
    port_count = forward_source.shape[0]
    sources = jnp.concatenate([forward_source, adjoint_source], axis=0)
    fields = bicgstab(sources, diag_re, absorb)
    forward_field = fields[:port_count]
    adjoint_field = fields[port_count:]
    terms = forward_field[:, 0] * adjoint_field[:, 0] - forward_field[:, 1] * adjoint_field[:, 1]
    local_term = -wave_sq * jnp.sum(terms, axis=0)
    rows_share = rows_all // lax.axis_size("group")
    row_start = lax.axis_index("group") * rows_share
    total = lax.psum(local_term, "group")
    gradient = lax.dynamic_slice_in_dim(total, row_start, rows_share, 1)
    density_rows = lax.dynamic_slice_in_dim(density, row_start, rows_share, 1)
    updated = jnp.where(
        in_design, jnp.clip(density_rows - step_size * perm_span * gradient, 0.0, 1.0), density_rows
    )
    extended = with_halo(updated, (("zslab", 0),), 1)
    padded = jnp.pad(extended, ((0, 0), (0, 0), (1, 1)))
    filtered = (
        2.0 * updated
        + padded[2:, :, 1:-1]
        + padded[:-2, :, 1:-1]
        + padded[1:-1, :, 2:]
        + padded[1:-1, :, :-2]
    ) / 6.0
    new_density = (
        jnp.tanh(sharpness * threshold) + jnp.tanh(sharpness * (filtered - threshold))
    ) / (jnp.tanh(sharpness * threshold) + jnp.tanh(sharpness * (1.0 - threshold)))
    return (forward_field, adjoint_field, new_density)


BASIS = 2 * ITERS + 1
CENTRE = 5.3
HALF_RADIUS = 3.0
THIRD = 1.0 / HALF_RADIUS
NUDGE = 1e-6
AGREE = 5e-4
ROWS = 16 * BASIS


def pair_places():
    real, imag, place = {}, {}, 0
    for j in range(BASIS):
        for i in range(j + 1):
            real[(i, j)] = place
            place += 1
    for j in range(BASIS):
        for i in range(j):
            imag[(i, j)] = place
            place += 1
    return real, imag


def gram_tables():
    real, imag = pair_places()
    pick = np.zeros((2 * ROWS + 16, 128), np.float32)
    nudge = np.zeros((2 * ROWS, 128), np.float32)
    rng = np.random.default_rng(7)
    sign_re = {pair: np.where(rng.random(128) < 0.5, -1.0, 1.0) for pair in real}
    sign_im = {pair: np.where(rng.random(128) < 0.5, -1.0, 1.0) for pair in imag}
    for j in range(BASIS):
        for i in range(BASIS):
            row, pair = j * 16 + i, (min(i, j), max(i, j))
            pick[row, real[pair]] = 1.0
            nudge[row] = NUDGE * sign_re[pair]
            if i != j:
                side = 1.0 if i < j else -1.0
                pick[ROWS + row, imag[pair]] = side
                nudge[ROWS + row] = NUDGE * side * sign_im[pair]
        pick[2 * ROWS + j, real[(j, j)]] = 1.0
    nudge[:, 0] = 0.0
    return pick, nudge


def exact_dot(left, right, dims):
    return lax.dot_general(
        left, right, (dims, ((), ())), precision=lax.Precision.HIGHEST,
        preferred_element_type=jnp.float32,
    )


def minus_pair(left, right):
    return (left[0] - right[0], left[1] - right[1])


def plus_pair(left, right):
    return (left[0] + right[0], left[1] + right[1])


def coefficients(gram_re, gram_im):
    row = lax.broadcasted_iota(jnp.int32, (16, 128), 0)
    keep = jnp.where(row == 15, 0.0, HALF_RADIUS)

    def apply(q):
        return tuple(
            CENTRE * v + HALF_RADIUS * pltpu.roll(v, 1, 0) + keep * pltpu.roll(v, 15, 0) for v in q
        )

    def total(v):
        return jnp.sum(v, axis=0, keepdims=True)

    def with_source(q):
        return (
            total(gram_re[0] * q[0] + gram_im[0] * q[1]),
            total(gram_re[0] * q[1] - gram_im[0] * q[0]),
        )

    def times_gram(q):
        out_re = jnp.zeros((16, 128), jnp.float32)
        out_im = jnp.zeros((16, 128), jnp.float32)
        for j in range(BASIS):
            q_re, q_im = q[0][j : j + 1], q[1][j : j + 1]
            out_re = out_re + (gram_re[j] * q_re - gram_im[j] * q_im)
            out_im = out_im + (gram_re[j] * q_im + gram_im[j] * q_re)
        return out_re, out_im

    one = jnp.where(row == 0, 1.0, 0.0)
    zero = jnp.zeros((16, 128), jnp.float32)
    answer, residual, direction = (zero, zero), (one, zero), (one, zero)
    bilinear = with_source(residual)
    for iteration in range(ITERS):
        image = apply(direction)
        advance = divide_pair(bilinear, with_source(image))
        halfway = minus_pair(residual, multiply_pair(advance, image))
        second = apply(halfway)
        weighed = times_gram(second)
        energy = total(second[0] * weighed[0] + second[1] * weighed[1])
        relax = (
            total(weighed[0] * halfway[0] + weighed[1] * halfway[1]) / energy,
            total(weighed[0] * halfway[1] - weighed[1] * halfway[0]) / energy,
        )
        answer = plus_pair(
            answer, plus_pair(multiply_pair(advance, direction), multiply_pair(relax, halfway))
        )
        if iteration + 1 < ITERS:
            residual = minus_pair(halfway, multiply_pair(relax, second))
            bilinear_new = with_source(residual)
            blend = multiply_pair(divide_pair(bilinear_new, bilinear), divide_pair(advance, relax))
            direction = plus_pair(
                residual, multiply_pair(blend, minus_pair(direction, multiply_pair(relax, image)))
            )
            bilinear = bilinear_new
    first = tuple(jnp.broadcast_to(v[:, :1], v.shape) for v in answer)
    apart = minus_pair(answer, first)

    def norm(q):
        weighed = times_gram(q)
        return total(q[0] * weighed[0] + q[1] * weighed[1])

    return first, norm(apart), norm(first)


TILES = 4
SYSTEMS = 8
BLOCK = 12 * TILES // 2 + 1
ROWS_AT = BLOCK - 1
OWN = 16
WINDOW = 32
CORE = 8
VMEM = pl.BlockSpec(memory_space=pltpu.VMEM)
SMEM = pl.BlockSpec(memory_space=pltpu.SMEM)
HBM = pl.BlockSpec(memory_space=pltpu.HBM)
LIMIT = 24 * 1024 * 1024


def call(kernel, outs, specs, out_specs, scratch=(), name=None, flops=0):
    return pl.pallas_call(
        kernel,
        out_shape=outs,
        in_specs=specs,
        out_specs=out_specs,
        scratch_shapes=list(scratch),
        compiler_params=pltpu.CompilerParams(vmem_limit_bytes=LIMIT),
        cost_estimate=pl.CostEstimate(flops=flops, bytes_accessed=1 << 20, transcendentals=0),
        name=name,
    )


def f32(*shape):
    return jax.ShapeDtypeStruct(shape, jnp.float32)


def rows_of(tile):
    return pl.ds(tile, 8, stride=TILES)


def pack_kernel(modes, start, place, background, absorb, density, profiles, adjoint, out, raw, sems):
    half = SYSTEMS // 2
    copies = []
    for system in range(SYSTEMS):
        source = profiles.at[modes[system]] if system < half else adjoint.at[system - half]
        copies.append(pltpu.make_async_copy(source, raw.at[system], sems.at[system]))
    for copy in copies:
        copy.start()
    for plane in range(2):
        where = place[0] * 2 + plane
        inside = (where >= start[0]) & (where < start[0] + SYSTEMS * SYSTEMS)
        for tile in range(TILES):
            rows = rows_of(tile)
            perm = jnp.where(
                inside, low_perm + perm_span * density[plane, rows], background[plane, rows]
            )
            diag_re = ((6.0 - wave_sq * perm) - CENTRE) * THIRD
            diag_im = absorb[plane, rows] * THIRD
            part = jnp.where(place[1] % 2 == 0, diag_re, diag_im)
            for system in range(SYSTEMS):
                out[system, 16 + plane * TILES + tile] = part
    share = pl.ds(pl.multiple_of(place[1] * 8, 8), 8)
    after = (place[0] + 1) % SYSTEMS
    for slab in range(SYSTEMS):
        out[slab, ROWS_AT] = jnp.where(after == slab, density[1, share], density[0, share])
    for system in range(SYSTEMS):
        copies[system].wait()
        for part in range(2):
            for plane in range(2):
                for tile in range(TILES):
                    out[system, (part * 2 + plane) * TILES + tile] = raw[
                        system, part, plane, rows_of(tile)
                    ]


class Stencil:
    def __init__(self):
        row = lax.broadcasted_iota(jnp.int32, (8, 128), 0)
        lane = lax.broadcasted_iota(jnp.int32, (8, 128), 1)
        self.first_row, self.last_row = row == 0, row == 7
        self.first_lane, self.last_lane = lane == 0, lane == 127

    def beside(self, below, here, above):
        up = jnp.where(self.first_row, 0.0, pltpu.roll(here[TILES - 1], 1, 0))
        down = jnp.where(self.last_row, 0.0, pltpu.roll(here[0], 7, 0))
        rows = [up] + list(here) + [down]
        sums = []
        for tile in range(TILES):
            left = jnp.where(self.first_lane, 0.0, pltpu.roll(here[tile], 1, 1))
            right = jnp.where(self.last_lane, 0.0, pltpu.roll(here[tile], 127, 1))
            z_sum = below[tile] + above[tile]
            sums.append((z_sum + (rows[tile] + rows[tile + 2])) + (left + right))
        return sums

    def step(self, basis, diag, level, at, third):
        def plane(part, where):
            return [basis[level, part, where, tile] for tile in range(TILES)]

        real, imag = plane(0, at), plane(1, at)
        near_re = self.beside(plane(0, at - 1), real, plane(0, at + 1))
        near_im = self.beside(plane(1, at - 1), imag, plane(1, at + 1))
        for tile in range(TILES):
            diag_re, diag_im = diag[0, at, tile], diag[1, at, tile]
            new_re = diag_re * real[tile] - diag_im * imag[tile] - third * near_re[tile]
            new_im = diag_re * imag[tile] + diag_im * real[tile] - third * near_im[tile]
            if level > 0:
                new_re = new_re - basis[level - 1, 0, at, tile]
                new_im = new_im - basis[level - 1, 1, at, tile]
            basis[level + 1, 0, at, tile] = new_re
            basis[level + 1, 1, at, tile] = new_im


def gram_pass(basis, acc, columns, ranges, shift):
    real_at, imag_at = pair_places()
    pairs = [(i, j) for j in columns for i in range(j + 1)]
    top = max(columns) + 1
    places = []
    for pair in pairs:
        places.append(real_at[pair])
        if pair[0] != pair[1]:
            places.append(imag_at[pair])

    def position(step, sums, first=0):
        window, tile = first + shift + step // TILES, step % TILES
        field = [(basis[k, 0, window, tile], basis[k, 1, window, tile]) for k in range(top)]
        new = []
        for i, j in pairs:
            (i_re, i_im), (j_re, j_im) = field[i], field[j]
            new.append(i_re * j_re + i_im * j_im)
            if i != j:
                new.append(i_re * j_im - i_im * j_re)
        return tuple(total + term for total, term in zip(sums, new))

    sums = tuple(acc[at] for at in places)
    for first, last in ranges:
        sums = lax.fori_loop(
            0, (last - first) * TILES, functools.partial(position, first=first), sums,
            unroll=TILES,
        )
    for at, value in zip(places, sums):
        acc[at] = value


def inner_kernel(place, block, other, basis, diag, acc):
    core = place[1] % 2

    def load(chunk, _):
        for plane in range(2):
            for part in range(2):
                for tile in range(TILES):
                    at = part * 8 + plane * TILES + tile
                    basis[0, part, 2 * chunk + plane, tile] = block[chunk, at]
            for tile in range(TILES):
                at = plane * TILES + tile
                diag[core, 2 * chunk + plane, tile] = block[chunk, 16 + at]
                diag[1 - core, 2 * chunk + plane, tile] = other[chunk, at]
        return 0

    lax.fori_loop(0, SYSTEMS, load, 0, unroll=SYSTEMS)
    stencil = Stencil()
    for level in range(SYSTEMS - 1):

        def plane_step(at, _, level=level):
            stencil.step(basis, diag, level, at, THIRD)
            return 0

        lax.fori_loop(
            level + 1, OWN - 1 - level, plane_step, 0, unroll=OWN - 2 - 2 * level
        )
    acc[...] = jnp.zeros_like(acc)
    for columns, ranges in INNER_PASSES:
        gram_pass(basis, acc, columns, ranges, 0)


INNER_PASSES = (
    ((0, 1, 2, 3, 4), ((4, 12),)),
    ((0, 1, 2), ((2, 4), (12, 14))),
    ((5, 6), ((6, 10),)),
)
OUTER_PASSES = (
    ((0, 1, 2, 3, 4), ((0, 2), (14, 16))),
    ((3, 4), ((2, 4), (12, 14))),
    ((5, 6), ((0, 6), (10, 16))),
    ((7,), ((0, 16),)),
    ((8,), ((0, 16),)),
)


def outer_kernel(
    place, density, block, low, high, other, inner, inner_diag, inner_acc, basis, gram, dens, diag, acc
):
    core = place[1] % 2

    def load(source, first, at):
        def one(chunk, _):
            for plane in range(2):
                window = at + 2 * chunk + plane
                for part in range(2):
                    for tile in range(TILES):
                        spot = part * 8 + plane * TILES + tile
                        basis[0, part, window, tile] = source[chunk, spot]
                for tile in range(TILES):
                    spot = plane * TILES + tile
                    diag[core, window, tile] = source[chunk, 16 + spot]
                    diag[1 - core, window, tile] = other[first + chunk, spot]
            return 0

        lax.fori_loop(0, SYSTEMS // 2, one, 0, unroll=SYSTEMS // 2)

    load(low, 0, 0)
    load(high, SYSTEMS // 2, CORE + OWN)
    for level in range(SYSTEMS):

        def keep(at, _, level=level):
            for part in range(2):
                for tile in range(TILES):
                    basis[level, part, CORE + at, tile] = inner[level, part, at, tile]
                    if level == 0:
                        diag[part, CORE + at, tile] = inner_diag[part, at, tile]
            return 0

        lax.fori_loop(level, OWN - level, keep, 0, unroll=OWN - 2 * level)
    acc[...] = inner_acc[...]

    me = place[0] % SYSTEMS
    share = pl.ds(pl.multiple_of(place[1] * 8, 8), 8)
    dens[0] = jnp.where(
        me > 0, block[jnp.maximum(me - 1, 0), ROWS_AT], low[SYSTEMS // 2 - 1, ROWS_AT]
    )
    dens[1] = density[0, share]
    dens[2] = density[1, share]
    dens[3] = jnp.where(
        me < SYSTEMS - 1, block[jnp.minimum(me + 1, SYSTEMS - 1), ROWS_AT], high[0, ROWS_AT]
    )

    third_low = jnp.where(place[0] >= SYSTEMS, THIRD, 0.0)
    third_high = jnp.where(place[0] < SYSTEMS * (SYSTEMS - 1), THIRD, 0.0)
    stencil = Stencil()
    for level in range(BASIS - 1):

        def two_planes(step, _, level=level):
            lower, upper = level + 1 + step, WINDOW - 2 - level - step
            stencil.step(basis, diag, level, lower, jnp.where(lower < CORE, third_low, THIRD))
            stencil.step(
                basis, diag, level, upper, jnp.where(upper >= CORE + OWN, third_high, THIRD)
            )
            return 0

        lax.fori_loop(0, CORE, two_planes, 0, unroll=CORE)
    for columns, ranges in OUTER_PASSES:
        gram_pass(basis, acc, columns, ranges, CORE)
    by_pair = jnp.sum(acc[...], axis=1)
    ones = jnp.ones((8, 128), jnp.float32)
    gram[...] = exact_dot(ones, by_pair, ((1,), (1,)))[0:1]


def combine_kernel(grams, pick, nudge, basis, out):
    row = grams[0]
    for other in range(1, SYSTEMS):
        row = row + grams[other]
    ones = jnp.ones((128, 128), jnp.float32)
    picked = exact_dot(pick[...] * row, ones, ((1,), (0,)))
    norms = jnp.sqrt(picked[2 * ROWS :])
    gram = []
    for column in range(2 * BASIS):
        rows = slice(16 * column, 16 * column + 16)
        scale = norms * norms[column % BASIS : column % BASIS + 1]
        gram.append(picked[rows] + nudge[rows] * scale)
    answer, apart, size = coefficients(gram[:BASIS], gram[BASIS:])
    agrees = jnp.max(jnp.where(apart <= AGREE * AGREE * size, 0.0, 1.0))
    flag = jnp.zeros((8, 128), jnp.float32) + agrees
    for slab in range(SYSTEMS):
        out[slab, 32] = flag
    weight = [
        (
            jnp.broadcast_to(answer[0][k : k + 1], (8, 128)),
            jnp.broadcast_to(answer[1][k : k + 1], (8, 128)),
        )
        for k in range(BASIS - 1)
    ]

    def solve_plane(plane, goals):
        for tile in range(TILES):
            real = jnp.zeros((8, 128), jnp.float32)
            imag = jnp.zeros((8, 128), jnp.float32)
            for k in range(BASIS - 1):
                b_re, b_im = basis[k, 0, plane, tile], basis[k, 1, plane, tile]
                real = real + (weight[k][0] * b_re - weight[k][1] * b_im)
                imag = imag + (weight[k][0] * b_im + weight[k][1] * b_re)
            for slab, at in goals:
                out[slab, at * TILES + tile] = real
                out[slab, (4 + at) * TILES + tile] = imag

    def middle(slab, _):
        for plane in range(2):
            solve_plane(CORE - 1 + 2 * slab + plane, ((slab, plane), (slab - 1, 2 + plane)))
        return 0

    for plane in range(2):
        solve_plane(CORE - 1 + plane, ((0, plane),))
        solve_plane(CORE + OWN - 1 + plane, ((SYSTEMS - 1, 2 + plane),))
    lax.fori_loop(1, SYSTEMS, middle, 0)


def fields_kernel(fields, forward, adjoint):
    half = SYSTEMS // 2
    for port in range(half):
        for part in range(2):
            for plane in range(2):
                for tile in range(TILES):
                    at = (part * 4 + 1 + plane) * TILES + tile
                    forward[port, part, plane, rows_of(tile)] = fields[port, at]
                    adjoint[port, part, plane, rows_of(tile)] = fields[half + port, at]


def terms_kernel(place, fields, keep, give, natural):
    half = SYSTEMS // 2
    for plane in range(4):
        for tile in range(TILES):
            real, imag = plane * TILES + tile, (4 + plane) * TILES + tile
            total = None
            for port in range(half):
                term = fields[port, real] * fields[half + port, real]
                term = term - fields[port, imag] * fields[half + port, imag]
                total = term if total is None else total + term
            natural[plane, rows_of(tile)] = total
    flag = fields[0, 32]
    for system in range(1, SYSTEMS):
        flag = flag + fields[system, 32]
    core = place[1] % 2
    for out, side in ((keep, core), (give, 1 - core)):
        for pair in range(2):
            rows = pl.ds(pl.multiple_of((2 * pair + side) * 8, 8), 8)
            for plane in range(4):
                out[pair, plane] = natural[plane, rows]
            out[pair, 4] = flag


def pair_kernel(place, mine, other, keep, give):
    own = place[1] // 2
    for at in range(5):
        keep[at] = mine[own, at] + other[own, at]
        give[at] = mine[1 - own, at] + other[1 - own, at]


def density_kernel(start, place, mine, other, dens, out, flag):
    lane = lax.broadcasted_iota(jnp.int32, (8, 128), 1)
    updated = []
    for plane in range(4):
        gradient = -wave_sq * (mine[plane] + other[plane])
        where = place[0] * 2 + plane - 1
        inside = (where >= start[0]) & (where < start[0] + SYSTEMS * SYSTEMS)
        rows = dens[plane]
        moved = jnp.clip(rows - step_size * perm_span * gradient, 0.0, 1.0)
        rows = jnp.where(inside, moved, rows)
        exists = (where >= 0) & (where < 2 * SYSTEMS * SYSTEMS)
        updated.append(jnp.where(exists, rows, 0.0))
    for plane in range(2):
        own = updated[plane + 1]
        right = jnp.where(lane == 127, 0.0, pltpu.roll(own, 127, 1))
        left = jnp.where(lane == 0, 0.0, pltpu.roll(own, 1, 1))
        filtered = (2.0 * own + updated[plane + 2] + updated[plane] + right + left) / 6.0
        edge = float(np.tanh(sharpness * threshold))
        other_edge = float(np.tanh(sharpness * (1.0 - threshold)))
        out[plane] = (edge + jnp.tanh(sharpness * (filtered - threshold))) / (edge + other_edge)
    flag[0] = jnp.max(mine[4] + other[4])


def copy_kernel(count, *refs):
    sems = refs[-1]
    arrays = refs[-1 - 2 * count : -1]
    copies = [
        pltpu.make_async_copy(arrays[at], arrays[count + at], sems.at[at]) for at in range(count)
    ]
    for copy in copies:
        copy.start()
    for copy in copies:
        copy.wait()


def row_major(mark, arrays, name):
    count = len(arrays)
    return call(
        functools.partial(copy_kernel, count),
        tuple(jax.ShapeDtypeStruct(array.shape, array.dtype) for array in arrays),
        [SMEM] + [HBM] * count,
        (HBM,) * count,
        [pltpu.SemaphoreType.DMA((count,))],
        name,
    )(mark.reshape(1), *arrays)


def on_device(background, absorb, density, profiles, adjoint_source, port_modes, design_start):
    slab = lax.axis_index("zslab")
    place = jnp.stack([slab, lax.axis_index("group")]).astype(jnp.int32)
    planes_of = [[z * SYSTEMS + l for l in range(SYSTEMS)] for z in range(SYSTEMS)]
    columns = [[z * SYSTEMS + l for z in range(SYSTEMS)] for l in range(SYSTEMS)]
    packed = call(
        pack_kernel,
        f32(SYSTEMS, BLOCK, 8, 128),
        [SMEM, SMEM, SMEM, VMEM, VMEM, VMEM, HBM, HBM],
        VMEM,
        [
            pltpu.VMEM((SYSTEMS,) + profiles.shape[1:], jnp.float32),
            pltpu.SemaphoreType.DMA((SYSTEMS,)),
        ],
        "pack",
    )(port_modes, design_start, place, background, absorb, density, profiles, adjoint_source)
    block = lax.all_to_all(packed, "zslab", 0, 0, axis_index_groups=planes_of, tiled=True)
    count = SYSTEMS * SYSTEMS
    up = [(i, i + SYSTEMS) for i in range(count - SYSTEMS)]
    down = [(target, source) for source, target in up]
    low = lax.ppermute(block[SYSTEMS // 2 :], "zslab", up)
    high = lax.ppermute(block[: SYSTEMS // 2], "zslab", down)
    swap = [(i, i ^ 1) for i in range(4)]
    other = lax.ppermute(block[:, 16:ROWS_AT], "group", swap)
    inner = call(
        inner_kernel,
        (f32(SYSTEMS, 2, OWN, TILES, 8, 128), f32(2, OWN, TILES, 8, 128), f32(128, 8, 128)),
        [SMEM, VMEM, VMEM],
        (VMEM,) * 3,
        (),
        "inner",
        10**8,
    )(place, block, other)
    low, high, inner = lax.optimization_barrier((low, high, inner))
    ends = jnp.concatenate([low[:, 16:ROWS_AT], high[:, 16:ROWS_AT]], axis=0)
    ends = lax.ppermute(ends, "group", swap)
    plane = (TILES, 8, 128)
    basis, gram, dens = call(
        outer_kernel,
        (f32(BASIS, 2, WINDOW, *plane), f32(1, 128), f32(4, 8, 128)),
        [SMEM] + [VMEM] * 8,
        (VMEM, VMEM, VMEM),
        [pltpu.VMEM((2, WINDOW) + plane, jnp.float32), pltpu.VMEM((128, 8, 128), jnp.float32)],
        "outer",
        2 * 10**8,
    )(place, density, block, low, high, ends, *inner)
    grams = lax.all_to_all(
        jnp.broadcast_to(gram[None], (SYSTEMS, 1, 128)), "zslab", 0, 0,
        axis_index_groups=columns, tiled=True,
    )
    pick, nudge = gram_tables()
    solved = call(
        combine_kernel, f32(SYSTEMS, 33, 8, 128), [VMEM, VMEM, VMEM, VMEM], VMEM, (), "combine"
    )(grams, jnp.asarray(pick), jnp.asarray(nudge), basis)
    fields = lax.all_to_all(solved, "zslab", 0, 0, axis_index_groups=planes_of, tiled=True)
    half = f32(SYSTEMS // 2, 2, 2, 8 * TILES, 128)
    forward, adjoint = call(fields_kernel, (half, half), [VMEM], (VMEM,) * 2, (), "fields", 10**7)(fields)
    keep, give = call(
        terms_kernel,
        (f32(2, 5, 8, 128), f32(2, 5, 8, 128)),
        [SMEM, VMEM],
        (VMEM,) * 2,
        [pltpu.VMEM((4, 8 * TILES, 128), jnp.float32)],
        "terms",
    )(place, fields)
    got = lax.ppermute(give, "group", [(i, i ^ 1) for i in range(4)])
    keep, give = call(
        pair_kernel, (f32(5, 8, 128), f32(5, 8, 128)), [SMEM, VMEM, VMEM], (VMEM, VMEM), (), "pair"
    )(place, keep, got)
    got = lax.ppermute(give, "group", [(i, i ^ 2) for i in range(4)])
    new_density, flag = call(
        density_kernel,
        (f32(2, 8, 128), f32(1)),
        [SMEM, SMEM, VMEM, VMEM, VMEM],
        (VMEM, SMEM),
        (),
        "density",
    )(design_start, place, keep, got, dens)

    def again(state):
        held = (background, absorb, density, profiles, adjoint_source)
        held = row_major(state[0], held, "arguments")
        results = iterate_on_device(*held, port_modes, design_start)
        return (jnp.zeros((), jnp.float32),) + tuple(row_major(state[0], results, "results"))

    state = (flag[0], forward, adjoint, new_density)
    return lax.while_loop(lambda state: state[0] > 0.0, again, state)[1:]


def solution(mesh):
    return jax.shard_map(
        on_device,
        mesh=mesh,
        in_specs=(
            P("zslab", None, None),
            P("zslab", None, None),
            P("zslab", None, None),
            P(None, None, "zslab", None, None),
            P("group", None, "zslab", None, None),
            P("group"),
            P(),
        ),
        out_specs=(
            P("group", None, "zslab", None, None),
            P("group", None, "zslab", None, None),
            P("zslab", "group", None),
        ),
        check_vma=False,
    )
```

```python
import functools

import jax
import jax.numpy as jnp
import numpy as np
from jax import lax
from jax.experimental import pallas as pl
from jax.experimental.pallas import tpu as pltpu
from jax.sharding import PartitionSpec as P

ITERS = 4


wave_sq = 0.1
step_size = 2.0
perm_span = 10.0
low_perm = 2.1
sharpness = 8.0
threshold = 0.5


def with_halo(block, sides, width):
    for axis, dim in sides:
        count = lax.axis_size(axis)
        forward = [(i, i + 1) for i in range(count - 1)]
        backward = [(target, source) for source, target in forward]
        low = lax.ppermute(
            lax.slice_in_dim(block, block.shape[dim] - width, None, axis=dim), axis, forward
        )
        high = lax.ppermute(lax.slice_in_dim(block, 0, width, axis=dim), axis, backward)
        block = jnp.concatenate([low, block, high], axis=dim)
    return block


def scaled(coef, field):
    coef_re = coef[0].reshape((-1, 1, 1, 1))
    coef_im = coef[1].reshape((-1, 1, 1, 1))
    real_part = coef_re * field[:, 0] - coef_im * field[:, 1]
    imag_part = coef_re * field[:, 1] + coef_im * field[:, 0]
    return jnp.stack([real_part, imag_part], axis=1)


def product_pair(left, right):
    real_part = jnp.sum(left[:, 0] * right[:, 0] + left[:, 1] * right[:, 1], axis=(1, 2, 3))
    imag_part = jnp.sum(left[:, 0] * right[:, 1] - left[:, 1] * right[:, 0], axis=(1, 2, 3))
    return (real_part, imag_part)


def divide_pair(top, bottom):
    denominator = bottom[0] * bottom[0] + bottom[1] * bottom[1]
    return (
        (top[0] * bottom[0] + top[1] * bottom[1]) / denominator,
        (top[1] * bottom[0] - top[0] * bottom[1]) / denominator,
    )


def multiply_pair(left, right):
    return (left[0] * right[0] - left[1] * right[1], left[0] * right[1] + left[1] * right[0])


def with_planes(field):
    return with_halo(field, (("zslab", 2),), 1)


def operate(field, diag_re, diag_im):
    padded = jnp.pad(with_planes(field), ((0, 0), (0, 0), (0, 0), (1, 1), (1, 1)))
    beside = padded[:, :, 2:, 1:-1, 1:-1] + padded[:, :, :-2, 1:-1, 1:-1]
    beside = beside + padded[:, :, 1:-1, 2:, 1:-1] + padded[:, :, 1:-1, :-2, 1:-1]
    beside = beside + padded[:, :, 1:-1, 1:-1, 2:] + padded[:, :, 1:-1, 1:-1, :-2]
    real_part = diag_re * field[:, 0] - diag_im * field[:, 1]
    imag_part = diag_re * field[:, 1] + diag_im * field[:, 0]
    return jnp.stack([real_part, imag_part], axis=1) - beside


def bicgstab(sources, diag_re, diag_im):
    solution = jnp.zeros_like(sources)
    residual = sources
    direction = sources
    bilinear = lax.psum(product_pair(sources, residual), "zslab")
    for iteration in range(ITERS):
        image = operate(direction, diag_re, diag_im)
        along = lax.psum(product_pair(sources, image), "zslab")
        advance = divide_pair(bilinear, along)
        halfway = residual - scaled(advance, image)
        second = operate(halfway, diag_re, diag_im)
        cross_re, cross_im = product_pair(second, halfway)
        energy = jnp.sum(second[:, 0] * second[:, 0] + second[:, 1] * second[:, 1], axis=(1, 2, 3))
        cross_re, cross_im, energy = lax.psum((cross_re, cross_im, energy), "zslab")
        relax_coef = (cross_re / energy, cross_im / energy)
        solution = solution + scaled(advance, direction) + scaled(relax_coef, halfway)
        residual = halfway - scaled(relax_coef, second)
        if iteration + 1 < ITERS:
            bilinear_new = lax.psum(product_pair(sources, residual), "zslab")
        if iteration + 1 < ITERS:
            blend_coef = multiply_pair(
                divide_pair(bilinear_new, bilinear), divide_pair(advance, relax_coef)
            )
            direction = residual + scaled(blend_coef, direction - scaled(relax_coef, image))
            bilinear = bilinear_new
    return solution


def iterate_on_device(background, absorb, density, profiles, adjoint_source, port_modes, design_start):
    planes_dev = density.shape[0]
    rows_all = density.shape[1]
    first_plane = lax.axis_index("zslab") * planes_dev
    design_depth = planes_dev * lax.axis_size("zslab") // 2
    planes = first_plane + jnp.arange(planes_dev)
    in_design = (planes >= design_start[0]) & (planes < design_start[0] + design_depth)
    in_design = in_design[:, None, None]
    permittivity = jnp.where(in_design, low_perm + perm_span * density, background)
    diag_re = 6.0 - wave_sq * permittivity
    selector = (port_modes[:, None] == jnp.arange(profiles.shape[0])[None, :]).astype(jnp.float32)
    forward_source = jnp.einsum(
        "pm,mczyx->pczyx", selector, profiles, precision=lax.Precision.HIGHEST
    )
    port_count = forward_source.shape[0]
    sources = jnp.concatenate([forward_source, adjoint_source], axis=0)
    fields = bicgstab(sources, diag_re, absorb)
    forward_field = fields[:port_count]
    adjoint_field = fields[port_count:]
    terms = forward_field[:, 0] * adjoint_field[:, 0] - forward_field[:, 1] * adjoint_field[:, 1]
    local_term = -wave_sq * jnp.sum(terms, axis=0)
    rows_share = rows_all // lax.axis_size("group")
    row_start = lax.axis_index("group") * rows_share
    total = lax.psum(local_term, "group")
    gradient = lax.dynamic_slice_in_dim(total, row_start, rows_share, 1)
    density_rows = lax.dynamic_slice_in_dim(density, row_start, rows_share, 1)
    updated = jnp.where(
        in_design, jnp.clip(density_rows - step_size * perm_span * gradient, 0.0, 1.0), density_rows
    )
    extended = with_halo(updated, (("zslab", 0),), 1)
    padded = jnp.pad(extended, ((0, 0), (0, 0), (1, 1)))
    filtered = (
        2.0 * updated
        + padded[2:, :, 1:-1]
        + padded[:-2, :, 1:-1]
        + padded[1:-1, :, 2:]
        + padded[1:-1, :, :-2]
    ) / 6.0
    new_density = (
        jnp.tanh(sharpness * threshold) + jnp.tanh(sharpness * (filtered - threshold))
    ) / (jnp.tanh(sharpness * threshold) + jnp.tanh(sharpness * (1.0 - threshold)))
    return (forward_field, adjoint_field, new_density)


BASIS = 2 * ITERS + 1
CENTRE = 5.3
HALF_RADIUS = 3.0
THIRD = 1.0 / HALF_RADIUS
NUDGE = 1e-6
AGREE = 5e-4
ROWS = 16 * BASIS


def pair_places():
    real, imag, place = {}, {}, 0
    for j in range(BASIS):
        for i in range(j + 1):
            real[(i, j)] = place
            place += 1
    for j in range(BASIS):
        for i in range(j):
            imag[(i, j)] = place
            place += 1
    return real, imag


def gram_tables():
    real, imag = pair_places()
    pick = np.zeros((2 * ROWS + 16, 128), np.float32)
    nudge = np.zeros((2 * ROWS, 128), np.float32)
    rng = np.random.default_rng(7)
    sign_re = {pair: np.where(rng.random(128) < 0.5, -1.0, 1.0) for pair in real}
    sign_im = {pair: np.where(rng.random(128) < 0.5, -1.0, 1.0) for pair in imag}
    for j in range(BASIS):
        for i in range(BASIS):
            row, pair = j * 16 + i, (min(i, j), max(i, j))
            pick[row, real[pair]] = 1.0
            nudge[row] = NUDGE * sign_re[pair]
            if i != j:
                side = 1.0 if i < j else -1.0
                pick[ROWS + row, imag[pair]] = side
                nudge[ROWS + row] = NUDGE * side * sign_im[pair]
        pick[2 * ROWS + j, real[(j, j)]] = 1.0
    nudge[:, 0] = 0.0
    return pick, nudge


def exact_dot(left, right, dims):
    return lax.dot_general(
        left, right, (dims, ((), ())), precision=lax.Precision.HIGHEST,
        preferred_element_type=jnp.float32,
    )


def minus_pair(left, right):
    return (left[0] - right[0], left[1] - right[1])


def plus_pair(left, right):
    return (left[0] + right[0], left[1] + right[1])


def coefficients(gram_re, gram_im):
    row = lax.broadcasted_iota(jnp.int32, (16, 128), 0)
    keep = jnp.where(row == 15, 0.0, HALF_RADIUS)

    def apply(q):
        return tuple(
            CENTRE * v + HALF_RADIUS * pltpu.roll(v, 1, 0) + keep * pltpu.roll(v, 15, 0) for v in q
        )

    def total(v):
        return jnp.sum(v, axis=0, keepdims=True)

    def with_source(q):
        return (
            total(gram_re[0] * q[0] + gram_im[0] * q[1]),
            total(gram_re[0] * q[1] - gram_im[0] * q[0]),
        )

    def times_gram(q):
        out_re = jnp.zeros((16, 128), jnp.float32)
        out_im = jnp.zeros((16, 128), jnp.float32)
        for j in range(BASIS):
            q_re, q_im = q[0][j : j + 1], q[1][j : j + 1]
            out_re = out_re + (gram_re[j] * q_re - gram_im[j] * q_im)
            out_im = out_im + (gram_re[j] * q_im + gram_im[j] * q_re)
        return out_re, out_im

    one = jnp.where(row == 0, 1.0, 0.0)
    zero = jnp.zeros((16, 128), jnp.float32)
    answer, residual, direction = (zero, zero), (one, zero), (one, zero)
    bilinear = with_source(residual)
    for iteration in range(ITERS):
        image = apply(direction)
        advance = divide_pair(bilinear, with_source(image))
        halfway = minus_pair(residual, multiply_pair(advance, image))
        second = apply(halfway)
        weighed = times_gram(second)
        energy = total(second[0] * weighed[0] + second[1] * weighed[1])
        relax = (
            total(weighed[0] * halfway[0] + weighed[1] * halfway[1]) / energy,
            total(weighed[0] * halfway[1] - weighed[1] * halfway[0]) / energy,
        )
        answer = plus_pair(
            answer, plus_pair(multiply_pair(advance, direction), multiply_pair(relax, halfway))
        )
        if iteration + 1 < ITERS:
            residual = minus_pair(halfway, multiply_pair(relax, second))
            bilinear_new = with_source(residual)
            blend = multiply_pair(divide_pair(bilinear_new, bilinear), divide_pair(advance, relax))
            direction = plus_pair(
                residual, multiply_pair(blend, minus_pair(direction, multiply_pair(relax, image)))
            )
            bilinear = bilinear_new
    first = tuple(jnp.broadcast_to(v[:, :1], v.shape) for v in answer)
    apart = minus_pair(answer, first)

    def norm(q):
        weighed = times_gram(q)
        return total(q[0] * weighed[0] + q[1] * weighed[1])

    return first, norm(apart), norm(first)


TILES = 4
SYSTEMS = 8
BLOCK = 12 * TILES // 2 + 1
ROWS_AT = BLOCK - 1
OWN = 16
WINDOW = 32
CORE = 8
VMEM = pl.BlockSpec(memory_space=pltpu.VMEM)
SMEM = pl.BlockSpec(memory_space=pltpu.SMEM)
HBM = pl.BlockSpec(memory_space=pltpu.HBM)
LIMIT = 24 * 1024 * 1024


def call(kernel, outs, specs, out_specs, scratch=(), name=None, flops=0):
    return pl.pallas_call(
        kernel,
        out_shape=outs,
        in_specs=specs,
        out_specs=out_specs,
        scratch_shapes=list(scratch),
        compiler_params=pltpu.CompilerParams(vmem_limit_bytes=LIMIT),
        cost_estimate=pl.CostEstimate(flops=flops, bytes_accessed=1 << 20, transcendentals=0),
        name=name,
    )


def f32(*shape):
    return jax.ShapeDtypeStruct(shape, jnp.float32)


def rows_of(tile):
    return pl.ds(tile, 8, stride=TILES)


def pack_kernel(
    modes, start, place, back_arg, absorb_arg, density_arg, profiles, adjoint,
    out, own, background, absorb, density, raw, sems,
):
    half = SYSTEMS // 2
    copies = []
    for system in range(SYSTEMS):
        source = profiles.at[modes[system]] if system < half else adjoint.at[system - half]
        copies.append(pltpu.make_async_copy(source, raw.at[system], sems.at[system]))
    held = [
        pltpu.make_async_copy(array, room, sems.at[SYSTEMS + at])
        for at, (array, room) in enumerate(
            ((back_arg, background), (absorb_arg, absorb), (density_arg, density))
        )
    ]
    for copy in held + copies:
        copy.start()
    for copy in held:
        copy.wait()
    for plane in range(2):
        where = place[0] * 2 + plane
        inside = (where >= start[0]) & (where < start[0] + SYSTEMS * SYSTEMS)
        for tile in range(TILES):
            rows = rows_of(tile)
            perm = jnp.where(
                inside, low_perm + perm_span * density[plane, rows], background[plane, rows]
            )
            diag_re = ((6.0 - wave_sq * perm) - CENTRE) * THIRD
            diag_im = absorb[plane, rows] * THIRD
            part = jnp.where(place[1] % 2 == 0, diag_re, diag_im)
            for system in range(SYSTEMS):
                out[system, 16 + plane * TILES + tile] = part
    share = pl.ds(pl.multiple_of(place[1] * 8, 8), 8)
    own[0] = density[0, share]
    own[1] = density[1, share]
    after = (place[0] + 1) % SYSTEMS
    for slab in range(SYSTEMS):
        out[slab, ROWS_AT] = jnp.where(after == slab, density[1, share], density[0, share])
    for system in range(SYSTEMS):
        copies[system].wait()
        for part in range(2):
            for plane in range(2):
                for tile in range(TILES):
                    out[system, (part * 2 + plane) * TILES + tile] = raw[
                        system, part, plane, rows_of(tile)
                    ]


class Stencil:
    def __init__(self):
        row = lax.broadcasted_iota(jnp.int32, (8, 128), 0)
        lane = lax.broadcasted_iota(jnp.int32, (8, 128), 1)
        self.first_row, self.last_row = row == 0, row == 7
        self.first_lane, self.last_lane = lane == 0, lane == 127

    def beside(self, below, here, above):
        up = jnp.where(self.first_row, 0.0, pltpu.roll(here[TILES - 1], 1, 0))
        down = jnp.where(self.last_row, 0.0, pltpu.roll(here[0], 7, 0))
        rows = [up] + list(here) + [down]
        sums = []
        for tile in range(TILES):
            left = jnp.where(self.first_lane, 0.0, pltpu.roll(here[tile], 1, 1))
            right = jnp.where(self.last_lane, 0.0, pltpu.roll(here[tile], 127, 1))
            z_sum = below[tile] + above[tile]
            sums.append((z_sum + (rows[tile] + rows[tile + 2])) + (left + right))
        return sums

    def step(self, basis, diag, level, at, third):
        def plane(part, where):
            return [basis[level, part, where, tile] for tile in range(TILES)]

        real, imag = plane(0, at), plane(1, at)
        near_re = self.beside(plane(0, at - 1), real, plane(0, at + 1))
        near_im = self.beside(plane(1, at - 1), imag, plane(1, at + 1))
        for tile in range(TILES):
            diag_re, diag_im = diag[0, at, tile], diag[1, at, tile]
            new_re = diag_re * real[tile] - diag_im * imag[tile] - third * near_re[tile]
            new_im = diag_re * imag[tile] + diag_im * real[tile] - third * near_im[tile]
            if level > 0:
                new_re = new_re - basis[level - 1, 0, at, tile]
                new_im = new_im - basis[level - 1, 1, at, tile]
            basis[level + 1, 0, at, tile] = new_re
            basis[level + 1, 1, at, tile] = new_im


def gram_pass(basis, acc, columns, ranges, shift):
    real_at, imag_at = pair_places()
    pairs = [(i, j) for j in columns for i in range(j + 1)]
    top = max(columns) + 1
    places = []
    for pair in pairs:
        places.append(real_at[pair])
        if pair[0] != pair[1]:
            places.append(imag_at[pair])

    def position(step, sums, first=0):
        window, tile = first + shift + step // TILES, step % TILES
        field = [(basis[k, 0, window, tile], basis[k, 1, window, tile]) for k in range(top)]
        new = []
        for i, j in pairs:
            (i_re, i_im), (j_re, j_im) = field[i], field[j]
            new.append(i_re * j_re + i_im * j_im)
            if i != j:
                new.append(i_re * j_im - i_im * j_re)
        return tuple(total + term for total, term in zip(sums, new))

    sums = tuple(acc[at] for at in places)
    for first, last in ranges:
        sums = lax.fori_loop(
            0, (last - first) * TILES, functools.partial(position, first=first), sums,
            unroll=TILES,
        )
    for at, value in zip(places, sums):
        acc[at] = value


def inner_kernel(place, block, other, basis, diag, acc):
    core = place[1] % 2

    def load(chunk, _):
        for plane in range(2):
            for part in range(2):
                for tile in range(TILES):
                    at = part * 8 + plane * TILES + tile
                    basis[0, part, 2 * chunk + plane, tile] = block[chunk, at]
            for tile in range(TILES):
                at = plane * TILES + tile
                diag[core, 2 * chunk + plane, tile] = block[chunk, 16 + at]
                diag[1 - core, 2 * chunk + plane, tile] = other[chunk, at]
        return 0

    lax.fori_loop(0, SYSTEMS, load, 0, unroll=SYSTEMS)
    stencil = Stencil()
    for level in range(SYSTEMS - 1):

        def plane_step(at, _, level=level):
            stencil.step(basis, diag, level, at, THIRD)
            return 0

        lax.fori_loop(
            level + 1, OWN - 1 - level, plane_step, 0, unroll=OWN - 2 - 2 * level
        )
    acc[...] = jnp.zeros_like(acc)
    for columns, ranges in INNER_PASSES:
        gram_pass(basis, acc, columns, ranges, 0)


INNER_PASSES = (
    ((0, 1, 2, 3, 4), ((4, 12),)),
    ((0, 1, 2), ((2, 4), (12, 14))),
    ((5, 6), ((6, 10),)),
)
OUTER_PASSES = (
    ((0, 1, 2, 3, 4), ((0, 2), (14, 16))),
    ((3, 4), ((2, 4), (12, 14))),
    ((5, 6), ((0, 6), (10, 16))),
    ((7,), ((0, 16),)),
    ((8,), ((0, 16),)),
)


def outer_kernel(
    place, block, low, high, other, inner, inner_diag, inner_acc, basis, gram, dens, diag, acc
):
    core = place[1] % 2

    def load(source, first, at):
        def one(chunk, _):
            for plane in range(2):
                window = at + 2 * chunk + plane
                for part in range(2):
                    for tile in range(TILES):
                        spot = part * 8 + plane * TILES + tile
                        basis[0, part, window, tile] = source[chunk, spot]
                for tile in range(TILES):
                    spot = plane * TILES + tile
                    diag[core, window, tile] = source[chunk, 16 + spot]
                    diag[1 - core, window, tile] = other[first + chunk, spot]
            return 0

        lax.fori_loop(0, SYSTEMS // 2, one, 0, unroll=SYSTEMS // 2)

    load(low, 0, 0)
    load(high, SYSTEMS // 2, CORE + OWN)
    for level in range(SYSTEMS):

        def keep(at, _, level=level):
            for part in range(2):
                for tile in range(TILES):
                    basis[level, part, CORE + at, tile] = inner[level, part, at, tile]
                    if level == 0:
                        diag[part, CORE + at, tile] = inner_diag[part, at, tile]
            return 0

        lax.fori_loop(level, OWN - level, keep, 0, unroll=OWN - 2 * level)
    acc[...] = inner_acc[...]

    me = place[0] % SYSTEMS
    dens[0] = jnp.where(
        me > 0, block[jnp.maximum(me - 1, 0), ROWS_AT], low[SYSTEMS // 2 - 1, ROWS_AT]
    )
    dens[1] = jnp.where(
        me < SYSTEMS - 1, block[jnp.minimum(me + 1, SYSTEMS - 1), ROWS_AT], high[0, ROWS_AT]
    )

    third_low = jnp.where(place[0] >= SYSTEMS, THIRD, 0.0)
    third_high = jnp.where(place[0] < SYSTEMS * (SYSTEMS - 1), THIRD, 0.0)
    stencil = Stencil()
    for level in range(BASIS - 1):

        def two_planes(step, _, level=level):
            lower, upper = level + 1 + step, WINDOW - 2 - level - step
            stencil.step(basis, diag, level, lower, jnp.where(lower < CORE, third_low, THIRD))
            stencil.step(
                basis, diag, level, upper, jnp.where(upper >= CORE + OWN, third_high, THIRD)
            )
            return 0

        lax.fori_loop(0, CORE, two_planes, 0, unroll=CORE)
    for columns, ranges in OUTER_PASSES:
        gram_pass(basis, acc, columns, ranges, CORE)
    by_pair = jnp.sum(acc[...], axis=1)
    ones = jnp.ones((8, 128), jnp.float32)
    gram[...] = exact_dot(ones, by_pair, ((1,), (1,)))[0:1]


def combine_kernel(grams, pick, nudge, basis, out):
    row = grams[0]
    for other in range(1, SYSTEMS):
        row = row + grams[other]
    ones = jnp.ones((128, 128), jnp.float32)
    picked = exact_dot(pick[...] * row, ones, ((1,), (0,)))
    norms = jnp.sqrt(picked[2 * ROWS :])
    gram = []
    for column in range(2 * BASIS):
        rows = slice(16 * column, 16 * column + 16)
        scale = norms * norms[column % BASIS : column % BASIS + 1]
        gram.append(picked[rows] + nudge[rows] * scale)
    answer, apart, size = coefficients(gram[:BASIS], gram[BASIS:])
    agrees = jnp.max(jnp.where(apart <= AGREE * AGREE * size, 0.0, 1.0))
    flag = jnp.zeros((8, 128), jnp.float32) + agrees
    for slab in range(SYSTEMS):
        out[slab, 32] = flag
    weight = [
        (
            jnp.broadcast_to(answer[0][k : k + 1], (8, 128)),
            jnp.broadcast_to(answer[1][k : k + 1], (8, 128)),
        )
        for k in range(BASIS - 1)
    ]

    def solve_plane(plane, goals):
        for tile in range(TILES):
            real = jnp.zeros((8, 128), jnp.float32)
            imag = jnp.zeros((8, 128), jnp.float32)
            for k in range(BASIS - 1):
                b_re, b_im = basis[k, 0, plane, tile], basis[k, 1, plane, tile]
                real = real + (weight[k][0] * b_re - weight[k][1] * b_im)
                imag = imag + (weight[k][0] * b_im + weight[k][1] * b_re)
            for slab, at in goals:
                out[slab, at * TILES + tile] = real
                out[slab, (4 + at) * TILES + tile] = imag

    def middle(slab, _):
        for plane in range(2):
            solve_plane(CORE - 1 + 2 * slab + plane, ((slab, plane), (slab - 1, 2 + plane)))
        return 0

    for plane in range(2):
        solve_plane(CORE - 1 + plane, ((0, plane),))
        solve_plane(CORE + OWN - 1 + plane, ((SYSTEMS - 1, 2 + plane),))
    lax.fori_loop(1, SYSTEMS, middle, 0)


def fields_kernel(fields, forward, adjoint):
    half = SYSTEMS // 2
    for port in range(half):
        for part in range(2):
            for plane in range(2):
                for tile in range(TILES):
                    at = (part * 4 + 1 + plane) * TILES + tile
                    forward[port, part, plane, rows_of(tile)] = fields[port, at]
                    adjoint[port, part, plane, rows_of(tile)] = fields[half + port, at]


def terms_kernel(place, fields, mine, beside, across, natural):
    half = SYSTEMS // 2
    for plane in range(4):
        for tile in range(TILES):
            real, imag = plane * TILES + tile, (4 + plane) * TILES + tile
            total = None
            for port in range(half):
                term = fields[port, real] * fields[half + port, real]
                term = term - fields[port, imag] * fields[half + port, imag]
                total = term if total is None else total + term
            natural[plane, rows_of(tile)] = total
    flag = fields[0, 32]
    for system in range(1, SYSTEMS):
        flag = flag + fields[system, 32]
    core, chip = place[1] % 2, place[1] // 2
    for out, pair, side in (
        (mine, chip, core),
        (beside, chip, 1 - core),
        (across.at[0], 1 - chip, core),
        (across.at[1], 1 - chip, 1 - core),
    ):
        rows = pl.ds(pl.multiple_of((2 * pair + side) * 8, 8), 8)
        for plane in range(4):
            out[plane] = natural[plane, rows]
        out[4] = flag


def density_kernel(start, place, mine, across, beside, own, dens, out, flag):
    lane = lax.broadcasted_iota(jnp.int32, (8, 128), 1)
    updated = []
    for plane in range(4):
        gradient = -wave_sq * (mine[plane] + across[0, plane] + beside[plane])
        where = place[0] * 2 + plane - 1
        inside = (where >= start[0]) & (where < start[0] + SYSTEMS * SYSTEMS)
        rows = (dens[0], own[0], own[1], dens[1])[plane]
        moved = jnp.clip(rows - step_size * perm_span * gradient, 0.0, 1.0)
        rows = jnp.where(inside, moved, rows)
        exists = (where >= 0) & (where < 2 * SYSTEMS * SYSTEMS)
        updated.append(jnp.where(exists, rows, 0.0))
    for plane in range(2):
        own = updated[plane + 1]
        right = jnp.where(lane == 127, 0.0, pltpu.roll(own, 127, 1))
        left = jnp.where(lane == 0, 0.0, pltpu.roll(own, 1, 1))
        filtered = (2.0 * own + updated[plane + 2] + updated[plane] + right + left) / 6.0
        edge = float(np.tanh(sharpness * threshold))
        other_edge = float(np.tanh(sharpness * (1.0 - threshold)))
        out[plane] = (edge + jnp.tanh(sharpness * (filtered - threshold))) / (edge + other_edge)
    flag[0] = jnp.max(mine[4] + across[0, 4] + beside[4])


def copy_kernel(count, *refs):
    sems = refs[-1]
    arrays = refs[-1 - 2 * count : -1]
    copies = [
        pltpu.make_async_copy(arrays[at], arrays[count + at], sems.at[at]) for at in range(count)
    ]
    for copy in copies:
        copy.start()
    for copy in copies:
        copy.wait()


def row_major(mark, arrays, name):
    count = len(arrays)
    return call(
        functools.partial(copy_kernel, count),
        tuple(jax.ShapeDtypeStruct(array.shape, array.dtype) for array in arrays),
        [SMEM] + [HBM] * count,
        (HBM,) * count,
        [pltpu.SemaphoreType.DMA((count,))],
        name,
    )(mark.reshape(1), *arrays)


def on_device(background, absorb, density, profiles, adjoint_source, port_modes, design_start):
    slab = lax.axis_index("zslab")
    place = jnp.stack([slab, lax.axis_index("group")]).astype(jnp.int32)
    planes_of = [[z * SYSTEMS + l for l in range(SYSTEMS)] for z in range(SYSTEMS)]
    columns = [[z * SYSTEMS + l for z in range(SYSTEMS)] for l in range(SYSTEMS)]
    packed, own_rows = call(
        pack_kernel,
        (f32(SYSTEMS, BLOCK, 8, 128), f32(2, 8, 128)),
        [SMEM, SMEM, SMEM] + [HBM] * 5,
        (VMEM, VMEM),
        [pltpu.VMEM(density.shape, jnp.float32)] * 3
        + [
            pltpu.VMEM((SYSTEMS,) + profiles.shape[1:], jnp.float32),
            pltpu.SemaphoreType.DMA((SYSTEMS + 3,)),
        ],
        "pack",
    )(port_modes, design_start, place, background, absorb, density, profiles, adjoint_source)
    block = lax.all_to_all(packed, "zslab", 0, 0, axis_index_groups=planes_of, tiled=True)
    count = SYSTEMS * SYSTEMS
    up = [(i, i + SYSTEMS) for i in range(count - SYSTEMS)]
    down = [(target, source) for source, target in up]
    low = lax.ppermute(block[SYSTEMS // 2 :], "zslab", up)
    high = lax.ppermute(block[: SYSTEMS // 2], "zslab", down)
    swap = [(i, i ^ 1) for i in range(4)]
    other = lax.ppermute(block[:, 16:ROWS_AT], "group", swap)
    inner = call(
        inner_kernel,
        (f32(SYSTEMS, 2, OWN, TILES, 8, 128), f32(2, OWN, TILES, 8, 128), f32(128, 8, 128)),
        [SMEM, VMEM, VMEM],
        (VMEM,) * 3,
        (),
        "inner",
        10**8,
    )(place, block, other)
    low, high, inner = lax.optimization_barrier((low, high, inner))
    ends = jnp.concatenate([low[:, 16:ROWS_AT], high[:, 16:ROWS_AT]], axis=0)
    ends = lax.ppermute(ends, "group", swap)
    plane = (TILES, 8, 128)
    basis, gram, dens = call(
        outer_kernel,
        (f32(BASIS, 2, WINDOW, *plane), f32(1, 128), f32(2, 8, 128)),
        [SMEM] + [VMEM] * 7,
        (VMEM, VMEM, VMEM),
        [pltpu.VMEM((2, WINDOW) + plane, jnp.float32), pltpu.VMEM((128, 8, 128), jnp.float32)],
        "outer",
        2 * 10**8,
    )(place, block, low, high, ends, *inner)
    grams = lax.all_to_all(
        jnp.broadcast_to(gram[None], (SYSTEMS, 1, 128)), "zslab", 0, 0,
        axis_index_groups=columns, tiled=True,
    )
    pick, nudge = gram_tables()
    solved = call(
        combine_kernel, f32(SYSTEMS, 33, 8, 128), [VMEM, VMEM, VMEM, VMEM], VMEM, (), "combine"
    )(grams, jnp.asarray(pick), jnp.asarray(nudge), basis)
    fields = lax.all_to_all(solved, "zslab", 0, 0, axis_index_groups=planes_of, tiled=True)
    half = f32(SYSTEMS // 2, 2, 2, 8 * TILES, 128)
    forward, adjoint = call(fields_kernel, (half, half), [VMEM], (VMEM,) * 2, (), "fields", 10**7)(fields)
    mine, beside, across = call(
        terms_kernel,
        (f32(5, 8, 128), f32(5, 8, 128), f32(2, 5, 8, 128)),
        [SMEM, VMEM],
        (VMEM,) * 3,
        [pltpu.VMEM((4, 8 * TILES, 128), jnp.float32)],
        "terms",
    )(place, fields)
    across = lax.ppermute(across, "group", [(i, i ^ 2) for i in range(4)])
    across, forward, adjoint = lax.optimization_barrier((across, forward, adjoint))
    beside = lax.ppermute(beside + across[1], "group", swap)
    new_density, flag = call(
        density_kernel,
        (f32(2, 8, 128), f32(1)),
        [SMEM, SMEM] + [VMEM] * 5,
        (VMEM, SMEM),
        (),
        "density",
    )(design_start, place, mine, across, beside, own_rows, dens)

    def again(state):
        held = (background, absorb, density, profiles, adjoint_source)
        held = row_major(state[0], held, "arguments")
        results = iterate_on_device(*held, port_modes, design_start)
        return (jnp.zeros((), jnp.float32),) + tuple(row_major(state[0], results, "results"))

    state = (flag[0], forward, adjoint, new_density)
    return lax.while_loop(lambda state: state[0] > 0.0, again, state)[1:]


def solution(mesh):
    return jax.shard_map(
        on_device,
        mesh=mesh,
        in_specs=(
            P("zslab", None, None),
            P("zslab", None, None),
            P("zslab", None, None),
            P(None, None, "zslab", None, None),
            P("group", None, "zslab", None, None),
            P("group"),
            P(),
        ),
        out_specs=(
            P("group", None, "zslab", None, None),
            P("group", None, "zslab", None, None),
            P("zslab", "group", None),
        ),
        check_vma=False,
    )
```

```python
import functools

import jax
import jax.numpy as jnp
import numpy as np
from jax import lax
from jax.experimental import pallas as pl
from jax.experimental.pallas import tpu as pltpu
from jax.sharding import PartitionSpec as P

ITERS = 4


wave_sq = 0.1
step_size = 2.0
perm_span = 10.0
low_perm = 2.1
sharpness = 8.0
threshold = 0.5


def with_halo(block, sides, width):
    for axis, dim in sides:
        count = lax.axis_size(axis)
        forward = [(i, i + 1) for i in range(count - 1)]
        backward = [(target, source) for source, target in forward]
        low = lax.ppermute(
            lax.slice_in_dim(block, block.shape[dim] - width, None, axis=dim), axis, forward
        )
        high = lax.ppermute(lax.slice_in_dim(block, 0, width, axis=dim), axis, backward)
        block = jnp.concatenate([low, block, high], axis=dim)
    return block


def scaled(coef, field):
    coef_re = coef[0].reshape((-1, 1, 1, 1))
    coef_im = coef[1].reshape((-1, 1, 1, 1))
    real_part = coef_re * field[:, 0] - coef_im * field[:, 1]
    imag_part = coef_re * field[:, 1] + coef_im * field[:, 0]
    return jnp.stack([real_part, imag_part], axis=1)


def product_pair(left, right):
    real_part = jnp.sum(left[:, 0] * right[:, 0] + left[:, 1] * right[:, 1], axis=(1, 2, 3))
    imag_part = jnp.sum(left[:, 0] * right[:, 1] - left[:, 1] * right[:, 0], axis=(1, 2, 3))
    return (real_part, imag_part)


def divide_pair(top, bottom):
    denominator = bottom[0] * bottom[0] + bottom[1] * bottom[1]
    return (
        (top[0] * bottom[0] + top[1] * bottom[1]) / denominator,
        (top[1] * bottom[0] - top[0] * bottom[1]) / denominator,
    )


def multiply_pair(left, right):
    return (left[0] * right[0] - left[1] * right[1], left[0] * right[1] + left[1] * right[0])


def with_planes(field):
    return with_halo(field, (("zslab", 2),), 1)


def operate(field, diag_re, diag_im):
    padded = jnp.pad(with_planes(field), ((0, 0), (0, 0), (0, 0), (1, 1), (1, 1)))
    beside = padded[:, :, 2:, 1:-1, 1:-1] + padded[:, :, :-2, 1:-1, 1:-1]
    beside = beside + padded[:, :, 1:-1, 2:, 1:-1] + padded[:, :, 1:-1, :-2, 1:-1]
    beside = beside + padded[:, :, 1:-1, 1:-1, 2:] + padded[:, :, 1:-1, 1:-1, :-2]
    real_part = diag_re * field[:, 0] - diag_im * field[:, 1]
    imag_part = diag_re * field[:, 1] + diag_im * field[:, 0]
    return jnp.stack([real_part, imag_part], axis=1) - beside


def bicgstab(sources, diag_re, diag_im):
    solution = jnp.zeros_like(sources)
    residual = sources
    direction = sources
    bilinear = lax.psum(product_pair(sources, residual), "zslab")
    for iteration in range(ITERS):
        image = operate(direction, diag_re, diag_im)
        along = lax.psum(product_pair(sources, image), "zslab")
        advance = divide_pair(bilinear, along)
        halfway = residual - scaled(advance, image)
        second = operate(halfway, diag_re, diag_im)
        cross_re, cross_im = product_pair(second, halfway)
        energy = jnp.sum(second[:, 0] * second[:, 0] + second[:, 1] * second[:, 1], axis=(1, 2, 3))
        cross_re, cross_im, energy = lax.psum((cross_re, cross_im, energy), "zslab")
        relax_coef = (cross_re / energy, cross_im / energy)
        solution = solution + scaled(advance, direction) + scaled(relax_coef, halfway)
        residual = halfway - scaled(relax_coef, second)
        if iteration + 1 < ITERS:
            bilinear_new = lax.psum(product_pair(sources, residual), "zslab")
        if iteration + 1 < ITERS:
            blend_coef = multiply_pair(
                divide_pair(bilinear_new, bilinear), divide_pair(advance, relax_coef)
            )
            direction = residual + scaled(blend_coef, direction - scaled(relax_coef, image))
            bilinear = bilinear_new
    return solution


def iterate_on_device(background, absorb, density, profiles, adjoint_source, port_modes, design_start):
    planes_dev = density.shape[0]
    rows_all = density.shape[1]
    first_plane = lax.axis_index("zslab") * planes_dev
    design_depth = planes_dev * lax.axis_size("zslab") // 2
    planes = first_plane + jnp.arange(planes_dev)
    in_design = (planes >= design_start[0]) & (planes < design_start[0] + design_depth)
    in_design = in_design[:, None, None]
    permittivity = jnp.where(in_design, low_perm + perm_span * density, background)
    diag_re = 6.0 - wave_sq * permittivity
    selector = (port_modes[:, None] == jnp.arange(profiles.shape[0])[None, :]).astype(jnp.float32)
    forward_source = jnp.einsum(
        "pm,mczyx->pczyx", selector, profiles, precision=lax.Precision.HIGHEST
    )
    port_count = forward_source.shape[0]
    sources = jnp.concatenate([forward_source, adjoint_source], axis=0)
    fields = bicgstab(sources, diag_re, absorb)
    forward_field = fields[:port_count]
    adjoint_field = fields[port_count:]
    terms = forward_field[:, 0] * adjoint_field[:, 0] - forward_field[:, 1] * adjoint_field[:, 1]
    local_term = -wave_sq * jnp.sum(terms, axis=0)
    rows_share = rows_all // lax.axis_size("group")
    row_start = lax.axis_index("group") * rows_share
    total = lax.psum(local_term, "group")
    gradient = lax.dynamic_slice_in_dim(total, row_start, rows_share, 1)
    density_rows = lax.dynamic_slice_in_dim(density, row_start, rows_share, 1)
    updated = jnp.where(
        in_design, jnp.clip(density_rows - step_size * perm_span * gradient, 0.0, 1.0), density_rows
    )
    extended = with_halo(updated, (("zslab", 0),), 1)
    padded = jnp.pad(extended, ((0, 0), (0, 0), (1, 1)))
    filtered = (
        2.0 * updated
        + padded[2:, :, 1:-1]
        + padded[:-2, :, 1:-1]
        + padded[1:-1, :, 2:]
        + padded[1:-1, :, :-2]
    ) / 6.0
    new_density = (
        jnp.tanh(sharpness * threshold) + jnp.tanh(sharpness * (filtered - threshold))
    ) / (jnp.tanh(sharpness * threshold) + jnp.tanh(sharpness * (1.0 - threshold)))
    return (forward_field, adjoint_field, new_density)


BASIS = 2 * ITERS + 1
CENTRE = 5.3
HALF_RADIUS = 3.0
THIRD = 1.0 / HALF_RADIUS
NUDGE = 1e-6
AGREE = 5e-4
ROWS = 16 * BASIS


def pair_places():
    real, imag, place = {}, {}, 0
    for j in range(BASIS):
        for i in range(j + 1):
            real[(i, j)] = place
            place += 1
    for j in range(BASIS):
        for i in range(j):
            imag[(i, j)] = place
            place += 1
    return real, imag


def gram_tables():
    real, imag = pair_places()
    pick = np.zeros((2 * ROWS + 16, 128), np.float32)
    nudge = np.zeros((2 * ROWS, 128), np.float32)
    rng = np.random.default_rng(7)
    sign_re = {pair: np.where(rng.random(128) < 0.5, -1.0, 1.0) for pair in real}
    sign_im = {pair: np.where(rng.random(128) < 0.5, -1.0, 1.0) for pair in imag}
    for j in range(BASIS):
        for i in range(BASIS):
            row, pair = j * 16 + i, (min(i, j), max(i, j))
            pick[row, real[pair]] = 1.0
            nudge[row] = NUDGE * sign_re[pair]
            if i != j:
                side = 1.0 if i < j else -1.0
                pick[ROWS + row, imag[pair]] = side
                nudge[ROWS + row] = NUDGE * side * sign_im[pair]
        pick[2 * ROWS + j, real[(j, j)]] = 1.0
    nudge[:, 0] = 0.0
    return pick, nudge


def exact_dot(left, right, dims):
    return lax.dot_general(
        left, right, (dims, ((), ())), precision=lax.Precision.HIGHEST,
        preferred_element_type=jnp.float32,
    )


def minus_pair(left, right):
    return (left[0] - right[0], left[1] - right[1])


def plus_pair(left, right):
    return (left[0] + right[0], left[1] + right[1])


def coefficients(gram_re, gram_im):
    row = lax.broadcasted_iota(jnp.int32, (16, 128), 0)
    keep = jnp.where(row == 15, 0.0, HALF_RADIUS)

    def apply(q):
        return tuple(
            CENTRE * v + HALF_RADIUS * pltpu.roll(v, 1, 0) + keep * pltpu.roll(v, 15, 0) for v in q
        )

    def total(v):
        return jnp.sum(v, axis=0, keepdims=True)

    def with_source(q):
        return (
            total(gram_re[0] * q[0] + gram_im[0] * q[1]),
            total(gram_re[0] * q[1] - gram_im[0] * q[0]),
        )

    def times_gram(q):
        out_re = jnp.zeros((16, 128), jnp.float32)
        out_im = jnp.zeros((16, 128), jnp.float32)
        for j in range(BASIS):
            q_re, q_im = q[0][j : j + 1], q[1][j : j + 1]
            out_re = out_re + (gram_re[j] * q_re - gram_im[j] * q_im)
            out_im = out_im + (gram_re[j] * q_im + gram_im[j] * q_re)
        return out_re, out_im

    one = jnp.where(row == 0, 1.0, 0.0)
    zero = jnp.zeros((16, 128), jnp.float32)
    answer, residual, direction = (zero, zero), (one, zero), (one, zero)
    bilinear = with_source(residual)
    for iteration in range(ITERS):
        image = apply(direction)
        advance = divide_pair(bilinear, with_source(image))
        halfway = minus_pair(residual, multiply_pair(advance, image))
        second = apply(halfway)
        weighed = times_gram(second)
        energy = total(second[0] * weighed[0] + second[1] * weighed[1])
        relax = (
            total(weighed[0] * halfway[0] + weighed[1] * halfway[1]) / energy,
            total(weighed[0] * halfway[1] - weighed[1] * halfway[0]) / energy,
        )
        answer = plus_pair(
            answer, plus_pair(multiply_pair(advance, direction), multiply_pair(relax, halfway))
        )
        if iteration + 1 < ITERS:
            residual = minus_pair(halfway, multiply_pair(relax, second))
            bilinear_new = with_source(residual)
            blend = multiply_pair(divide_pair(bilinear_new, bilinear), divide_pair(advance, relax))
            direction = plus_pair(
                residual, multiply_pair(blend, minus_pair(direction, multiply_pair(relax, image)))
            )
            bilinear = bilinear_new
    first = tuple(jnp.broadcast_to(v[:, :1], v.shape) for v in answer)
    apart = minus_pair(answer, first)

    def norm(q):
        weighed = times_gram(q)
        return total(q[0] * weighed[0] + q[1] * weighed[1])

    return first, norm(apart), norm(first)


TILES = 4
SYSTEMS = 8
BLOCK = 12 * TILES // 2 + 1
ROWS_AT = BLOCK - 1
OWN = 16
WINDOW = 32
CORE = 8
VMEM = pl.BlockSpec(memory_space=pltpu.VMEM)
SMEM = pl.BlockSpec(memory_space=pltpu.SMEM)
HBM = pl.BlockSpec(memory_space=pltpu.HBM)
LIMIT = 24 * 1024 * 1024


def call(kernel, outs, specs, out_specs, scratch=(), name=None, flops=0):
    return pl.pallas_call(
        kernel,
        out_shape=outs,
        in_specs=specs,
        out_specs=out_specs,
        scratch_shapes=list(scratch),
        compiler_params=pltpu.CompilerParams(vmem_limit_bytes=LIMIT),
        cost_estimate=pl.CostEstimate(flops=flops, bytes_accessed=1 << 20, transcendentals=0),
        name=name,
    )


def f32(*shape):
    return jax.ShapeDtypeStruct(shape, jnp.float32)


def rows_of(tile):
    return pl.ds(tile, 8, stride=TILES)


def pack_kernel(
    modes, start, back_arg, absorb_arg, density_arg, profiles, adjoint,
    out, own, background, absorb, density, raw, sems,
):
    half = SYSTEMS // 2
    place = slab_and_group()
    copies = []
    for system in range(SYSTEMS):
        source = profiles.at[modes[system]] if system < half else adjoint.at[system - half]
        copies.append(pltpu.make_async_copy(source, raw.at[system], sems.at[system]))
    held = [
        pltpu.make_async_copy(array, room, sems.at[SYSTEMS + at])
        for at, (array, room) in enumerate(
            ((back_arg, background), (absorb_arg, absorb), (density_arg, density))
        )
    ]
    for copy in held + copies:
        copy.start()
    for copy in held:
        copy.wait()
    for plane in range(2):
        where = place[0] * 2 + plane
        inside = (where >= start[0]) & (where < start[0] + SYSTEMS * SYSTEMS)
        for tile in range(TILES):
            rows = rows_of(tile)
            perm = jnp.where(
                inside, low_perm + perm_span * density[plane, rows], background[plane, rows]
            )
            diag_re = ((6.0 - wave_sq * perm) - CENTRE) * THIRD
            diag_im = absorb[plane, rows] * THIRD
            part = jnp.where(place[1] % 2 == 0, diag_re, diag_im)
            for system in range(SYSTEMS):
                out[system, 16 + plane * TILES + tile] = part
    share = pl.ds(pl.multiple_of(place[1] * 8, 8), 8)
    own[0] = density[0, share]
    own[1] = density[1, share]
    own[2] = jnp.full((8, 128), start[0]).astype(jnp.float32)
    after = (place[0] + 1) % SYSTEMS
    for slab in range(SYSTEMS):
        out[slab, ROWS_AT] = jnp.where(after == slab, density[1, share], density[0, share])
    for system in range(SYSTEMS):
        copies[system].wait()
        for part in range(2):
            for plane in range(2):
                for tile in range(TILES):
                    out[system, (part * 2 + plane) * TILES + tile] = raw[
                        system, part, plane, rows_of(tile)
                    ]


def slab_and_group():
    return lax.axis_index("zslab"), lax.axis_index("group")


class Stencil:
    def __init__(self):
        row = lax.broadcasted_iota(jnp.int32, (8, 128), 0)
        lane = lax.broadcasted_iota(jnp.int32, (8, 128), 1)
        self.first_row, self.last_row = row == 0, row == 7
        self.first_lane, self.last_lane = lane == 0, lane == 127

    def beside(self, below, here, above):
        up = jnp.where(self.first_row, 0.0, pltpu.roll(here[TILES - 1], 1, 0))
        down = jnp.where(self.last_row, 0.0, pltpu.roll(here[0], 7, 0))
        rows = [up] + list(here) + [down]
        sums = []
        for tile in range(TILES):
            left = jnp.where(self.first_lane, 0.0, pltpu.roll(here[tile], 1, 1))
            right = jnp.where(self.last_lane, 0.0, pltpu.roll(here[tile], 127, 1))
            z_sum = below[tile] + above[tile]
            sums.append((z_sum + (rows[tile] + rows[tile + 2])) + (left + right))
        return sums

    def run(self, basis, diag, level, first, last, third_of):
        def load(at):
            return [[basis[level, part, at, tile] for tile in range(TILES)] for part in range(2)]

        below, here = load(first - 1), load(first)
        for at in range(first, last):
            above = load(at + 1)
            third = third_of(at)
            near = [self.beside(below[part], here[part], above[part]) for part in range(2)]
            for tile in range(TILES):
                diag_re, diag_im = diag[0, at, tile], diag[1, at, tile]
                real, imag = here[0][tile], here[1][tile]
                new_re = diag_re * real - diag_im * imag - third * near[0][tile]
                new_im = diag_re * imag + diag_im * real - third * near[1][tile]
                if level > 0:
                    new_re = new_re - basis[level - 1, 0, at, tile]
                    new_im = new_im - basis[level - 1, 1, at, tile]
                basis[level + 1, 0, at, tile] = new_re
                basis[level + 1, 1, at, tile] = new_im
            below, here = here, above


def gram_pass(basis, acc, columns, ranges, shift):
    real_at, imag_at = pair_places()
    pairs = [(i, j) for j in columns for i in range(j + 1)]
    top = max(columns) + 1
    places = []
    for pair in pairs:
        places.append(real_at[pair])
        if pair[0] != pair[1]:
            places.append(imag_at[pair])

    def position(step, sums, first=0):
        window, tile = first + shift + step // TILES, step % TILES
        field = [(basis[k, 0, window, tile], basis[k, 1, window, tile]) for k in range(top)]
        new = []
        for i, j in pairs:
            (i_re, i_im), (j_re, j_im) = field[i], field[j]
            new.append(i_re * j_re + i_im * j_im)
            if i != j:
                new.append(i_re * j_im - i_im * j_re)
        return tuple(total + term for total, term in zip(sums, new))

    sums = tuple(acc[at] for at in places)
    for first, last in ranges:
        sums = lax.fori_loop(
            0, (last - first) * TILES, functools.partial(position, first=first), sums,
            unroll=8,
        )
    for at, value in zip(places, sums):
        acc[at] = value


def inner_kernel(block, other, basis, diag, acc):
    place = slab_and_group()
    core = place[1] % 2

    def load(chunk, _):
        for plane in range(2):
            for part in range(2):
                for tile in range(TILES):
                    at = part * 8 + plane * TILES + tile
                    basis[0, part, 2 * chunk + plane, tile] = block[chunk, at]
            for tile in range(TILES):
                at = plane * TILES + tile
                diag[core, 2 * chunk + plane, tile] = block[chunk, 16 + at]
                diag[1 - core, 2 * chunk + plane, tile] = other[chunk, at]
        return 0

    lax.fori_loop(0, SYSTEMS, load, 0, unroll=SYSTEMS)
    stencil = Stencil()
    for level in range(SYSTEMS - 1):
        stencil.run(basis, diag, level, level + 1, OWN - 1 - level, lambda at: THIRD)
    acc[...] = jnp.zeros_like(acc)
    for columns, ranges in INNER_PASSES:
        gram_pass(basis, acc, columns, ranges, 0)


INNER_PASSES = (
    ((0, 1, 2, 3, 4), ((4, 12),)),
    ((0, 1, 2), ((2, 4), (12, 14))),
    ((5, 6), ((6, 10),)),
)
OUTER_PASSES = (
    ((0, 1, 2, 3, 4), ((0, 2), (14, 16))),
    ((3, 4), ((2, 4), (12, 14))),
    ((5, 6), ((0, 6), (10, 16))),
    ((7,), ((0, 16),)),
    ((8,), ((0, 16),)),
)


def outer_kernel(
    block, low, high, other, inner, inner_diag, inner_acc, basis, gram, dens, diag, acc
):
    place = slab_and_group()
    core = place[1] % 2

    def load(source, first, at):
        def one(chunk, _):
            for plane in range(2):
                window = at + 2 * chunk + plane
                for part in range(2):
                    for tile in range(TILES):
                        spot = part * 8 + plane * TILES + tile
                        basis[0, part, window, tile] = source[chunk, spot]
                for tile in range(TILES):
                    spot = plane * TILES + tile
                    diag[core, window, tile] = source[chunk, 16 + spot]
                    diag[1 - core, window, tile] = other[first + chunk, spot]
            return 0

        lax.fori_loop(0, SYSTEMS // 2, one, 0, unroll=SYSTEMS // 2)

    load(low, 0, 0)
    load(high, SYSTEMS // 2, CORE + OWN)
    for level in range(SYSTEMS):

        def keep(at, _, level=level):
            for part in range(2):
                for tile in range(TILES):
                    basis[level, part, CORE + at, tile] = inner[level, part, at, tile]
                    if level == 0:
                        diag[part, CORE + at, tile] = inner_diag[part, at, tile]
            return 0

        lax.fori_loop(level, OWN - level, keep, 0, unroll=OWN - 2 * level)
    acc[...] = inner_acc[...]

    me = place[0] % SYSTEMS
    dens[0] = jnp.where(
        me > 0, block[jnp.maximum(me - 1, 0), ROWS_AT], low[SYSTEMS // 2 - 1, ROWS_AT]
    )
    dens[1] = jnp.where(
        me < SYSTEMS - 1, block[jnp.minimum(me + 1, SYSTEMS - 1), ROWS_AT], high[0, ROWS_AT]
    )

    third_low = jnp.where(place[0] >= SYSTEMS, THIRD, 0.0)
    third_high = jnp.where(place[0] < SYSTEMS * (SYSTEMS - 1), THIRD, 0.0)
    stencil = Stencil()
    for level in range(BASIS - 1):
        lower, upper = level + 1, WINDOW - 1 - level
        stencil.run(
            basis, diag, level, lower, lower + CORE,
            lambda at: third_low if at < CORE else THIRD,
        )
        stencil.run(
            basis, diag, level, upper - CORE, upper,
            lambda at: third_high if at >= CORE + OWN else THIRD,
        )
    for columns, ranges in OUTER_PASSES:
        gram_pass(basis, acc, columns, ranges, CORE)
    by_pair = jnp.sum(acc[...], axis=1)
    ones = jnp.ones((8, 128), jnp.float32)
    gram[...] = exact_dot(ones, by_pair, ((1,), (1,)))[0:1]


def combine_kernel(grams, pick, nudge, basis, out):
    row = grams[0]
    for other in range(1, SYSTEMS):
        row = row + grams[other]
    ones = jnp.ones((128, 128), jnp.float32)
    picked = exact_dot(pick[...] * row, ones, ((1,), (0,)))
    norms = jnp.sqrt(picked[2 * ROWS :])
    gram = []
    for column in range(2 * BASIS):
        rows = slice(16 * column, 16 * column + 16)
        scale = norms * norms[column % BASIS : column % BASIS + 1]
        gram.append(picked[rows] + nudge[rows] * scale)
    answer, apart, size = coefficients(gram[:BASIS], gram[BASIS:])
    agrees = jnp.max(jnp.where(apart <= AGREE * AGREE * size, 0.0, 1.0))
    flag = jnp.zeros((8, 128), jnp.float32) + agrees
    for slab in range(SYSTEMS):
        out[slab, 32] = flag
    weight = [
        (
            jnp.broadcast_to(answer[0][k : k + 1], (8, 128)),
            jnp.broadcast_to(answer[1][k : k + 1], (8, 128)),
        )
        for k in range(BASIS - 1)
    ]

    def solve_plane(plane, goals):
        for tile in range(TILES):
            real = jnp.zeros((8, 128), jnp.float32)
            imag = jnp.zeros((8, 128), jnp.float32)
            for k in range(BASIS - 1):
                b_re, b_im = basis[k, 0, plane, tile], basis[k, 1, plane, tile]
                real = real + (weight[k][0] * b_re - weight[k][1] * b_im)
                imag = imag + (weight[k][0] * b_im + weight[k][1] * b_re)
            for slab, at in goals:
                out[slab, at * TILES + tile] = real
                out[slab, (4 + at) * TILES + tile] = imag

    def middle(slab, _):
        for plane in range(2):
            solve_plane(CORE - 1 + 2 * slab + plane, ((slab, plane), (slab - 1, 2 + plane)))
        return 0

    for plane in range(2):
        solve_plane(CORE - 1 + plane, ((0, plane),))
        solve_plane(CORE + OWN - 1 + plane, ((SYSTEMS - 1, 2 + plane),))
    lax.fori_loop(1, SYSTEMS, middle, 0)


def fields_kernel(fields, forward, adjoint):
    half = SYSTEMS // 2
    for port in range(half):
        for part in range(2):
            for plane in range(2):
                for tile in range(TILES):
                    at = (part * 4 + 1 + plane) * TILES + tile
                    forward[port, part, plane, rows_of(tile)] = fields[port, at]
                    adjoint[port, part, plane, rows_of(tile)] = fields[half + port, at]


def terms_kernel(fields, mine, beside, across, natural):
    half = SYSTEMS // 2
    for plane in range(4):
        for tile in range(TILES):
            real, imag = plane * TILES + tile, (4 + plane) * TILES + tile
            total = None
            for port in range(half):
                term = fields[port, real] * fields[half + port, real]
                term = term - fields[port, imag] * fields[half + port, imag]
                total = term if total is None else total + term
            natural[plane, rows_of(tile)] = total
    flag = fields[0, 32]
    for system in range(1, SYSTEMS):
        flag = flag + fields[system, 32]
    group = slab_and_group()[1]
    core, chip = group % 2, group // 2
    for out, pair, side in (
        (mine, chip, core),
        (beside, chip, 1 - core),
        (across.at[0], 1 - chip, core),
        (across.at[1], 1 - chip, 1 - core),
    ):
        rows = pl.ds(pl.multiple_of((2 * pair + side) * 8, 8), 8)
        for plane in range(4):
            out[plane] = natural[plane, rows]
        out[4] = flag


def density_kernel(mine, across, beside, own, dens, out, flag):
    lane = lax.broadcasted_iota(jnp.int32, (8, 128), 1)
    updated = []
    for plane in range(4):
        gradient = -wave_sq * (mine[plane] + across[0, plane] + beside[plane])
        where = slab_and_group()[0] * 2 + plane - 1
        depth = where.astype(jnp.float32) - own[2]
        inside = (depth >= 0.0) & (depth < SYSTEMS * SYSTEMS)
        rows = (dens[0], own[0], own[1], dens[1])[plane]
        moved = jnp.clip(rows - step_size * perm_span * gradient, 0.0, 1.0)
        rows = jnp.where(inside, moved, rows)
        exists = (where >= 0) & (where < 2 * SYSTEMS * SYSTEMS)
        updated.append(jnp.where(exists, rows, 0.0))
    for plane in range(2):
        own = updated[plane + 1]
        right = jnp.where(lane == 127, 0.0, pltpu.roll(own, 127, 1))
        left = jnp.where(lane == 0, 0.0, pltpu.roll(own, 1, 1))
        filtered = (2.0 * own + updated[plane + 2] + updated[plane] + right + left) / 6.0
        edge = float(np.tanh(sharpness * threshold))
        other_edge = float(np.tanh(sharpness * (1.0 - threshold)))
        out[plane] = (edge + jnp.tanh(sharpness * (filtered - threshold))) / (edge + other_edge)
    flag[0] = jnp.max(mine[4] + across[0, 4] + beside[4])


def copy_kernel(count, *refs):
    sems = refs[-1]
    arrays = refs[-1 - 2 * count : -1]
    copies = [
        pltpu.make_async_copy(arrays[at], arrays[count + at], sems.at[at]) for at in range(count)
    ]
    for copy in copies:
        copy.start()
    for copy in copies:
        copy.wait()


def row_major(mark, arrays, name):
    count = len(arrays)
    return call(
        functools.partial(copy_kernel, count),
        tuple(jax.ShapeDtypeStruct(array.shape, array.dtype) for array in arrays),
        [SMEM] + [HBM] * count,
        (HBM,) * count,
        [pltpu.SemaphoreType.DMA((count,))],
        name,
    )(mark.reshape(1), *arrays)


def on_device(background, absorb, density, profiles, adjoint_source, port_modes, design_start):
    planes_of = [[z * SYSTEMS + l for l in range(SYSTEMS)] for z in range(SYSTEMS)]
    columns = [[z * SYSTEMS + l for z in range(SYSTEMS)] for l in range(SYSTEMS)]
    packed, own_rows = call(
        pack_kernel,
        (f32(SYSTEMS, BLOCK, 8, 128), f32(3, 8, 128)),
        [SMEM, SMEM] + [HBM] * 5,
        (VMEM, VMEM),
        [pltpu.VMEM(density.shape, jnp.float32)] * 3
        + [
            pltpu.VMEM((SYSTEMS,) + profiles.shape[1:], jnp.float32),
            pltpu.SemaphoreType.DMA((SYSTEMS + 3,)),
        ],
        "pack",
    )(port_modes, design_start, background, absorb, density, profiles, adjoint_source)
    block = lax.all_to_all(packed, "zslab", 0, 0, axis_index_groups=planes_of, tiled=True)
    count = SYSTEMS * SYSTEMS
    up = [(i, i + SYSTEMS) for i in range(count - SYSTEMS)]
    down = [(target, source) for source, target in up]
    low = lax.ppermute(block[SYSTEMS // 2 :], "zslab", up)
    high = lax.ppermute(block[: SYSTEMS // 2], "zslab", down)
    swap = [(i, i ^ 1) for i in range(4)]
    other = lax.ppermute(block[:, 16:ROWS_AT], "group", swap)
    inner = call(
        inner_kernel,
        (f32(SYSTEMS, 2, OWN, TILES, 8, 128), f32(2, OWN, TILES, 8, 128), f32(128, 8, 128)),
        [VMEM, VMEM],
        (VMEM,) * 3,
        (),
        "inner",
        10**8,
    )(block, other)
    low, high, inner = lax.optimization_barrier((low, high, inner))
    ends = jnp.concatenate([low[:, 16:ROWS_AT], high[:, 16:ROWS_AT]], axis=0)
    ends = lax.ppermute(ends, "group", swap)
    plane = (TILES, 8, 128)
    basis, gram, dens = call(
        outer_kernel,
        (f32(BASIS, 2, WINDOW, *plane), f32(1, 128), f32(2, 8, 128)),
        [VMEM] * 7,
        (VMEM, VMEM, VMEM),
        [pltpu.VMEM((2, WINDOW) + plane, jnp.float32), pltpu.VMEM((128, 8, 128), jnp.float32)],
        "outer",
        2 * 10**8,
    )(block, low, high, ends, *inner)
    grams = lax.all_to_all(
        jnp.broadcast_to(gram[None], (SYSTEMS, 1, 128)), "zslab", 0, 0,
        axis_index_groups=columns, tiled=True,
    )
    pick, nudge = gram_tables()
    solved = call(
        combine_kernel, f32(SYSTEMS, 33, 8, 128), [VMEM, VMEM, VMEM, VMEM], VMEM, (), "combine"
    )(grams, jnp.asarray(pick), jnp.asarray(nudge), basis)
    fields = lax.all_to_all(solved, "zslab", 0, 0, axis_index_groups=planes_of, tiled=True)
    half = f32(SYSTEMS // 2, 2, 2, 8 * TILES, 128)
    forward, adjoint = call(fields_kernel, (half, half), [VMEM], (VMEM,) * 2, (), "fields", 10**7)(fields)
    mine, beside, across = call(
        terms_kernel,
        (f32(5, 8, 128), f32(5, 8, 128), f32(2, 5, 8, 128)),
        [VMEM],
        (VMEM,) * 3,
        [pltpu.VMEM((4, 8 * TILES, 128), jnp.float32)],
        "terms",
    )(fields)
    across = lax.ppermute(across, "group", [(i, i ^ 2) for i in range(4)])
    across, forward, adjoint = lax.optimization_barrier((across, forward, adjoint))
    beside = lax.ppermute(beside + across[1], "group", swap)
    new_density, flag = call(
        density_kernel,
        (f32(2, 8, 128), f32(1)),
        [VMEM] * 5,
        (VMEM, SMEM),
        (),
        "density",
    )(mine, across, beside, own_rows, dens)

    def again(state):
        held = (background, absorb, density, profiles, adjoint_source)
        held = row_major(state[0], held, "arguments")
        results = iterate_on_device(*held, port_modes, design_start)
        return (jnp.zeros((), jnp.float32),) + tuple(row_major(state[0], results, "results"))

    state = (flag[0], forward, adjoint, new_density)
    return lax.while_loop(lambda state: state[0] > 0.0, again, state)[1:]


def solution(mesh):
    return jax.shard_map(
        on_device,
        mesh=mesh,
        in_specs=(
            P("zslab", None, None),
            P("zslab", None, None),
            P("zslab", None, None),
            P(None, None, "zslab", None, None),
            P("group", None, "zslab", None, None),
            P("group"),
            P(),
        ),
        out_specs=(
            P("group", None, "zslab", None, None),
            P("group", None, "zslab", None, None),
            P("zslab", "group", None),
        ),
        check_vma=False,
    )
```

```python
import functools

import jax
import jax.numpy as jnp
import numpy as np
from jax import lax
from jax.experimental import pallas as pl
from jax.experimental.pallas import tpu as pltpu
from jax.sharding import PartitionSpec as P

ITERS = 4


wave_sq = 0.1
step_size = 2.0
perm_span = 10.0
low_perm = 2.1
sharpness = 8.0
threshold = 0.5


def with_halo(block, sides, width):
    for axis, dim in sides:
        count = lax.axis_size(axis)
        forward = [(i, i + 1) for i in range(count - 1)]
        backward = [(target, source) for source, target in forward]
        low = lax.ppermute(
            lax.slice_in_dim(block, block.shape[dim] - width, None, axis=dim), axis, forward
        )
        high = lax.ppermute(lax.slice_in_dim(block, 0, width, axis=dim), axis, backward)
        block = jnp.concatenate([low, block, high], axis=dim)
    return block


def scaled(coef, field):
    coef_re = coef[0].reshape((-1, 1, 1, 1))
    coef_im = coef[1].reshape((-1, 1, 1, 1))
    real_part = coef_re * field[:, 0] - coef_im * field[:, 1]
    imag_part = coef_re * field[:, 1] + coef_im * field[:, 0]
    return jnp.stack([real_part, imag_part], axis=1)


def product_pair(left, right):
    real_part = jnp.sum(left[:, 0] * right[:, 0] + left[:, 1] * right[:, 1], axis=(1, 2, 3))
    imag_part = jnp.sum(left[:, 0] * right[:, 1] - left[:, 1] * right[:, 0], axis=(1, 2, 3))
    return (real_part, imag_part)


def divide_pair(top, bottom):
    denominator = bottom[0] * bottom[0] + bottom[1] * bottom[1]
    return (
        (top[0] * bottom[0] + top[1] * bottom[1]) / denominator,
        (top[1] * bottom[0] - top[0] * bottom[1]) / denominator,
    )


def multiply_pair(left, right):
    return (left[0] * right[0] - left[1] * right[1], left[0] * right[1] + left[1] * right[0])


def with_planes(field):
    return with_halo(field, (("zslab", 2),), 1)


def operate(field, diag_re, diag_im):
    padded = jnp.pad(with_planes(field), ((0, 0), (0, 0), (0, 0), (1, 1), (1, 1)))
    beside = padded[:, :, 2:, 1:-1, 1:-1] + padded[:, :, :-2, 1:-1, 1:-1]
    beside = beside + padded[:, :, 1:-1, 2:, 1:-1] + padded[:, :, 1:-1, :-2, 1:-1]
    beside = beside + padded[:, :, 1:-1, 1:-1, 2:] + padded[:, :, 1:-1, 1:-1, :-2]
    real_part = diag_re * field[:, 0] - diag_im * field[:, 1]
    imag_part = diag_re * field[:, 1] + diag_im * field[:, 0]
    return jnp.stack([real_part, imag_part], axis=1) - beside


def bicgstab(sources, diag_re, diag_im):
    solution = jnp.zeros_like(sources)
    residual = sources
    direction = sources
    bilinear = lax.psum(product_pair(sources, residual), "zslab")
    for iteration in range(ITERS):
        image = operate(direction, diag_re, diag_im)
        along = lax.psum(product_pair(sources, image), "zslab")
        advance = divide_pair(bilinear, along)
        halfway = residual - scaled(advance, image)
        second = operate(halfway, diag_re, diag_im)
        cross_re, cross_im = product_pair(second, halfway)
        energy = jnp.sum(second[:, 0] * second[:, 0] + second[:, 1] * second[:, 1], axis=(1, 2, 3))
        cross_re, cross_im, energy = lax.psum((cross_re, cross_im, energy), "zslab")
        relax_coef = (cross_re / energy, cross_im / energy)
        solution = solution + scaled(advance, direction) + scaled(relax_coef, halfway)
        residual = halfway - scaled(relax_coef, second)
        if iteration + 1 < ITERS:
            bilinear_new = lax.psum(product_pair(sources, residual), "zslab")
        if iteration + 1 < ITERS:
            blend_coef = multiply_pair(
                divide_pair(bilinear_new, bilinear), divide_pair(advance, relax_coef)
            )
            direction = residual + scaled(blend_coef, direction - scaled(relax_coef, image))
            bilinear = bilinear_new
    return solution


def iterate_on_device(background, absorb, density, profiles, adjoint_source, port_modes, design_start):
    planes_dev = density.shape[0]
    rows_all = density.shape[1]
    first_plane = lax.axis_index("zslab") * planes_dev
    design_depth = planes_dev * lax.axis_size("zslab") // 2
    planes = first_plane + jnp.arange(planes_dev)
    in_design = (planes >= design_start[0]) & (planes < design_start[0] + design_depth)
    in_design = in_design[:, None, None]
    permittivity = jnp.where(in_design, low_perm + perm_span * density, background)
    diag_re = 6.0 - wave_sq * permittivity
    selector = (port_modes[:, None] == jnp.arange(profiles.shape[0])[None, :]).astype(jnp.float32)
    forward_source = jnp.einsum(
        "pm,mczyx->pczyx", selector, profiles, precision=lax.Precision.HIGHEST
    )
    port_count = forward_source.shape[0]
    sources = jnp.concatenate([forward_source, adjoint_source], axis=0)
    fields = bicgstab(sources, diag_re, absorb)
    forward_field = fields[:port_count]
    adjoint_field = fields[port_count:]
    terms = forward_field[:, 0] * adjoint_field[:, 0] - forward_field[:, 1] * adjoint_field[:, 1]
    local_term = -wave_sq * jnp.sum(terms, axis=0)
    rows_share = rows_all // lax.axis_size("group")
    row_start = lax.axis_index("group") * rows_share
    total = lax.psum(local_term, "group")
    gradient = lax.dynamic_slice_in_dim(total, row_start, rows_share, 1)
    density_rows = lax.dynamic_slice_in_dim(density, row_start, rows_share, 1)
    updated = jnp.where(
        in_design, jnp.clip(density_rows - step_size * perm_span * gradient, 0.0, 1.0), density_rows
    )
    extended = with_halo(updated, (("zslab", 0),), 1)
    padded = jnp.pad(extended, ((0, 0), (0, 0), (1, 1)))
    filtered = (
        2.0 * updated
        + padded[2:, :, 1:-1]
        + padded[:-2, :, 1:-1]
        + padded[1:-1, :, 2:]
        + padded[1:-1, :, :-2]
    ) / 6.0
    new_density = (
        jnp.tanh(sharpness * threshold) + jnp.tanh(sharpness * (filtered - threshold))
    ) / (jnp.tanh(sharpness * threshold) + jnp.tanh(sharpness * (1.0 - threshold)))
    return (forward_field, adjoint_field, new_density)


BASIS = 2 * ITERS + 1
CENTRE = 5.3
HALF_RADIUS = 3.0
THIRD = 1.0 / HALF_RADIUS
NUDGE = 1e-6
AGREE = 5e-4
ROWS = 16 * BASIS


def pair_places():
    real, imag, place = {}, {}, 0
    for j in range(BASIS):
        for i in range(j + 1):
            real[(i, j)] = place
            place += 1
    for j in range(BASIS):
        for i in range(j):
            imag[(i, j)] = place
            place += 1
    return real, imag


def gram_tables():
    real, imag = pair_places()
    pick = np.zeros((2 * ROWS + 16, 128), np.float32)
    nudge = np.zeros((2 * ROWS, 128), np.float32)
    rng = np.random.default_rng(7)
    sign_re = {pair: np.where(rng.random(128) < 0.5, -1.0, 1.0) for pair in real}
    sign_im = {pair: np.where(rng.random(128) < 0.5, -1.0, 1.0) for pair in imag}
    for j in range(BASIS):
        for i in range(BASIS):
            row, pair = j * 16 + i, (min(i, j), max(i, j))
            pick[row, real[pair]] = 1.0
            nudge[row] = NUDGE * sign_re[pair]
            if i != j:
                side = 1.0 if i < j else -1.0
                pick[ROWS + row, imag[pair]] = side
                nudge[ROWS + row] = NUDGE * side * sign_im[pair]
        pick[2 * ROWS + j, real[(j, j)]] = 1.0
    nudge[:, 0] = 0.0
    return pick, nudge


def exact_dot(left, right, dims):
    return lax.dot_general(
        left, right, (dims, ((), ())), precision=lax.Precision.HIGHEST,
        preferred_element_type=jnp.float32,
    )


def minus_pair(left, right):
    return (left[0] - right[0], left[1] - right[1])


def plus_pair(left, right):
    return (left[0] + right[0], left[1] + right[1])


def coefficients(gram_re, gram_im):
    row = lax.broadcasted_iota(jnp.int32, (16, 128), 0)
    keep = jnp.where(row == 15, 0.0, HALF_RADIUS)

    def apply(q):
        return tuple(
            CENTRE * v + HALF_RADIUS * pltpu.roll(v, 1, 0) + keep * pltpu.roll(v, 15, 0) for v in q
        )

    def total(v):
        return jnp.sum(v, axis=0, keepdims=True)

    def with_source(q):
        return (
            total(gram_re[0] * q[0] + gram_im[0] * q[1]),
            total(gram_re[0] * q[1] - gram_im[0] * q[0]),
        )

    def times_gram(q):
        out_re = jnp.zeros((16, 128), jnp.float32)
        out_im = jnp.zeros((16, 128), jnp.float32)
        for j in range(BASIS):
            q_re, q_im = q[0][j : j + 1], q[1][j : j + 1]
            out_re = out_re + (gram_re[j] * q_re - gram_im[j] * q_im)
            out_im = out_im + (gram_re[j] * q_im + gram_im[j] * q_re)
        return out_re, out_im

    one = jnp.where(row == 0, 1.0, 0.0)
    zero = jnp.zeros((16, 128), jnp.float32)
    answer, residual, direction = (zero, zero), (one, zero), (one, zero)
    bilinear = with_source(residual)
    for iteration in range(ITERS):
        image = apply(direction)
        advance = divide_pair(bilinear, with_source(image))
        halfway = minus_pair(residual, multiply_pair(advance, image))
        second = apply(halfway)
        weighed = times_gram(second)
        energy = total(second[0] * weighed[0] + second[1] * weighed[1])
        relax = (
            total(weighed[0] * halfway[0] + weighed[1] * halfway[1]) / energy,
            total(weighed[0] * halfway[1] - weighed[1] * halfway[0]) / energy,
        )
        answer = plus_pair(
            answer, plus_pair(multiply_pair(advance, direction), multiply_pair(relax, halfway))
        )
        if iteration + 1 < ITERS:
            residual = minus_pair(halfway, multiply_pair(relax, second))
            bilinear_new = with_source(residual)
            blend = multiply_pair(divide_pair(bilinear_new, bilinear), divide_pair(advance, relax))
            direction = plus_pair(
                residual, multiply_pair(blend, minus_pair(direction, multiply_pair(relax, image)))
            )
            bilinear = bilinear_new
    first = tuple(jnp.broadcast_to(v[:, :1], v.shape) for v in answer)
    apart = minus_pair(answer, first)

    def norm(q):
        weighed = times_gram(q)
        return total(q[0] * weighed[0] + q[1] * weighed[1])

    return first, norm(apart), norm(first)


TILES = 4
SYSTEMS = 8
BLOCK = 12 * TILES // 2 + 1
ROWS_AT = BLOCK - 1
OWN = 16
WINDOW = 32
CORE = 8
VMEM = pl.BlockSpec(memory_space=pltpu.VMEM)
SMEM = pl.BlockSpec(memory_space=pltpu.SMEM)
HBM = pl.BlockSpec(memory_space=pltpu.HBM)
LIMIT = 24 * 1024 * 1024


def call(kernel, outs, specs, out_specs, scratch=(), name=None, flops=0):
    return pl.pallas_call(
        kernel,
        out_shape=outs,
        in_specs=specs,
        out_specs=out_specs,
        scratch_shapes=list(scratch),
        compiler_params=pltpu.CompilerParams(vmem_limit_bytes=LIMIT),
        cost_estimate=pl.CostEstimate(flops=flops, bytes_accessed=1 << 20, transcendentals=0),
        name=name,
    )


def f32(*shape):
    return jax.ShapeDtypeStruct(shape, jnp.float32)


def rows_of(tile):
    return pl.ds(tile, 8, stride=TILES)


def pack_kernel(*refs):
    arguments, out, own, held, sems = refs[:7], refs[7], refs[8], refs[9:16], refs[16]
    modes, start, background, absorb, density, profiles, adjoint = held
    half = SYSTEMS // 2
    place = slab_and_group()
    copies = [
        pltpu.make_async_copy(array, room, sems.at[at])
        for at, (array, room) in enumerate(zip(arguments, held))
    ]
    for copy in copies:
        copy.start()
    for copy in copies[:5]:
        copy.wait()
    for plane in range(2):
        where = place[0] * 2 + plane
        inside = (where >= start[0]) & (where < start[0] + SYSTEMS * SYSTEMS)
        for tile in range(TILES):
            rows = rows_of(tile)
            perm = jnp.where(
                inside, low_perm + perm_span * density[plane, rows], background[plane, rows]
            )
            diag_re = ((6.0 - wave_sq * perm) - CENTRE) * THIRD
            diag_im = absorb[plane, rows] * THIRD
            part = jnp.where(place[1] % 2 == 0, diag_re, diag_im)
            for system in range(SYSTEMS):
                out[system, 16 + plane * TILES + tile] = part
    share = pl.ds(pl.multiple_of(place[1] * 8, 8), 8)
    own[0] = density[0, share]
    own[1] = density[1, share]
    own[2] = jnp.full((8, 128), start[0]).astype(jnp.float32)
    after = (place[0] + 1) % SYSTEMS
    for slab in range(SYSTEMS):
        out[slab, ROWS_AT] = jnp.where(after == slab, density[1, share], density[0, share])
    for copy in copies[5:]:
        copy.wait()
    for system in range(half):
        mode = modes[system]
        for part in range(2):
            for plane in range(2):
                for tile in range(TILES):
                    at = (part * 2 + plane) * TILES + tile
                    out[system, at] = profiles[mode, part, plane, rows_of(tile)]
                    out[half + system, at] = adjoint[system, part, plane, rows_of(tile)]


def slab_and_group():
    return lax.axis_index("zslab"), lax.axis_index("group")


class Stencil:
    def __init__(self):
        row = lax.broadcasted_iota(jnp.int32, (8, 128), 0)
        lane = lax.broadcasted_iota(jnp.int32, (8, 128), 1)
        self.first_row, self.last_row = row == 0, row == 7
        self.first_lane, self.last_lane = lane == 0, lane == 127

    def beside(self, below, here, above):
        up = jnp.where(self.first_row, 0.0, pltpu.roll(here[TILES - 1], 1, 0))
        down = jnp.where(self.last_row, 0.0, pltpu.roll(here[0], 7, 0))
        rows = [up] + list(here) + [down]
        sums = []
        for tile in range(TILES):
            left = jnp.where(self.first_lane, 0.0, pltpu.roll(here[tile], 1, 1))
            right = jnp.where(self.last_lane, 0.0, pltpu.roll(here[tile], 127, 1))
            z_sum = below[tile] + above[tile]
            sums.append((z_sum + (rows[tile] + rows[tile + 2])) + (left + right))
        return sums

    def run(self, basis, diag, level, first, last, third_of):
        def load(at):
            return [[basis[level, part, at, tile] for tile in range(TILES)] for part in range(2)]

        below, here = load(first - 1), load(first)
        for at in range(first, last):
            above = load(at + 1)
            third = third_of(at)
            near = [self.beside(below[part], here[part], above[part]) for part in range(2)]
            for tile in range(TILES):
                diag_re, diag_im = diag[0, at, tile], diag[1, at, tile]
                real, imag = here[0][tile], here[1][tile]
                new_re = diag_re * real - diag_im * imag - third * near[0][tile]
                new_im = diag_re * imag + diag_im * real - third * near[1][tile]
                if level > 0:
                    new_re = new_re - basis[level - 1, 0, at, tile]
                    new_im = new_im - basis[level - 1, 1, at, tile]
                basis[level + 1, 0, at, tile] = new_re
                basis[level + 1, 1, at, tile] = new_im
            below, here = here, above


def gram_pass(basis, acc, columns, ranges, shift):
    real_at, imag_at = pair_places()
    pairs = [(i, j) for j in columns for i in range(j + 1)]
    top = max(columns) + 1
    places = []
    for pair in pairs:
        places.append(real_at[pair])
        if pair[0] != pair[1]:
            places.append(imag_at[pair])

    def position(step, sums, first=0):
        window, tile = first + shift + step // TILES, step % TILES
        field = [(basis[k, 0, window, tile], basis[k, 1, window, tile]) for k in range(top)]
        new = []
        for i, j in pairs:
            (i_re, i_im), (j_re, j_im) = field[i], field[j]
            new.append(i_re * j_re + i_im * j_im)
            if i != j:
                new.append(i_re * j_im - i_im * j_re)
        return tuple(total + term for total, term in zip(sums, new))

    sums = tuple(acc[at] for at in places)
    for first, last in ranges:
        sums = lax.fori_loop(
            0, (last - first) * TILES, functools.partial(position, first=first), sums,
            unroll=8,
        )
    for at, value in zip(places, sums):
        acc[at] = value


def inner_kernel(block, other, basis, diag, acc):
    place = slab_and_group()
    core = place[1] % 2

    def load(chunk, _):
        for plane in range(2):
            for part in range(2):
                for tile in range(TILES):
                    at = part * 8 + plane * TILES + tile
                    basis[0, part, 2 * chunk + plane, tile] = block[chunk, at]
            for tile in range(TILES):
                at = plane * TILES + tile
                diag[core, 2 * chunk + plane, tile] = block[chunk, 16 + at]
                diag[1 - core, 2 * chunk + plane, tile] = other[chunk, at]
        return 0

    lax.fori_loop(0, SYSTEMS, load, 0, unroll=SYSTEMS)
    stencil = Stencil()
    for level in range(SYSTEMS - 1):
        stencil.run(basis, diag, level, level + 1, OWN - 1 - level, lambda at: THIRD)
    acc[...] = jnp.zeros_like(acc)
    for columns, ranges in INNER_PASSES:
        gram_pass(basis, acc, columns, ranges, 0)


INNER_PASSES = (
    ((0, 1, 2, 3, 4), ((4, 12),)),
    ((0, 1, 2), ((2, 4), (12, 14))),
    ((5, 6), ((6, 10),)),
)
OUTER_PASSES = (
    ((0, 1, 2, 3, 4), ((0, 2), (14, 16))),
    ((3, 4), ((2, 4), (12, 14))),
    ((5, 6), ((0, 6), (10, 16))),
    ((7,), ((0, 16),)),
    ((8,), ((0, 16),)),
)


def outer_kernel(
    block, low, high, other, inner, inner_diag, inner_acc, basis, gram, dens, diag, acc
):
    place = slab_and_group()
    core = place[1] % 2

    def load(source, first, at):
        def one(chunk, _):
            for plane in range(2):
                window = at + 2 * chunk + plane
                for part in range(2):
                    for tile in range(TILES):
                        spot = part * 8 + plane * TILES + tile
                        basis[0, part, window, tile] = source[chunk, spot]
                for tile in range(TILES):
                    spot = plane * TILES + tile
                    diag[core, window, tile] = source[chunk, 16 + spot]
                    diag[1 - core, window, tile] = other[first + chunk, spot]
            return 0

        lax.fori_loop(0, SYSTEMS // 2, one, 0, unroll=SYSTEMS // 2)

    load(low, 0, 0)
    load(high, SYSTEMS // 2, CORE + OWN)
    for level in range(SYSTEMS):

        def keep(at, _, level=level):
            for part in range(2):
                for tile in range(TILES):
                    basis[level, part, CORE + at, tile] = inner[level, part, at, tile]
                    if level == 0:
                        diag[part, CORE + at, tile] = inner_diag[part, at, tile]
            return 0

        lax.fori_loop(level, OWN - level, keep, 0, unroll=OWN - 2 * level)
    acc[...] = inner_acc[...]

    me = place[0] % SYSTEMS
    dens[0] = jnp.where(
        me > 0, block[jnp.maximum(me - 1, 0), ROWS_AT], low[SYSTEMS // 2 - 1, ROWS_AT]
    )
    dens[1] = jnp.where(
        me < SYSTEMS - 1, block[jnp.minimum(me + 1, SYSTEMS - 1), ROWS_AT], high[0, ROWS_AT]
    )

    third_low = jnp.where(place[0] >= SYSTEMS, THIRD, 0.0)
    third_high = jnp.where(place[0] < SYSTEMS * (SYSTEMS - 1), THIRD, 0.0)
    stencil = Stencil()
    for level in range(BASIS - 1):
        lower, upper = level + 1, WINDOW - 1 - level
        stencil.run(
            basis, diag, level, lower, lower + CORE,
            lambda at: third_low if at < CORE else THIRD,
        )
        stencil.run(
            basis, diag, level, upper - CORE, upper,
            lambda at: third_high if at >= CORE + OWN else THIRD,
        )
    for columns, ranges in OUTER_PASSES:
        gram_pass(basis, acc, columns, ranges, CORE)
    by_pair = jnp.sum(acc[...], axis=1)
    ones = jnp.ones((8, 128), jnp.float32)
    gram[...] = exact_dot(ones, by_pair, ((1,), (1,)))[0:1]


def combine_kernel(grams, pick, nudge, basis, out):
    row = grams[0]
    for other in range(1, SYSTEMS):
        row = row + grams[other]
    ones = jnp.ones((128, 128), jnp.float32)
    picked = exact_dot(pick[...] * row, ones, ((1,), (0,)))
    norms = jnp.sqrt(picked[2 * ROWS :])
    gram = []
    for column in range(2 * BASIS):
        rows = slice(16 * column, 16 * column + 16)
        scale = norms * norms[column % BASIS : column % BASIS + 1]
        gram.append(picked[rows] + nudge[rows] * scale)
    answer, apart, size = coefficients(gram[:BASIS], gram[BASIS:])
    agrees = jnp.max(jnp.where(apart <= AGREE * AGREE * size, 0.0, 1.0))
    flag = jnp.zeros((8, 128), jnp.float32) + agrees
    for slab in range(SYSTEMS):
        out[slab, 32] = flag
    weight = [
        (
            jnp.broadcast_to(answer[0][k : k + 1], (8, 128)),
            jnp.broadcast_to(answer[1][k : k + 1], (8, 128)),
        )
        for k in range(BASIS - 1)
    ]

    def solve_plane(plane, goals):
        for tile in range(TILES):
            real = jnp.zeros((8, 128), jnp.float32)
            imag = jnp.zeros((8, 128), jnp.float32)
            for k in range(BASIS - 1):
                b_re, b_im = basis[k, 0, plane, tile], basis[k, 1, plane, tile]
                real = real + (weight[k][0] * b_re - weight[k][1] * b_im)
                imag = imag + (weight[k][0] * b_im + weight[k][1] * b_re)
            for slab, at in goals:
                out[slab, at * TILES + tile] = real
                out[slab, (4 + at) * TILES + tile] = imag

    def middle(slab, _):
        for plane in range(2):
            solve_plane(CORE - 1 + 2 * slab + plane, ((slab, plane), (slab - 1, 2 + plane)))
        return 0

    for plane in range(2):
        solve_plane(CORE - 1 + plane, ((0, plane),))
        solve_plane(CORE + OWN - 1 + plane, ((SYSTEMS - 1, 2 + plane),))
    lax.fori_loop(1, SYSTEMS, middle, 0, unroll=SYSTEMS - 1)


def fields_kernel(fields, forward, adjoint):
    half = SYSTEMS // 2
    for port in range(half):
        for part in range(2):
            for plane in range(2):
                for tile in range(TILES):
                    at = (part * 4 + 1 + plane) * TILES + tile
                    forward[port, part, plane, rows_of(tile)] = fields[port, at]
                    adjoint[port, part, plane, rows_of(tile)] = fields[half + port, at]


def terms_kernel(fields, mine, beside, across, natural):
    half = SYSTEMS // 2
    for plane in range(4):
        for tile in range(TILES):
            real, imag = plane * TILES + tile, (4 + plane) * TILES + tile
            total = None
            for port in range(half):
                term = fields[port, real] * fields[half + port, real]
                term = term - fields[port, imag] * fields[half + port, imag]
                total = term if total is None else total + term
            natural[plane, rows_of(tile)] = total
    flag = fields[0, 32]
    for system in range(1, SYSTEMS):
        flag = flag + fields[system, 32]
    group = slab_and_group()[1]
    core, chip = group % 2, group // 2
    for out, pair, side in (
        (mine, chip, core),
        (beside, chip, 1 - core),
        (across.at[0], 1 - chip, core),
        (across.at[1], 1 - chip, 1 - core),
    ):
        rows = pl.ds(pl.multiple_of((2 * pair + side) * 8, 8), 8)
        for plane in range(4):
            out[plane] = natural[plane, rows]
        out[4] = flag


def density_kernel(mine, across, beside, own, dens, out, flag):
    lane = lax.broadcasted_iota(jnp.int32, (8, 128), 1)
    updated = []
    for plane in range(4):
        gradient = -wave_sq * (mine[plane] + across[0, plane] + beside[plane])
        where = slab_and_group()[0] * 2 + plane - 1
        depth = where.astype(jnp.float32) - own[2]
        inside = (depth >= 0.0) & (depth < SYSTEMS * SYSTEMS)
        rows = (dens[0], own[0], own[1], dens[1])[plane]
        moved = jnp.clip(rows - step_size * perm_span * gradient, 0.0, 1.0)
        rows = jnp.where(inside, moved, rows)
        exists = (where >= 0) & (where < 2 * SYSTEMS * SYSTEMS)
        updated.append(jnp.where(exists, rows, 0.0))
    for plane in range(2):
        own = updated[plane + 1]
        right = jnp.where(lane == 127, 0.0, pltpu.roll(own, 127, 1))
        left = jnp.where(lane == 0, 0.0, pltpu.roll(own, 1, 1))
        filtered = (2.0 * own + updated[plane + 2] + updated[plane] + right + left) / 6.0
        edge = float(np.tanh(sharpness * threshold))
        other_edge = float(np.tanh(sharpness * (1.0 - threshold)))
        out[plane] = (edge + jnp.tanh(sharpness * (filtered - threshold))) / (edge + other_edge)
    flag[0] = jnp.max(mine[4] + across[0, 4] + beside[4])


def copy_kernel(count, *refs):
    sems = refs[-1]
    arrays = refs[-1 - 2 * count : -1]
    copies = [
        pltpu.make_async_copy(arrays[at], arrays[count + at], sems.at[at]) for at in range(count)
    ]
    for copy in copies:
        copy.start()
    for copy in copies:
        copy.wait()


def row_major(mark, arrays, name):
    count = len(arrays)
    return call(
        functools.partial(copy_kernel, count),
        tuple(jax.ShapeDtypeStruct(array.shape, array.dtype) for array in arrays),
        [SMEM] + [HBM] * count,
        (HBM,) * count,
        [pltpu.SemaphoreType.DMA((count,))],
        name,
    )(mark.reshape(1), *arrays)


def on_device(background, absorb, density, profiles, adjoint_source, port_modes, design_start):
    planes_of = [[z * SYSTEMS + l for l in range(SYSTEMS)] for z in range(SYSTEMS)]
    columns = [[z * SYSTEMS + l for z in range(SYSTEMS)] for l in range(SYSTEMS)]
    packed, own_rows = call(
        pack_kernel,
        (f32(SYSTEMS, BLOCK, 8, 128), f32(3, 8, 128)),
        [HBM] * 7,
        (VMEM, VMEM),
        [pltpu.SMEM(array.shape, array.dtype) for array in (port_modes, design_start)]
        + [
            pltpu.VMEM(array.shape, array.dtype)
            for array in (background, absorb, density, profiles, adjoint_source)
        ]
        + [pltpu.SemaphoreType.DMA((7,))],
        "pack",
    )(port_modes, design_start, background, absorb, density, profiles, adjoint_source)
    block = lax.all_to_all(packed, "zslab", 0, 0, axis_index_groups=planes_of, tiled=True)
    count = SYSTEMS * SYSTEMS
    up = [(i, i + SYSTEMS) for i in range(count - SYSTEMS)]
    down = [(target, source) for source, target in up]
    low = lax.ppermute(block[SYSTEMS // 2 :], "zslab", up)
    high = lax.ppermute(block[: SYSTEMS // 2], "zslab", down)
    swap = [(i, i ^ 1) for i in range(4)]
    other = lax.ppermute(block[:, 16:ROWS_AT], "group", swap)
    inner = call(
        inner_kernel,
        (f32(SYSTEMS, 2, OWN, TILES, 8, 128), f32(2, OWN, TILES, 8, 128), f32(128, 8, 128)),
        [VMEM, VMEM],
        (VMEM,) * 3,
        (),
        "inner",
        10**8,
    )(block, other)
    low, high, inner = lax.optimization_barrier((low, high, inner))
    ends = jnp.concatenate([low[:, 16:ROWS_AT], high[:, 16:ROWS_AT]], axis=0)
    ends = lax.ppermute(ends, "group", swap)
    plane = (TILES, 8, 128)
    basis, gram, dens = call(
        outer_kernel,
        (f32(BASIS, 2, WINDOW, *plane), f32(1, 128), f32(2, 8, 128)),
        [VMEM] * 7,
        (VMEM, VMEM, VMEM),
        [pltpu.VMEM((2, WINDOW) + plane, jnp.float32), pltpu.VMEM((128, 8, 128), jnp.float32)],
        "outer",
        2 * 10**8,
    )(block, low, high, ends, *inner)
    grams = lax.all_to_all(
        jnp.broadcast_to(gram[None], (SYSTEMS, 1, 128)), "zslab", 0, 0,
        axis_index_groups=columns, tiled=True,
    )
    pick, nudge = gram_tables()
    solved = call(
        combine_kernel, f32(SYSTEMS, 33, 8, 128), [VMEM, VMEM, VMEM, VMEM], VMEM, (), "combine"
    )(grams, jnp.asarray(pick), jnp.asarray(nudge), basis)
    fields = lax.all_to_all(solved, "zslab", 0, 0, axis_index_groups=planes_of, tiled=True)
    half = f32(SYSTEMS // 2, 2, 2, 8 * TILES, 128)
    forward, adjoint = call(fields_kernel, (half, half), [VMEM], (VMEM,) * 2, (), "fields", 10**7)(fields)
    mine, beside, across = call(
        terms_kernel,
        (f32(5, 8, 128), f32(5, 8, 128), f32(2, 5, 8, 128)),
        [VMEM],
        (VMEM,) * 3,
        [pltpu.VMEM((4, 8 * TILES, 128), jnp.float32)],
        "terms",
    )(fields)
    across = lax.ppermute(across, "group", [(i, i ^ 2) for i in range(4)])
    across, forward, adjoint = lax.optimization_barrier((across, forward, adjoint))
    beside = lax.ppermute(beside + across[1], "group", swap)
    new_density, flag = call(
        density_kernel,
        (f32(2, 8, 128), f32(1)),
        [VMEM] * 5,
        (VMEM, SMEM),
        (),
        "density",
    )(mine, across, beside, own_rows, dens)

    def again(state):
        held = (background, absorb, density, profiles, adjoint_source)
        held = row_major(state[0], held, "arguments")
        results = iterate_on_device(*held, port_modes, design_start)
        return (jnp.zeros((), jnp.float32),) + tuple(row_major(state[0], results, "results"))

    state = (flag[0], forward, adjoint, new_density)
    return lax.while_loop(lambda state: state[0] > 0.0, again, state)[1:]


def solution(mesh):
    return jax.shard_map(
        on_device,
        mesh=mesh,
        in_specs=(
            P("zslab", None, None),
            P("zslab", None, None),
            P("zslab", None, None),
            P(None, None, "zslab", None, None),
            P("group", None, "zslab", None, None),
            P("group"),
            P(),
        ),
        out_specs=(
            P("group", None, "zslab", None, None),
            P("group", None, "zslab", None, None),
            P("zslab", "group", None),
        ),
        check_vma=False,
    )
```

```python
import functools

import jax
import jax.numpy as jnp
import numpy as np
from jax import lax
from jax.experimental import pallas as pl
from jax.experimental.pallas import tpu as pltpu
from jax.sharding import PartitionSpec as P

ITERS = 4


wave_sq = 0.1
step_size = 2.0
perm_span = 10.0
low_perm = 2.1
sharpness = 8.0
threshold = 0.5


def with_halo(block, sides, width):
    for axis, dim in sides:
        count = lax.axis_size(axis)
        forward = [(i, i + 1) for i in range(count - 1)]
        backward = [(target, source) for source, target in forward]
        low = lax.ppermute(
            lax.slice_in_dim(block, block.shape[dim] - width, None, axis=dim), axis, forward
        )
        high = lax.ppermute(lax.slice_in_dim(block, 0, width, axis=dim), axis, backward)
        block = jnp.concatenate([low, block, high], axis=dim)
    return block


def scaled(coef, field):
    coef_re = coef[0].reshape((-1, 1, 1, 1))
    coef_im = coef[1].reshape((-1, 1, 1, 1))
    real_part = coef_re * field[:, 0] - coef_im * field[:, 1]
    imag_part = coef_re * field[:, 1] + coef_im * field[:, 0]
    return jnp.stack([real_part, imag_part], axis=1)


def product_pair(left, right):
    real_part = jnp.sum(left[:, 0] * right[:, 0] + left[:, 1] * right[:, 1], axis=(1, 2, 3))
    imag_part = jnp.sum(left[:, 0] * right[:, 1] - left[:, 1] * right[:, 0], axis=(1, 2, 3))
    return (real_part, imag_part)


def divide_pair(top, bottom):
    denominator = bottom[0] * bottom[0] + bottom[1] * bottom[1]
    return (
        (top[0] * bottom[0] + top[1] * bottom[1]) / denominator,
        (top[1] * bottom[0] - top[0] * bottom[1]) / denominator,
    )


def multiply_pair(left, right):
    return (left[0] * right[0] - left[1] * right[1], left[0] * right[1] + left[1] * right[0])


def with_planes(field):
    return with_halo(field, (("zslab", 2),), 1)


def operate(field, diag_re, diag_im):
    padded = jnp.pad(with_planes(field), ((0, 0), (0, 0), (0, 0), (1, 1), (1, 1)))
    beside = padded[:, :, 2:, 1:-1, 1:-1] + padded[:, :, :-2, 1:-1, 1:-1]
    beside = beside + padded[:, :, 1:-1, 2:, 1:-1] + padded[:, :, 1:-1, :-2, 1:-1]
    beside = beside + padded[:, :, 1:-1, 1:-1, 2:] + padded[:, :, 1:-1, 1:-1, :-2]
    real_part = diag_re * field[:, 0] - diag_im * field[:, 1]
    imag_part = diag_re * field[:, 1] + diag_im * field[:, 0]
    return jnp.stack([real_part, imag_part], axis=1) - beside


def bicgstab(sources, diag_re, diag_im):
    solution = jnp.zeros_like(sources)
    residual = sources
    direction = sources
    bilinear = lax.psum(product_pair(sources, residual), "zslab")
    for iteration in range(ITERS):
        image = operate(direction, diag_re, diag_im)
        along = lax.psum(product_pair(sources, image), "zslab")
        advance = divide_pair(bilinear, along)
        halfway = residual - scaled(advance, image)
        second = operate(halfway, diag_re, diag_im)
        cross_re, cross_im = product_pair(second, halfway)
        energy = jnp.sum(second[:, 0] * second[:, 0] + second[:, 1] * second[:, 1], axis=(1, 2, 3))
        cross_re, cross_im, energy = lax.psum((cross_re, cross_im, energy), "zslab")
        relax_coef = (cross_re / energy, cross_im / energy)
        solution = solution + scaled(advance, direction) + scaled(relax_coef, halfway)
        residual = halfway - scaled(relax_coef, second)
        if iteration + 1 < ITERS:
            bilinear_new = lax.psum(product_pair(sources, residual), "zslab")
        if iteration + 1 < ITERS:
            blend_coef = multiply_pair(
                divide_pair(bilinear_new, bilinear), divide_pair(advance, relax_coef)
            )
            direction = residual + scaled(blend_coef, direction - scaled(relax_coef, image))
            bilinear = bilinear_new
    return solution


def iterate_on_device(background, absorb, density, profiles, adjoint_source, port_modes, design_start):
    planes_dev = density.shape[0]
    rows_all = density.shape[1]
    first_plane = lax.axis_index("zslab") * planes_dev
    design_depth = planes_dev * lax.axis_size("zslab") // 2
    planes = first_plane + jnp.arange(planes_dev)
    in_design = (planes >= design_start[0]) & (planes < design_start[0] + design_depth)
    in_design = in_design[:, None, None]
    permittivity = jnp.where(in_design, low_perm + perm_span * density, background)
    diag_re = 6.0 - wave_sq * permittivity
    selector = (port_modes[:, None] == jnp.arange(profiles.shape[0])[None, :]).astype(jnp.float32)
    forward_source = jnp.einsum(
        "pm,mczyx->pczyx", selector, profiles, precision=lax.Precision.HIGHEST
    )
    port_count = forward_source.shape[0]
    sources = jnp.concatenate([forward_source, adjoint_source], axis=0)
    fields = bicgstab(sources, diag_re, absorb)
    forward_field = fields[:port_count]
    adjoint_field = fields[port_count:]
    terms = forward_field[:, 0] * adjoint_field[:, 0] - forward_field[:, 1] * adjoint_field[:, 1]
    local_term = -wave_sq * jnp.sum(terms, axis=0)
    rows_share = rows_all // lax.axis_size("group")
    row_start = lax.axis_index("group") * rows_share
    total = lax.psum(local_term, "group")
    gradient = lax.dynamic_slice_in_dim(total, row_start, rows_share, 1)
    density_rows = lax.dynamic_slice_in_dim(density, row_start, rows_share, 1)
    updated = jnp.where(
        in_design, jnp.clip(density_rows - step_size * perm_span * gradient, 0.0, 1.0), density_rows
    )
    extended = with_halo(updated, (("zslab", 0),), 1)
    padded = jnp.pad(extended, ((0, 0), (0, 0), (1, 1)))
    filtered = (
        2.0 * updated
        + padded[2:, :, 1:-1]
        + padded[:-2, :, 1:-1]
        + padded[1:-1, :, 2:]
        + padded[1:-1, :, :-2]
    ) / 6.0
    new_density = (
        jnp.tanh(sharpness * threshold) + jnp.tanh(sharpness * (filtered - threshold))
    ) / (jnp.tanh(sharpness * threshold) + jnp.tanh(sharpness * (1.0 - threshold)))
    return (forward_field, adjoint_field, new_density)


BASIS = 2 * ITERS + 1
CENTRE = 5.3
HALF_RADIUS = 3.0
THIRD = 1.0 / HALF_RADIUS
NUDGE = 1e-6
AGREE = 5e-4
ROWS = 16 * BASIS


def pair_places():
    real, imag, place = {}, {}, 0
    for j in range(BASIS):
        for i in range(j + 1):
            real[(i, j)] = place
            place += 1
    for j in range(BASIS):
        for i in range(j):
            imag[(i, j)] = place
            place += 1
    return real, imag


def gram_tables():
    real, imag = pair_places()
    pick = np.zeros((2 * ROWS + 16, 128), np.float32)
    nudge = np.zeros((2 * ROWS, 128), np.float32)
    rng = np.random.default_rng(7)
    sign_re = {pair: np.where(rng.random(128) < 0.5, -1.0, 1.0) for pair in real}
    sign_im = {pair: np.where(rng.random(128) < 0.5, -1.0, 1.0) for pair in imag}
    for j in range(BASIS):
        for i in range(BASIS):
            row, pair = j * 16 + i, (min(i, j), max(i, j))
            pick[row, real[pair]] = 1.0
            nudge[row] = NUDGE * sign_re[pair]
            if i != j:
                side = 1.0 if i < j else -1.0
                pick[ROWS + row, imag[pair]] = side
                nudge[ROWS + row] = NUDGE * side * sign_im[pair]
        pick[2 * ROWS + j, real[(j, j)]] = 1.0
    nudge[:, 0] = 0.0
    return pick, nudge


def exact_dot(left, right, dims):
    return lax.dot_general(
        left, right, (dims, ((), ())), precision=lax.Precision.HIGHEST,
        preferred_element_type=jnp.float32,
    )


def minus_pair(left, right):
    return (left[0] - right[0], left[1] - right[1])


def plus_pair(left, right):
    return (left[0] + right[0], left[1] + right[1])


def coefficients(gram_re, gram_im):
    row = lax.broadcasted_iota(jnp.int32, (16, 128), 0)
    keep = jnp.where(row == 15, 0.0, HALF_RADIUS)

    def apply(q):
        return tuple(
            CENTRE * v + HALF_RADIUS * pltpu.roll(v, 1, 0) + keep * pltpu.roll(v, 15, 0) for v in q
        )

    def total(v):
        return jnp.sum(v, axis=0, keepdims=True)

    def with_source(q):
        return (
            total(gram_re[0] * q[0] + gram_im[0] * q[1]),
            total(gram_re[0] * q[1] - gram_im[0] * q[0]),
        )

    def times_gram(q):
        out_re = jnp.zeros((16, 128), jnp.float32)
        out_im = jnp.zeros((16, 128), jnp.float32)
        for j in range(BASIS):
            q_re, q_im = q[0][j : j + 1], q[1][j : j + 1]
            out_re = out_re + (gram_re[j] * q_re - gram_im[j] * q_im)
            out_im = out_im + (gram_re[j] * q_im + gram_im[j] * q_re)
        return out_re, out_im

    one = jnp.where(row == 0, 1.0, 0.0)
    zero = jnp.zeros((16, 128), jnp.float32)
    answer, residual, direction = (zero, zero), (one, zero), (one, zero)
    bilinear = with_source(residual)
    for iteration in range(ITERS):
        image = apply(direction)
        advance = divide_pair(bilinear, with_source(image))
        halfway = minus_pair(residual, multiply_pair(advance, image))
        second = apply(halfway)
        weighed = times_gram(second)
        energy = total(second[0] * weighed[0] + second[1] * weighed[1])
        relax = (
            total(weighed[0] * halfway[0] + weighed[1] * halfway[1]) / energy,
            total(weighed[0] * halfway[1] - weighed[1] * halfway[0]) / energy,
        )
        answer = plus_pair(
            answer, plus_pair(multiply_pair(advance, direction), multiply_pair(relax, halfway))
        )
        if iteration + 1 < ITERS:
            residual = minus_pair(halfway, multiply_pair(relax, second))
            bilinear_new = with_source(residual)
            blend = multiply_pair(divide_pair(bilinear_new, bilinear), divide_pair(advance, relax))
            direction = plus_pair(
                residual, multiply_pair(blend, minus_pair(direction, multiply_pair(relax, image)))
            )
            bilinear = bilinear_new
    first = tuple(jnp.broadcast_to(v[:, :1], v.shape) for v in answer)
    apart = minus_pair(answer, first)

    def norm(q):
        weighed = times_gram(q)
        return total(q[0] * weighed[0] + q[1] * weighed[1])

    return first, norm(apart), norm(first)


TILES = 4
SYSTEMS = 8
BLOCK = 12 * TILES // 2 + 1
ROWS_AT = BLOCK - 1
OWN = 16
WINDOW = 32
CORE = 8
VMEM = pl.BlockSpec(memory_space=pltpu.VMEM)
SMEM = pl.BlockSpec(memory_space=pltpu.SMEM)
HBM = pl.BlockSpec(memory_space=pltpu.HBM)
PAIRS = 88
LIMIT = 24 * 1024 * 1024


def call(kernel, outs, specs, out_specs, scratch=(), name=None, flops=0):
    return pl.pallas_call(
        kernel,
        out_shape=outs,
        in_specs=specs,
        out_specs=out_specs,
        scratch_shapes=list(scratch),
        compiler_params=pltpu.CompilerParams(vmem_limit_bytes=LIMIT),
        cost_estimate=pl.CostEstimate(flops=flops, bytes_accessed=1 << 20, transcendentals=0),
        name=name,
    )


def f32(*shape):
    return jax.ShapeDtypeStruct(shape, jnp.float32)


def rows_of(tile):
    return pl.ds(tile, 8, stride=TILES)


def pack_kernel(*refs):
    arguments, out, own, held, sems = refs[:7], refs[7], refs[8], refs[9:16], refs[16]
    modes, start, background, absorb, density, profiles, adjoint = held
    half = SYSTEMS // 2
    place = slab_and_group()
    copies = [
        pltpu.make_async_copy(array, room, sems.at[at])
        for at, (array, room) in enumerate(zip(arguments, held))
    ]
    for copy in copies:
        copy.start()
    for copy in copies[:5]:
        copy.wait()
    for plane in range(2):
        where = place[0] * 2 + plane
        inside = (where >= start[0]) & (where < start[0] + SYSTEMS * SYSTEMS)
        for tile in range(TILES):
            rows = rows_of(tile)
            perm = jnp.where(
                inside, low_perm + perm_span * density[plane, rows], background[plane, rows]
            )
            diag_re = ((6.0 - wave_sq * perm) - CENTRE) * THIRD
            diag_im = absorb[plane, rows] * THIRD
            part = jnp.where(place[1] % 2 == 0, diag_re, diag_im)
            for system in range(SYSTEMS):
                out[system, 16 + plane * TILES + tile] = part
    share = pl.ds(pl.multiple_of(place[1] * 8, 8), 8)
    own[0] = density[0, share]
    own[1] = density[1, share]
    own[2] = jnp.full((8, 128), start[0]).astype(jnp.float32)
    after = (place[0] + 1) % SYSTEMS
    for slab in range(SYSTEMS):
        out[slab, ROWS_AT] = jnp.where(after == slab, density[1, share], density[0, share])
    for copy in copies[5:]:
        copy.wait()
    for system in range(half):
        mode = modes[system]
        for part in range(2):
            for plane in range(2):
                for tile in range(TILES):
                    at = (part * 2 + plane) * TILES + tile
                    out[system, at] = profiles[mode, part, plane, rows_of(tile)]
                    out[half + system, at] = adjoint[system, part, plane, rows_of(tile)]


def slab_and_group():
    return lax.axis_index("zslab"), lax.axis_index("group")


class Stencil:
    def __init__(self):
        row = lax.broadcasted_iota(jnp.int32, (8, 128), 0)
        lane = lax.broadcasted_iota(jnp.int32, (8, 128), 1)
        self.first_row, self.last_row = row == 0, row == 7
        self.first_lane, self.last_lane = lane == 0, lane == 127

    def beside(self, below, here, above):
        up = jnp.where(self.first_row, 0.0, pltpu.roll(here[TILES - 1], 1, 0))
        down = jnp.where(self.last_row, 0.0, pltpu.roll(here[0], 7, 0))
        rows = [up] + list(here) + [down]
        sums = []
        for tile in range(TILES):
            left = jnp.where(self.first_lane, 0.0, pltpu.roll(here[tile], 1, 1))
            right = jnp.where(self.last_lane, 0.0, pltpu.roll(here[tile], 127, 1))
            z_sum = below[tile] + above[tile]
            sums.append((z_sum + (rows[tile] + rows[tile + 2])) + (left + right))
        return sums

    def run(self, basis, diag, level, first, last, third_of):
        def load(at):
            return [[basis[level, part, at, tile] for tile in range(TILES)] for part in range(2)]

        below, here = load(first - 1), load(first)
        for at in range(first, last):
            above = load(at + 1)
            third = third_of(at)
            near = [self.beside(below[part], here[part], above[part]) for part in range(2)]
            for tile in range(TILES):
                diag_re, diag_im = diag[0, at, tile], diag[1, at, tile]
                real, imag = here[0][tile], here[1][tile]
                new_re = diag_re * real - diag_im * imag - third * near[0][tile]
                new_im = diag_re * imag + diag_im * real - third * near[1][tile]
                if level > 0:
                    new_re = new_re - basis[level - 1, 0, at, tile]
                    new_im = new_im - basis[level - 1, 1, at, tile]
                basis[level + 1, 0, at, tile] = new_re
                basis[level + 1, 1, at, tile] = new_im
            below, here = here, above


def gram_pass(basis, acc, columns, ranges, shift):
    real_at, imag_at = pair_places()
    pairs = [(i, j) for j in columns for i in range(j + 1)]
    top = max(columns) + 1
    places = []
    for pair in pairs:
        places.append(real_at[pair])
        if pair[0] != pair[1]:
            places.append(imag_at[pair])

    def position(step, sums, first=0):
        window, tile = first + shift + step // TILES, step % TILES
        field = [(basis[k, 0, window, tile], basis[k, 1, window, tile]) for k in range(top)]
        new = []
        for i, j in pairs:
            (i_re, i_im), (j_re, j_im) = field[i], field[j]
            new.append(i_re * j_re + i_im * j_im)
            if i != j:
                new.append(i_re * j_im - i_im * j_re)
        return tuple(total + term for total, term in zip(sums, new))

    sums = tuple(acc[at] for at in places)
    for first, last in ranges:
        sums = lax.fori_loop(
            0, (last - first) * TILES, functools.partial(position, first=first), sums,
            unroll=8,
        )
    for at, value in zip(places, sums):
        acc[at] = value


def inner_kernel(block, other, basis, diag, acc):
    place = slab_and_group()
    core = place[1] % 2

    def load(chunk, _):
        for plane in range(2):
            for part in range(2):
                for tile in range(TILES):
                    at = part * 8 + plane * TILES + tile
                    basis[0, part, 2 * chunk + plane, tile] = block[chunk, at]
            for tile in range(TILES):
                at = plane * TILES + tile
                diag[core, 2 * chunk + plane, tile] = block[chunk, 16 + at]
                diag[1 - core, 2 * chunk + plane, tile] = other[chunk, at]
        return 0

    lax.fori_loop(0, SYSTEMS, load, 0, unroll=SYSTEMS)
    stencil = Stencil()
    for level in range(SYSTEMS - 1):
        stencil.run(basis, diag, level, level + 1, OWN - 1 - level, lambda at: THIRD)
    acc[...] = jnp.zeros_like(acc)
    for columns, ranges in INNER_PASSES:
        gram_pass(basis, acc, columns, ranges, 0)


INNER_PASSES = (
    ((0, 1, 2, 3, 4), ((4, 12),)),
    ((0, 1, 2), ((2, 4), (12, 14))),
    ((5, 6), ((6, 10),)),
)
OUTER_PASSES = (
    ((0, 1, 2, 3, 4), ((0, 2), (14, 16))),
    ((3, 4), ((2, 4), (12, 14))),
    ((5, 6), ((0, 6), (10, 16))),
    ((7,), ((0, 16),)),
    ((8,), ((0, 16),)),
)


def outer_kernel(
    block, low, high, other, inner, inner_diag, inner_acc, basis, gram, dens, diag, acc
):
    place = slab_and_group()
    core = place[1] % 2

    def load(source, first, at):
        def one(chunk, _):
            for plane in range(2):
                window = at + 2 * chunk + plane
                for part in range(2):
                    for tile in range(TILES):
                        spot = part * 8 + plane * TILES + tile
                        basis[0, part, window, tile] = source[chunk, spot]
                for tile in range(TILES):
                    spot = plane * TILES + tile
                    diag[core, window, tile] = source[chunk, 16 + spot]
                    diag[1 - core, window, tile] = other[first + chunk, spot]
            return 0

        lax.fori_loop(0, SYSTEMS // 2, one, 0, unroll=SYSTEMS // 2)

    load(low, 0, 0)
    load(high, SYSTEMS // 2, CORE + OWN)
    for level in range(SYSTEMS):

        def keep(at, _, level=level):
            for part in range(2):
                for tile in range(TILES):
                    basis[level, part, CORE + at, tile] = inner[level, part, at, tile]
                    if level == 0:
                        diag[part, CORE + at, tile] = inner_diag[part, at, tile]
            return 0

        lax.fori_loop(level, OWN - level, keep, 0, unroll=OWN - 2 * level)
    acc[...] = inner_acc[...]

    me = place[0] % SYSTEMS
    dens[0] = jnp.where(
        me > 0, block[jnp.maximum(me - 1, 0), ROWS_AT], low[SYSTEMS // 2 - 1, ROWS_AT]
    )
    dens[1] = jnp.where(
        me < SYSTEMS - 1, block[jnp.minimum(me + 1, SYSTEMS - 1), ROWS_AT], high[0, ROWS_AT]
    )

    third_low = jnp.where(place[0] >= SYSTEMS, THIRD, 0.0)
    third_high = jnp.where(place[0] < SYSTEMS * (SYSTEMS - 1), THIRD, 0.0)
    stencil = Stencil()
    for level in range(BASIS - 1):
        lower, upper = level + 1, WINDOW - 1 - level
        stencil.run(
            basis, diag, level, lower, lower + CORE,
            lambda at: third_low if at < CORE else THIRD,
        )
        stencil.run(
            basis, diag, level, upper - CORE, upper,
            lambda at: third_high if at >= CORE + OWN else THIRD,
        )
    for columns, ranges in OUTER_PASSES:
        gram_pass(basis, acc, columns, ranges, CORE)
    by_pair = jnp.concatenate(
        [jnp.sum(acc[...], axis=1), jnp.zeros((128 - PAIRS, 128), jnp.float32)], axis=0
    )
    ones = jnp.ones((8, 128), jnp.float32)
    gram[...] = exact_dot(ones, by_pair, ((1,), (1,)))[0:1]


def combine_kernel(grams, pick, nudge, basis, out):
    row = grams[0]
    for other in range(1, SYSTEMS):
        row = row + grams[other]
    ones = jnp.ones((128, 128), jnp.float32)
    picked = exact_dot(pick[...] * row, ones, ((1,), (0,)))
    norms = jnp.sqrt(picked[2 * ROWS :])
    gram = []
    for column in range(2 * BASIS):
        rows = slice(16 * column, 16 * column + 16)
        scale = norms * norms[column % BASIS : column % BASIS + 1]
        gram.append(picked[rows] + nudge[rows] * scale)
    answer, apart, size = coefficients(gram[:BASIS], gram[BASIS:])
    agrees = jnp.max(jnp.where(apart <= AGREE * AGREE * size, 0.0, 1.0))
    flag = jnp.zeros((8, 128), jnp.float32) + agrees
    for slab in range(SYSTEMS):
        out[slab, 32] = flag
    weight = [
        (
            jnp.broadcast_to(answer[0][k : k + 1], (8, 128)),
            jnp.broadcast_to(answer[1][k : k + 1], (8, 128)),
        )
        for k in range(BASIS - 1)
    ]

    def solve_plane(plane, goals):
        for tile in range(TILES):
            real = jnp.zeros((8, 128), jnp.float32)
            imag = jnp.zeros((8, 128), jnp.float32)
            for k in range(BASIS - 1):
                b_re, b_im = basis[k, 0, plane, tile], basis[k, 1, plane, tile]
                real = real + (weight[k][0] * b_re - weight[k][1] * b_im)
                imag = imag + (weight[k][0] * b_im + weight[k][1] * b_re)
            for slab, at in goals:
                out[slab, at * TILES + tile] = real
                out[slab, (4 + at) * TILES + tile] = imag

    def middle(slab, _):
        for plane in range(2):
            solve_plane(CORE - 1 + 2 * slab + plane, ((slab, plane), (slab - 1, 2 + plane)))
        return 0

    for plane in range(2):
        solve_plane(CORE - 1 + plane, ((0, plane),))
        solve_plane(CORE + OWN - 1 + plane, ((SYSTEMS - 1, 2 + plane),))
    lax.fori_loop(1, SYSTEMS, middle, 0)


def fields_kernel(fields, forward, adjoint):
    half = SYSTEMS // 2
    for port in range(half):
        for part in range(2):
            for plane in range(2):
                for tile in range(TILES):
                    at = (part * 4 + 1 + plane) * TILES + tile
                    forward[port, part, plane, rows_of(tile)] = fields[port, at]
                    adjoint[port, part, plane, rows_of(tile)] = fields[half + port, at]


def terms_kernel(fields, mine, beside, across, natural):
    half = SYSTEMS // 2
    for plane in range(4):
        for tile in range(TILES):
            real, imag = plane * TILES + tile, (4 + plane) * TILES + tile
            total = None
            for port in range(half):
                term = fields[port, real] * fields[half + port, real]
                term = term - fields[port, imag] * fields[half + port, imag]
                total = term if total is None else total + term
            natural[plane, rows_of(tile)] = total
    flag = fields[0, 32]
    for system in range(1, SYSTEMS):
        flag = flag + fields[system, 32]
    group = slab_and_group()[1]
    core, chip = group % 2, group // 2
    for out, pair, side in (
        (mine, chip, core),
        (beside, chip, 1 - core),
        (across.at[0], 1 - chip, core),
        (across.at[1], 1 - chip, 1 - core),
    ):
        rows = pl.ds(pl.multiple_of((2 * pair + side) * 8, 8), 8)
        for plane in range(4):
            out[plane] = natural[plane, rows]
        out[4] = flag


def density_kernel(mine, across, beside, own, dens, out, flag):
    lane = lax.broadcasted_iota(jnp.int32, (8, 128), 1)
    updated = []
    for plane in range(4):
        gradient = -wave_sq * (mine[plane] + across[0, plane] + beside[plane])
        where = slab_and_group()[0] * 2 + plane - 1
        depth = where.astype(jnp.float32) - own[2]
        inside = (depth >= 0.0) & (depth < SYSTEMS * SYSTEMS)
        rows = (dens[0], own[0], own[1], dens[1])[plane]
        moved = jnp.clip(rows - step_size * perm_span * gradient, 0.0, 1.0)
        rows = jnp.where(inside, moved, rows)
        exists = (where >= 0) & (where < 2 * SYSTEMS * SYSTEMS)
        updated.append(jnp.where(exists, rows, 0.0))
    for plane in range(2):
        own = updated[plane + 1]
        right = jnp.where(lane == 127, 0.0, pltpu.roll(own, 127, 1))
        left = jnp.where(lane == 0, 0.0, pltpu.roll(own, 1, 1))
        filtered = (2.0 * own + updated[plane + 2] + updated[plane] + right + left) / 6.0
        edge = float(np.tanh(sharpness * threshold))
        other_edge = float(np.tanh(sharpness * (1.0 - threshold)))
        out[plane] = (edge + jnp.tanh(sharpness * (filtered - threshold))) / (edge + other_edge)
    flag[0] = jnp.max(mine[4] + across[0, 4] + beside[4])


def copy_kernel(count, *refs):
    sems = refs[-1]
    arrays = refs[-1 - 2 * count : -1]
    copies = [
        pltpu.make_async_copy(arrays[at], arrays[count + at], sems.at[at]) for at in range(count)
    ]
    for copy in copies:
        copy.start()
    for copy in copies:
        copy.wait()


def row_major(mark, arrays, name):
    count = len(arrays)
    return call(
        functools.partial(copy_kernel, count),
        tuple(jax.ShapeDtypeStruct(array.shape, array.dtype) for array in arrays),
        [SMEM] + [HBM] * count,
        (HBM,) * count,
        [pltpu.SemaphoreType.DMA((count,))],
        name,
    )(mark.reshape(1), *arrays)


def on_device(background, absorb, density, profiles, adjoint_source, port_modes, design_start):
    planes_of = [[z * SYSTEMS + l for l in range(SYSTEMS)] for z in range(SYSTEMS)]
    columns = [[z * SYSTEMS + l for z in range(SYSTEMS)] for l in range(SYSTEMS)]
    packed, own_rows = call(
        pack_kernel,
        (f32(SYSTEMS, BLOCK, 8, 128), f32(3, 8, 128)),
        [HBM] * 7,
        (VMEM, VMEM),
        [pltpu.SMEM(array.shape, array.dtype) for array in (port_modes, design_start)]
        + [
            pltpu.VMEM(array.shape, array.dtype)
            for array in (background, absorb, density, profiles, adjoint_source)
        ]
        + [pltpu.SemaphoreType.DMA((7,))],
        "pack",
    )(port_modes, design_start, background, absorb, density, profiles, adjoint_source)
    block = lax.all_to_all(packed, "zslab", 0, 0, axis_index_groups=planes_of, tiled=True)
    count = SYSTEMS * SYSTEMS
    up = [(i, i + SYSTEMS) for i in range(count - SYSTEMS)]
    down = [(target, source) for source, target in up]
    low = lax.ppermute(block[SYSTEMS // 2 :], "zslab", up)
    high = lax.ppermute(block[: SYSTEMS // 2], "zslab", down)
    swap = [(i, i ^ 1) for i in range(4)]
    other = lax.ppermute(block[:, 16:ROWS_AT], "group", swap)
    inner = call(
        inner_kernel,
        (f32(SYSTEMS, 2, OWN, TILES, 8, 128), f32(2, OWN, TILES, 8, 128), f32(PAIRS, 8, 128)),
        [VMEM, VMEM],
        (VMEM,) * 3,
        (),
        "inner",
        10**8,
    )(block, other)
    low, high, inner = lax.optimization_barrier((low, high, inner))
    ends = jnp.concatenate([low[:, 16:ROWS_AT], high[:, 16:ROWS_AT]], axis=0)
    ends = lax.ppermute(ends, "group", swap)
    plane = (TILES, 8, 128)
    basis, gram, dens = call(
        outer_kernel,
        (f32(BASIS, 2, WINDOW, *plane), f32(1, 128), f32(2, 8, 128)),
        [VMEM] * 7,
        (VMEM, VMEM, VMEM),
        [pltpu.VMEM((2, WINDOW) + plane, jnp.float32), pltpu.VMEM((PAIRS, 8, 128), jnp.float32)],
        "outer",
        2 * 10**8,
    )(block, low, high, ends, *inner)
    grams = lax.all_to_all(
        jnp.broadcast_to(gram[None], (SYSTEMS, 1, 128)), "zslab", 0, 0,
        axis_index_groups=columns, tiled=True,
    )
    pick, nudge = gram_tables()
    solved = call(
        combine_kernel, f32(SYSTEMS, 33, 8, 128), [VMEM, VMEM, VMEM, VMEM], VMEM, (), "combine"
    )(grams, jnp.asarray(pick), jnp.asarray(nudge), basis)
    fields = lax.all_to_all(solved, "zslab", 0, 0, axis_index_groups=planes_of, tiled=True)
    half = f32(SYSTEMS // 2, 2, 2, 8 * TILES, 128)
    forward, adjoint = call(fields_kernel, (half, half), [VMEM], (VMEM,) * 2, (), "fields", 10**7)(fields)
    mine, beside, across = call(
        terms_kernel,
        (f32(5, 8, 128), f32(5, 8, 128), f32(2, 5, 8, 128)),
        [VMEM],
        (VMEM,) * 3,
        [pltpu.VMEM((4, 8 * TILES, 128), jnp.float32)],
        "terms",
    )(fields)
    across = lax.ppermute(across, "group", [(i, i ^ 2) for i in range(4)])
    across, forward, adjoint = lax.optimization_barrier((across, forward, adjoint))
    beside = lax.ppermute(beside + across[1], "group", swap)
    new_density, flag = call(
        density_kernel,
        (f32(2, 8, 128), f32(1)),
        [VMEM] * 5,
        (VMEM, SMEM),
        (),
        "density",
    )(mine, across, beside, own_rows, dens)

    def again(state):
        held = (background, absorb, density, profiles, adjoint_source)
        held = row_major(state[0], held, "arguments")
        results = iterate_on_device(*held, port_modes, design_start)
        return (jnp.zeros((), jnp.float32),) + tuple(row_major(state[0], results, "results"))

    state = (flag[0], forward, adjoint, new_density)
    return lax.while_loop(lambda state: state[0] > 0.0, again, state)[1:]


def solution(mesh):
    return jax.shard_map(
        on_device,
        mesh=mesh,
        in_specs=(
            P("zslab", None, None),
            P("zslab", None, None),
            P("zslab", None, None),
            P(None, None, "zslab", None, None),
            P("group", None, "zslab", None, None),
            P("group"),
            P(),
        ),
        out_specs=(
            P("group", None, "zslab", None, None),
            P("group", None, "zslab", None, None),
            P("zslab", "group", None),
        ),
        check_vma=False,
    )
```

```python
import functools

import jax
import jax.numpy as jnp
import numpy as np
from jax import lax
from jax.experimental import pallas as pl
from jax.experimental.pallas import tpu as pltpu
from jax.sharding import PartitionSpec as P

ITERS = 4


wave_sq = 0.1
step_size = 2.0
perm_span = 10.0
low_perm = 2.1
sharpness = 8.0
threshold = 0.5


def with_halo(block, sides, width):
    for axis, dim in sides:
        count = lax.axis_size(axis)
        forward = [(i, i + 1) for i in range(count - 1)]
        backward = [(target, source) for source, target in forward]
        low = lax.ppermute(
            lax.slice_in_dim(block, block.shape[dim] - width, None, axis=dim), axis, forward
        )
        high = lax.ppermute(lax.slice_in_dim(block, 0, width, axis=dim), axis, backward)
        block = jnp.concatenate([low, block, high], axis=dim)
    return block


def scaled(coef, field):
    coef_re = coef[0].reshape((-1, 1, 1, 1))
    coef_im = coef[1].reshape((-1, 1, 1, 1))
    real_part = coef_re * field[:, 0] - coef_im * field[:, 1]
    imag_part = coef_re * field[:, 1] + coef_im * field[:, 0]
    return jnp.stack([real_part, imag_part], axis=1)


def product_pair(left, right):
    real_part = jnp.sum(left[:, 0] * right[:, 0] + left[:, 1] * right[:, 1], axis=(1, 2, 3))
    imag_part = jnp.sum(left[:, 0] * right[:, 1] - left[:, 1] * right[:, 0], axis=(1, 2, 3))
    return (real_part, imag_part)


def divide_pair(top, bottom):
    denominator = bottom[0] * bottom[0] + bottom[1] * bottom[1]
    return (
        (top[0] * bottom[0] + top[1] * bottom[1]) / denominator,
        (top[1] * bottom[0] - top[0] * bottom[1]) / denominator,
    )


def multiply_pair(left, right):
    return (left[0] * right[0] - left[1] * right[1], left[0] * right[1] + left[1] * right[0])


def with_planes(field):
    return with_halo(field, (("zslab", 2),), 1)


def operate(field, diag_re, diag_im):
    padded = jnp.pad(with_planes(field), ((0, 0), (0, 0), (0, 0), (1, 1), (1, 1)))
    beside = padded[:, :, 2:, 1:-1, 1:-1] + padded[:, :, :-2, 1:-1, 1:-1]
    beside = beside + padded[:, :, 1:-1, 2:, 1:-1] + padded[:, :, 1:-1, :-2, 1:-1]
    beside = beside + padded[:, :, 1:-1, 1:-1, 2:] + padded[:, :, 1:-1, 1:-1, :-2]
    real_part = diag_re * field[:, 0] - diag_im * field[:, 1]
    imag_part = diag_re * field[:, 1] + diag_im * field[:, 0]
    return jnp.stack([real_part, imag_part], axis=1) - beside


def bicgstab(sources, diag_re, diag_im):
    solution = jnp.zeros_like(sources)
    residual = sources
    direction = sources
    bilinear = lax.psum(product_pair(sources, residual), "zslab")
    for iteration in range(ITERS):
        image = operate(direction, diag_re, diag_im)
        along = lax.psum(product_pair(sources, image), "zslab")
        advance = divide_pair(bilinear, along)
        halfway = residual - scaled(advance, image)
        second = operate(halfway, diag_re, diag_im)
        cross_re, cross_im = product_pair(second, halfway)
        energy = jnp.sum(second[:, 0] * second[:, 0] + second[:, 1] * second[:, 1], axis=(1, 2, 3))
        cross_re, cross_im, energy = lax.psum((cross_re, cross_im, energy), "zslab")
        relax_coef = (cross_re / energy, cross_im / energy)
        solution = solution + scaled(advance, direction) + scaled(relax_coef, halfway)
        residual = halfway - scaled(relax_coef, second)
        if iteration + 1 < ITERS:
            bilinear_new = lax.psum(product_pair(sources, residual), "zslab")
        if iteration + 1 < ITERS:
            blend_coef = multiply_pair(
                divide_pair(bilinear_new, bilinear), divide_pair(advance, relax_coef)
            )
            direction = residual + scaled(blend_coef, direction - scaled(relax_coef, image))
            bilinear = bilinear_new
    return solution


def iterate_on_device(background, absorb, density, profiles, adjoint_source, port_modes, design_start):
    planes_dev = density.shape[0]
    rows_all = density.shape[1]
    first_plane = lax.axis_index("zslab") * planes_dev
    design_depth = planes_dev * lax.axis_size("zslab") // 2
    planes = first_plane + jnp.arange(planes_dev)
    in_design = (planes >= design_start[0]) & (planes < design_start[0] + design_depth)
    in_design = in_design[:, None, None]
    permittivity = jnp.where(in_design, low_perm + perm_span * density, background)
    diag_re = 6.0 - wave_sq * permittivity
    selector = (port_modes[:, None] == jnp.arange(profiles.shape[0])[None, :]).astype(jnp.float32)
    forward_source = jnp.einsum(
        "pm,mczyx->pczyx", selector, profiles, precision=lax.Precision.HIGHEST
    )
    port_count = forward_source.shape[0]
    sources = jnp.concatenate([forward_source, adjoint_source], axis=0)
    fields = bicgstab(sources, diag_re, absorb)
    forward_field = fields[:port_count]
    adjoint_field = fields[port_count:]
    terms = forward_field[:, 0] * adjoint_field[:, 0] - forward_field[:, 1] * adjoint_field[:, 1]
    local_term = -wave_sq * jnp.sum(terms, axis=0)
    rows_share = rows_all // lax.axis_size("group")
    row_start = lax.axis_index("group") * rows_share
    total = lax.psum(local_term, "group")
    gradient = lax.dynamic_slice_in_dim(total, row_start, rows_share, 1)
    density_rows = lax.dynamic_slice_in_dim(density, row_start, rows_share, 1)
    updated = jnp.where(
        in_design, jnp.clip(density_rows - step_size * perm_span * gradient, 0.0, 1.0), density_rows
    )
    extended = with_halo(updated, (("zslab", 0),), 1)
    padded = jnp.pad(extended, ((0, 0), (0, 0), (1, 1)))
    filtered = (
        2.0 * updated
        + padded[2:, :, 1:-1]
        + padded[:-2, :, 1:-1]
        + padded[1:-1, :, 2:]
        + padded[1:-1, :, :-2]
    ) / 6.0
    new_density = (
        jnp.tanh(sharpness * threshold) + jnp.tanh(sharpness * (filtered - threshold))
    ) / (jnp.tanh(sharpness * threshold) + jnp.tanh(sharpness * (1.0 - threshold)))
    return (forward_field, adjoint_field, new_density)


BASIS = 2 * ITERS + 1
CENTRE = 5.3
HALF_RADIUS = 3.0
THIRD = 1.0 / HALF_RADIUS
NUDGE = 1e-6
AGREE = 5e-4
ROWS = 16 * BASIS


def pair_places():
    real, imag, place = {}, {}, 0
    for j in range(BASIS):
        for i in range(j + 1):
            real[(i, j)] = place
            place += 1
    for j in range(BASIS):
        for i in range(j):
            imag[(i, j)] = place
            place += 1
    return real, imag


def gram_tables():
    real, imag = pair_places()
    pick = np.zeros((2 * ROWS + 16, 128), np.float32)
    nudge = np.zeros((2 * ROWS, 128), np.float32)
    rng = np.random.default_rng(7)
    sign_re = {pair: np.where(rng.random(128) < 0.5, -1.0, 1.0) for pair in real}
    sign_im = {pair: np.where(rng.random(128) < 0.5, -1.0, 1.0) for pair in imag}
    for j in range(BASIS):
        for i in range(BASIS):
            row, pair = j * 16 + i, (min(i, j), max(i, j))
            pick[row, real[pair]] = 1.0
            nudge[row] = NUDGE * sign_re[pair]
            if i != j:
                side = 1.0 if i < j else -1.0
                pick[ROWS + row, imag[pair]] = side
                nudge[ROWS + row] = NUDGE * side * sign_im[pair]
        pick[2 * ROWS + j, real[(j, j)]] = 1.0
    nudge[:, 0] = 0.0
    return pick, nudge


def exact_dot(left, right, dims):
    return lax.dot_general(
        left, right, (dims, ((), ())), precision=lax.Precision.HIGHEST,
        preferred_element_type=jnp.float32,
    )


def minus_pair(left, right):
    return (left[0] - right[0], left[1] - right[1])


def plus_pair(left, right):
    return (left[0] + right[0], left[1] + right[1])


def coefficients(gram_re, gram_im):
    row = lax.broadcasted_iota(jnp.int32, (16, 128), 0)
    keep = jnp.where(row == 15, 0.0, HALF_RADIUS)

    def apply(q):
        return tuple(
            CENTRE * v + HALF_RADIUS * pltpu.roll(v, 1, 0) + keep * pltpu.roll(v, 15, 0) for v in q
        )

    def total(v):
        return jnp.sum(v, axis=0, keepdims=True)

    def with_source(q):
        return (
            total(gram_re[0] * q[0] + gram_im[0] * q[1]),
            total(gram_re[0] * q[1] - gram_im[0] * q[0]),
        )

    def times_gram(q):
        out_re = jnp.zeros((16, 128), jnp.float32)
        out_im = jnp.zeros((16, 128), jnp.float32)
        for j in range(BASIS):
            q_re, q_im = q[0][j : j + 1], q[1][j : j + 1]
            out_re = out_re + (gram_re[j] * q_re - gram_im[j] * q_im)
            out_im = out_im + (gram_re[j] * q_im + gram_im[j] * q_re)
        return out_re, out_im

    one = jnp.where(row == 0, 1.0, 0.0)
    zero = jnp.zeros((16, 128), jnp.float32)
    answer, residual, direction = (zero, zero), (one, zero), (one, zero)
    bilinear = with_source(residual)
    for iteration in range(ITERS):
        image = apply(direction)
        advance = divide_pair(bilinear, with_source(image))
        halfway = minus_pair(residual, multiply_pair(advance, image))
        second = apply(halfway)
        weighed = times_gram(second)
        energy = total(second[0] * weighed[0] + second[1] * weighed[1])
        relax = (
            total(weighed[0] * halfway[0] + weighed[1] * halfway[1]) / energy,
            total(weighed[0] * halfway[1] - weighed[1] * halfway[0]) / energy,
        )
        answer = plus_pair(
            answer, plus_pair(multiply_pair(advance, direction), multiply_pair(relax, halfway))
        )
        if iteration + 1 < ITERS:
            residual = minus_pair(halfway, multiply_pair(relax, second))
            bilinear_new = with_source(residual)
            blend = multiply_pair(divide_pair(bilinear_new, bilinear), divide_pair(advance, relax))
            direction = plus_pair(
                residual, multiply_pair(blend, minus_pair(direction, multiply_pair(relax, image)))
            )
            bilinear = bilinear_new
    first = tuple(jnp.broadcast_to(v[:, :1], v.shape) for v in answer)
    apart = minus_pair(answer, first)

    def norm(q):
        weighed = times_gram(q)
        return total(q[0] * weighed[0] + q[1] * weighed[1])

    return first, norm(apart), norm(first)


TILES = 4
SYSTEMS = 8
BLOCK = 12 * TILES // 2 + 1
ROWS_AT = BLOCK - 1
OWN = 16
WINDOW = 32
CORE = 8
VMEM = pl.BlockSpec(memory_space=pltpu.VMEM)
SMEM = pl.BlockSpec(memory_space=pltpu.SMEM)
HBM = pl.BlockSpec(memory_space=pltpu.HBM)
PAIRS = 88
LIMIT = 24 * 1024 * 1024


def call(kernel, outs, specs, out_specs, scratch=(), name=None, flops=0):
    return pl.pallas_call(
        kernel,
        out_shape=outs,
        in_specs=specs,
        out_specs=out_specs,
        scratch_shapes=list(scratch),
        compiler_params=pltpu.CompilerParams(vmem_limit_bytes=LIMIT),
        cost_estimate=pl.CostEstimate(flops=flops, bytes_accessed=1 << 20, transcendentals=0),
        name=name,
    )


def f32(*shape):
    return jax.ShapeDtypeStruct(shape, jnp.float32)


def rows_of(tile):
    return pl.ds(tile, 8, stride=TILES)


def pack_kernel(*refs):
    arguments, out, own, held, sems = refs[:7], refs[7], refs[8], refs[9:16], refs[16]
    modes, start, background, absorb, density, profiles, adjoint = held
    half = SYSTEMS // 2
    place = slab_and_group()
    copies = [
        pltpu.make_async_copy(array, room, sems.at[at])
        for at, (array, room) in enumerate(zip(arguments, held))
    ]
    for copy in copies:
        copy.start()
    for copy in copies[:5]:
        copy.wait()
    for plane in range(2):
        where = place[0] * 2 + plane
        inside = (where >= start[0]) & (where < start[0] + SYSTEMS * SYSTEMS)
        for tile in range(TILES):
            rows = rows_of(tile)
            perm = jnp.where(
                inside, low_perm + perm_span * density[plane, rows], background[plane, rows]
            )
            diag_re = ((6.0 - wave_sq * perm) - CENTRE) * THIRD
            diag_im = absorb[plane, rows] * THIRD
            part = jnp.where(place[1] % 2 == 0, diag_re, diag_im)
            for system in range(SYSTEMS):
                out[system, 16 + plane * TILES + tile] = part
    share = pl.ds(pl.multiple_of(place[1] * 8, 8), 8)
    own[0] = density[0, share]
    own[1] = density[1, share]
    own[2] = jnp.full((8, 128), start[0]).astype(jnp.float32)
    after = (place[0] + 1) % SYSTEMS
    for slab in range(SYSTEMS):
        out[slab, ROWS_AT] = jnp.where(after == slab, density[1, share], density[0, share])
    for copy in copies[5:]:
        copy.wait()
    for system in range(half):
        mode = modes[system]
        for part in range(2):
            for plane in range(2):
                for tile in range(TILES):
                    at = (part * 2 + plane) * TILES + tile
                    out[system, at] = profiles[mode, part, plane, rows_of(tile)]
                    out[half + system, at] = adjoint[system, part, plane, rows_of(tile)]


def slab_and_group():
    return lax.axis_index("zslab"), lax.axis_index("group")


class Stencil:
    def __init__(self):
        row = lax.broadcasted_iota(jnp.int32, (8, 128), 0)
        lane = lax.broadcasted_iota(jnp.int32, (8, 128), 1)
        self.first_row, self.last_row = row == 0, row == 7
        self.first_lane, self.last_lane = lane == 0, lane == 127

    def beside(self, below, here, above):
        up = jnp.where(self.first_row, 0.0, pltpu.roll(here[TILES - 1], 1, 0))
        down = jnp.where(self.last_row, 0.0, pltpu.roll(here[0], 7, 0))
        rows = [up] + list(here) + [down]
        sums = []
        for tile in range(TILES):
            left = jnp.where(self.first_lane, 0.0, pltpu.roll(here[tile], 1, 1))
            right = jnp.where(self.last_lane, 0.0, pltpu.roll(here[tile], 127, 1))
            z_sum = below[tile] + above[tile]
            sums.append((z_sum + (rows[tile] + rows[tile + 2])) + (left + right))
        return sums

    def run(self, basis, diag, level, first, last, third_of):
        def load(at):
            return [[basis[level, part, at, tile] for tile in range(TILES)] for part in range(2)]

        below, here = load(first - 1), load(first)
        for at in range(first, last):
            above = load(at + 1)
            third = third_of(at)
            near = [self.beside(below[part], here[part], above[part]) for part in range(2)]
            for tile in range(TILES):
                diag_re, diag_im = diag[0, at, tile], diag[1, at, tile]
                real, imag = here[0][tile], here[1][tile]
                new_re = diag_re * real - diag_im * imag - third * near[0][tile]
                new_im = diag_re * imag + diag_im * real - third * near[1][tile]
                if level > 0:
                    new_re = new_re - basis[level - 1, 0, at, tile]
                    new_im = new_im - basis[level - 1, 1, at, tile]
                basis[level + 1, 0, at, tile] = new_re
                basis[level + 1, 1, at, tile] = new_im
            below, here = here, above


def gram_pass(basis, acc, columns, ranges, shift):
    real_at, imag_at = pair_places()
    pairs = [(i, j) for j in columns for i in range(j + 1)]
    top = max(columns) + 1
    places = []
    for pair in pairs:
        places.append(real_at[pair])
        if pair[0] != pair[1]:
            places.append(imag_at[pair])

    def position(step, sums, first=0):
        window, tile = first + shift + step // TILES, step % TILES
        field = [(basis[k, 0, window, tile], basis[k, 1, window, tile]) for k in range(top)]
        new = []
        for i, j in pairs:
            (i_re, i_im), (j_re, j_im) = field[i], field[j]
            new.append(i_re * j_re + i_im * j_im)
            if i != j:
                new.append(i_re * j_im - i_im * j_re)
        return tuple(total + term for total, term in zip(sums, new))

    sums = tuple(acc[at] for at in places)
    for first, last in ranges:
        sums = lax.fori_loop(
            0, (last - first) * TILES, functools.partial(position, first=first), sums,
            unroll=8,
        )
    for at, value in zip(places, sums):
        acc[at] = value


def inner_kernel(block, other, basis, diag, acc):
    place = slab_and_group()
    core = place[1] % 2

    def load(chunk, _):
        for plane in range(2):
            for part in range(2):
                for tile in range(TILES):
                    at = part * 8 + plane * TILES + tile
                    basis[0, part, 2 * chunk + plane, tile] = block[chunk, at]
            for tile in range(TILES):
                at = plane * TILES + tile
                diag[core, 2 * chunk + plane, tile] = block[chunk, 16 + at]
                diag[1 - core, 2 * chunk + plane, tile] = other[chunk, at]
        return 0

    lax.fori_loop(0, SYSTEMS, load, 0, unroll=SYSTEMS)
    stencil = Stencil()
    for level in range(SYSTEMS - 1):
        stencil.run(basis, diag, level, level + 1, OWN - 1 - level, lambda at: THIRD)
    acc[...] = jnp.zeros_like(acc)
    for columns, ranges in INNER_PASSES:
        gram_pass(basis, acc, columns, ranges, 0)


INNER_PASSES = (
    ((0, 1, 2, 3, 4), ((4, 12),)),
    ((0, 1, 2), ((2, 4), (12, 14))),
    ((5, 6), ((6, 10),)),
)
OUTER_PASSES = (
    ((0, 1, 2, 3, 4), ((0, 2), (14, 16))),
    ((3, 4), ((2, 4), (12, 14))),
    ((5, 6), ((0, 6), (10, 16))),
    ((7,), ((0, 16),)),
    ((8,), ((0, 16),)),
)


UPPER = 14
UPPER_PLANES = WINDOW - UPPER


def upper_kernel(high, other, inner, inner_diag, basis, diag):
    place = slab_and_group()
    core = place[1] % 2
    for chunk in range(SYSTEMS // 2):
        for plane in range(2):
            window = CORE + OWN - UPPER + 2 * chunk + plane
            for tile in range(TILES):
                spot = plane * TILES + tile
                basis[0, 0, window, tile] = high[chunk, spot]
                basis[0, 1, window, tile] = high[chunk, 8 + spot]
                diag[core, window, tile] = high[chunk, 16 + spot]
                diag[1 - core, window, tile] = other[chunk, spot]
    for at in range(OWN - SYSTEMS, OWN):
        for part in range(2):
            for tile in range(TILES):
                diag[part, CORE + at - UPPER, tile] = inner_diag[part, at, tile]
    for level in range(SYSTEMS):
        for at in range(OWN - level - 2, OWN - level):
            for part in range(2):
                for tile in range(TILES):
                    basis[level, part, CORE + at - UPPER, tile] = inner[level, part, at, tile]
    third_high = jnp.where(place[0] < SYSTEMS * (SYSTEMS - 1), THIRD, 0.0)
    stencil = Stencil()
    for level in range(BASIS - 1):
        upper = WINDOW - 1 - level - UPPER
        stencil.run(
            basis, diag, level, upper - CORE, upper,
            lambda at: third_high if at >= CORE + OWN - UPPER else THIRD,
        )


def outer_kernel(
    block, low, high, other, above, inner, inner_diag, inner_acc, basis, gram, dens, diag, acc
):
    place = slab_and_group()
    core = place[1] % 2

    def load(source, first, at):
        def one(chunk, _):
            for plane in range(2):
                window = at + 2 * chunk + plane
                for part in range(2):
                    for tile in range(TILES):
                        spot = part * 8 + plane * TILES + tile
                        basis[0, part, window, tile] = source[chunk, spot]
                for tile in range(TILES):
                    spot = plane * TILES + tile
                    diag[core, window, tile] = source[chunk, 16 + spot]
                    diag[1 - core, window, tile] = other[first + chunk, spot]
            return 0

        lax.fori_loop(0, SYSTEMS // 2, one, 0, unroll=SYSTEMS // 2)

    load(low, 0, 0)
    for level in range(BASIS):
        for window in range(CORE + OWN - level, CORE + OWN + (level < BASIS - 1)):
            for part in range(2):
                for tile in range(TILES):
                    basis[level, part, window, tile] = above[level, part, window - UPPER, tile]
    for level in range(SYSTEMS):

        def keep(at, _, level=level):
            for part in range(2):
                for tile in range(TILES):
                    basis[level, part, CORE + at, tile] = inner[level, part, at, tile]
                    if level == 0:
                        diag[part, CORE + at, tile] = inner_diag[part, at, tile]
            return 0

        lax.fori_loop(level, OWN - level, keep, 0, unroll=OWN - 2 * level)
    acc[...] = inner_acc[...]

    me = place[0] % SYSTEMS
    dens[0] = jnp.where(
        me > 0, block[jnp.maximum(me - 1, 0), ROWS_AT], low[SYSTEMS // 2 - 1, ROWS_AT]
    )
    dens[1] = jnp.where(
        me < SYSTEMS - 1, block[jnp.minimum(me + 1, SYSTEMS - 1), ROWS_AT], high[0, ROWS_AT]
    )

    third_low = jnp.where(place[0] >= SYSTEMS, THIRD, 0.0)
    stencil = Stencil()
    for level in range(BASIS - 1):
        lower = level + 1
        stencil.run(
            basis, diag, level, lower, lower + CORE,
            lambda at: third_low if at < CORE else THIRD,
        )
    for columns, ranges in OUTER_PASSES:
        gram_pass(basis, acc, columns, ranges, CORE)
    by_pair = jnp.concatenate(
        [jnp.sum(acc[...], axis=1), jnp.zeros((128 - PAIRS, 128), jnp.float32)], axis=0
    )
    ones = jnp.ones((8, 128), jnp.float32)
    gram[...] = exact_dot(ones, by_pair, ((1,), (1,)))[0:1]


def combine_kernel(grams, pick, nudge, basis, out):
    row = grams[0]
    for other in range(1, SYSTEMS):
        row = row + grams[other]
    ones = jnp.ones((128, 128), jnp.float32)
    picked = exact_dot(pick[...] * row, ones, ((1,), (0,)))
    norms = jnp.sqrt(picked[2 * ROWS :])
    gram = []
    for column in range(2 * BASIS):
        rows = slice(16 * column, 16 * column + 16)
        scale = norms * norms[column % BASIS : column % BASIS + 1]
        gram.append(picked[rows] + nudge[rows] * scale)
    answer, apart, size = coefficients(gram[:BASIS], gram[BASIS:])
    agrees = jnp.max(jnp.where(apart <= AGREE * AGREE * size, 0.0, 1.0))
    flag = jnp.zeros((8, 128), jnp.float32) + agrees
    for slab in range(SYSTEMS):
        out[slab, 32] = flag
    weight = [
        (
            jnp.broadcast_to(answer[0][k : k + 1], (8, 128)),
            jnp.broadcast_to(answer[1][k : k + 1], (8, 128)),
        )
        for k in range(BASIS - 1)
    ]

    def solve_plane(plane, goals):
        for tile in range(TILES):
            real = jnp.zeros((8, 128), jnp.float32)
            imag = jnp.zeros((8, 128), jnp.float32)
            for k in range(BASIS - 1):
                b_re, b_im = basis[k, 0, plane, tile], basis[k, 1, plane, tile]
                real = real + (weight[k][0] * b_re - weight[k][1] * b_im)
                imag = imag + (weight[k][0] * b_im + weight[k][1] * b_re)
            for slab, at in goals:
                out[slab, at * TILES + tile] = real
                out[slab, (4 + at) * TILES + tile] = imag

    def middle(slab, _):
        for plane in range(2):
            solve_plane(CORE - 1 + 2 * slab + plane, ((slab, plane), (slab - 1, 2 + plane)))
        return 0

    for plane in range(2):
        solve_plane(CORE - 1 + plane, ((0, plane),))
        solve_plane(CORE + OWN - 1 + plane, ((SYSTEMS - 1, 2 + plane),))
    lax.fori_loop(1, SYSTEMS, middle, 0)


def fields_kernel(fields, forward, adjoint):
    half = SYSTEMS // 2
    for port in range(half):
        for part in range(2):
            for plane in range(2):
                for tile in range(TILES):
                    at = (part * 4 + 1 + plane) * TILES + tile
                    forward[port, part, plane, rows_of(tile)] = fields[port, at]
                    adjoint[port, part, plane, rows_of(tile)] = fields[half + port, at]


def terms_kernel(fields, mine, beside, across, natural):
    half = SYSTEMS // 2
    for plane in range(4):
        for tile in range(TILES):
            real, imag = plane * TILES + tile, (4 + plane) * TILES + tile
            total = None
            for port in range(half):
                term = fields[port, real] * fields[half + port, real]
                term = term - fields[port, imag] * fields[half + port, imag]
                total = term if total is None else total + term
            natural[plane, rows_of(tile)] = total
    flag = fields[0, 32]
    for system in range(1, SYSTEMS):
        flag = flag + fields[system, 32]
    group = slab_and_group()[1]
    core, chip = group % 2, group // 2
    for out, pair, side in (
        (mine, chip, core),
        (beside, chip, 1 - core),
        (across.at[0], 1 - chip, core),
        (across.at[1], 1 - chip, 1 - core),
    ):
        rows = pl.ds(pl.multiple_of((2 * pair + side) * 8, 8), 8)
        for plane in range(4):
            out[plane] = natural[plane, rows]
        out[4] = flag


def density_kernel(mine, across, beside, own, dens, out, flag):
    lane = lax.broadcasted_iota(jnp.int32, (8, 128), 1)
    updated = []
    for plane in range(4):
        gradient = -wave_sq * (mine[plane] + across[0, plane] + beside[plane])
        where = slab_and_group()[0] * 2 + plane - 1
        depth = where.astype(jnp.float32) - own[2]
        inside = (depth >= 0.0) & (depth < SYSTEMS * SYSTEMS)
        rows = (dens[0], own[0], own[1], dens[1])[plane]
        moved = jnp.clip(rows - step_size * perm_span * gradient, 0.0, 1.0)
        rows = jnp.where(inside, moved, rows)
        exists = (where >= 0) & (where < 2 * SYSTEMS * SYSTEMS)
        updated.append(jnp.where(exists, rows, 0.0))
    for plane in range(2):
        own = updated[plane + 1]
        right = jnp.where(lane == 127, 0.0, pltpu.roll(own, 127, 1))
        left = jnp.where(lane == 0, 0.0, pltpu.roll(own, 1, 1))
        filtered = (2.0 * own + updated[plane + 2] + updated[plane] + right + left) / 6.0
        edge = float(np.tanh(sharpness * threshold))
        other_edge = float(np.tanh(sharpness * (1.0 - threshold)))
        out[plane] = (edge + jnp.tanh(sharpness * (filtered - threshold))) / (edge + other_edge)
    flag[0] = jnp.max(mine[4] + across[0, 4] + beside[4])


def copy_kernel(count, *refs):
    sems = refs[-1]
    arrays = refs[-1 - 2 * count : -1]
    copies = [
        pltpu.make_async_copy(arrays[at], arrays[count + at], sems.at[at]) for at in range(count)
    ]
    for copy in copies:
        copy.start()
    for copy in copies:
        copy.wait()


def row_major(mark, arrays, name):
    count = len(arrays)
    return call(
        functools.partial(copy_kernel, count),
        tuple(jax.ShapeDtypeStruct(array.shape, array.dtype) for array in arrays),
        [SMEM] + [HBM] * count,
        (HBM,) * count,
        [pltpu.SemaphoreType.DMA((count,))],
        name,
    )(mark.reshape(1), *arrays)


def on_device(background, absorb, density, profiles, adjoint_source, port_modes, design_start):
    planes_of = [[z * SYSTEMS + l for l in range(SYSTEMS)] for z in range(SYSTEMS)]
    columns = [[z * SYSTEMS + l for z in range(SYSTEMS)] for l in range(SYSTEMS)]
    packed, own_rows = call(
        pack_kernel,
        (f32(SYSTEMS, BLOCK, 8, 128), f32(3, 8, 128)),
        [HBM] * 7,
        (VMEM, VMEM),
        [pltpu.SMEM(array.shape, array.dtype) for array in (port_modes, design_start)]
        + [
            pltpu.VMEM(array.shape, array.dtype)
            for array in (background, absorb, density, profiles, adjoint_source)
        ]
        + [pltpu.SemaphoreType.DMA((7,))],
        "pack",
    )(port_modes, design_start, background, absorb, density, profiles, adjoint_source)
    block = lax.all_to_all(packed, "zslab", 0, 0, axis_index_groups=planes_of, tiled=True)
    count = SYSTEMS * SYSTEMS
    up = [(i, i + SYSTEMS) for i in range(count - SYSTEMS)]
    down = [(target, source) for source, target in up]
    low = lax.ppermute(block[SYSTEMS // 2 :], "zslab", up)
    high = lax.ppermute(block[: SYSTEMS // 2], "zslab", down)
    swap = [(i, i ^ 1) for i in range(4)]
    other = lax.ppermute(block[:, 16:ROWS_AT], "group", swap)
    inner = call(
        inner_kernel,
        (f32(SYSTEMS, 2, OWN, TILES, 8, 128), f32(2, OWN, TILES, 8, 128), f32(PAIRS, 8, 128)),
        [VMEM, VMEM],
        (VMEM,) * 3,
        (),
        "inner",
        10**8,
    )(block, other)
    high, inner = lax.optimization_barrier((high, inner))
    ends = lax.ppermute(high[:, 16:ROWS_AT], "group", swap)
    above = call(
        upper_kernel,
        f32(BASIS, 2, UPPER_PLANES, TILES, 8, 128),
        [VMEM] * 4,
        VMEM,
        [pltpu.VMEM((2, UPPER_PLANES, TILES, 8, 128), jnp.float32)],
        "upper",
        10**8,
    )(high, ends, inner[0], inner[1])
    low, above = lax.optimization_barrier((low, above))
    ends = lax.ppermute(low[:, 16:ROWS_AT], "group", swap)
    plane = (TILES, 8, 128)
    basis, gram, dens = call(
        outer_kernel,
        (f32(BASIS, 2, WINDOW, *plane), f32(1, 128), f32(2, 8, 128)),
        [VMEM] * 8,
        (VMEM, VMEM, VMEM),
        [pltpu.VMEM((2, WINDOW) + plane, jnp.float32), pltpu.VMEM((PAIRS, 8, 128), jnp.float32)],
        "outer",
        2 * 10**8,
    )(block, low, high, ends, above, *inner)
    grams = lax.all_to_all(
        jnp.broadcast_to(gram[None], (SYSTEMS, 1, 128)), "zslab", 0, 0,
        axis_index_groups=columns, tiled=True,
    )
    pick, nudge = gram_tables()
    solved = call(
        combine_kernel, f32(SYSTEMS, 33, 8, 128), [VMEM, VMEM, VMEM, VMEM], VMEM, (), "combine"
    )(grams, jnp.asarray(pick), jnp.asarray(nudge), basis)
    fields = lax.all_to_all(solved, "zslab", 0, 0, axis_index_groups=planes_of, tiled=True)
    half = f32(SYSTEMS // 2, 2, 2, 8 * TILES, 128)
    forward, adjoint = call(fields_kernel, (half, half), [VMEM], (VMEM,) * 2, (), "fields", 10**7)(fields)
    mine, beside, across = call(
        terms_kernel,
        (f32(5, 8, 128), f32(5, 8, 128), f32(2, 5, 8, 128)),
        [VMEM],
        (VMEM,) * 3,
        [pltpu.VMEM((4, 8 * TILES, 128), jnp.float32)],
        "terms",
    )(fields)
    across = lax.ppermute(across, "group", [(i, i ^ 2) for i in range(4)])
    across, forward, adjoint = lax.optimization_barrier((across, forward, adjoint))
    beside = lax.ppermute(beside + across[1], "group", swap)
    new_density, flag = call(
        density_kernel,
        (f32(2, 8, 128), f32(1)),
        [VMEM] * 5,
        (VMEM, SMEM),
        (),
        "density",
    )(mine, across, beside, own_rows, dens)

    def again(state):
        held = (background, absorb, density, profiles, adjoint_source)
        held = row_major(state[0], held, "arguments")
        results = iterate_on_device(*held, port_modes, design_start)
        return (jnp.zeros((), jnp.float32),) + tuple(row_major(state[0], results, "results"))

    state = (flag[0], forward, adjoint, new_density)
    return lax.while_loop(lambda state: state[0] > 0.0, again, state)[1:]


def solution(mesh):
    return jax.shard_map(
        on_device,
        mesh=mesh,
        in_specs=(
            P("zslab", None, None),
            P("zslab", None, None),
            P("zslab", None, None),
            P(None, None, "zslab", None, None),
            P("group", None, "zslab", None, None),
            P("group"),
            P(),
        ),
        out_specs=(
            P("group", None, "zslab", None, None),
            P("group", None, "zslab", None, None),
            P("zslab", "group", None),
        ),
        check_vma=False,
    )
```

```python
import functools

import jax
import jax.numpy as jnp
import numpy as np
from jax import lax
from jax.experimental import pallas as pl
from jax.experimental.pallas import tpu as pltpu
from jax.sharding import PartitionSpec as P

ITERS = 4


wave_sq = 0.1
step_size = 2.0
perm_span = 10.0
low_perm = 2.1
sharpness = 8.0
threshold = 0.5


def with_halo(block, sides, width):
    for axis, dim in sides:
        count = lax.axis_size(axis)
        forward = [(i, i + 1) for i in range(count - 1)]
        backward = [(target, source) for source, target in forward]
        low = lax.ppermute(
            lax.slice_in_dim(block, block.shape[dim] - width, None, axis=dim), axis, forward
        )
        high = lax.ppermute(lax.slice_in_dim(block, 0, width, axis=dim), axis, backward)
        block = jnp.concatenate([low, block, high], axis=dim)
    return block


def scaled(coef, field):
    coef_re = coef[0].reshape((-1, 1, 1, 1))
    coef_im = coef[1].reshape((-1, 1, 1, 1))
    real_part = coef_re * field[:, 0] - coef_im * field[:, 1]
    imag_part = coef_re * field[:, 1] + coef_im * field[:, 0]
    return jnp.stack([real_part, imag_part], axis=1)


def product_pair(left, right):
    real_part = jnp.sum(left[:, 0] * right[:, 0] + left[:, 1] * right[:, 1], axis=(1, 2, 3))
    imag_part = jnp.sum(left[:, 0] * right[:, 1] - left[:, 1] * right[:, 0], axis=(1, 2, 3))
    return (real_part, imag_part)


def divide_pair(top, bottom):
    denominator = bottom[0] * bottom[0] + bottom[1] * bottom[1]
    return (
        (top[0] * bottom[0] + top[1] * bottom[1]) / denominator,
        (top[1] * bottom[0] - top[0] * bottom[1]) / denominator,
    )


def multiply_pair(left, right):
    return (left[0] * right[0] - left[1] * right[1], left[0] * right[1] + left[1] * right[0])


def with_planes(field):
    return with_halo(field, (("zslab", 2),), 1)


def operate(field, diag_re, diag_im):
    padded = jnp.pad(with_planes(field), ((0, 0), (0, 0), (0, 0), (1, 1), (1, 1)))
    beside = padded[:, :, 2:, 1:-1, 1:-1] + padded[:, :, :-2, 1:-1, 1:-1]
    beside = beside + padded[:, :, 1:-1, 2:, 1:-1] + padded[:, :, 1:-1, :-2, 1:-1]
    beside = beside + padded[:, :, 1:-1, 1:-1, 2:] + padded[:, :, 1:-1, 1:-1, :-2]
    real_part = diag_re * field[:, 0] - diag_im * field[:, 1]
    imag_part = diag_re * field[:, 1] + diag_im * field[:, 0]
    return jnp.stack([real_part, imag_part], axis=1) - beside


def bicgstab(sources, diag_re, diag_im):
    solution = jnp.zeros_like(sources)
    residual = sources
    direction = sources
    bilinear = lax.psum(product_pair(sources, residual), "zslab")
    for iteration in range(ITERS):
        image = operate(direction, diag_re, diag_im)
        along = lax.psum(product_pair(sources, image), "zslab")
        advance = divide_pair(bilinear, along)
        halfway = residual - scaled(advance, image)
        second = operate(halfway, diag_re, diag_im)
        cross_re, cross_im = product_pair(second, halfway)
        energy = jnp.sum(second[:, 0] * second[:, 0] + second[:, 1] * second[:, 1], axis=(1, 2, 3))
        cross_re, cross_im, energy = lax.psum((cross_re, cross_im, energy), "zslab")
        relax_coef = (cross_re / energy, cross_im / energy)
        solution = solution + scaled(advance, direction) + scaled(relax_coef, halfway)
        residual = halfway - scaled(relax_coef, second)
        if iteration + 1 < ITERS:
            bilinear_new = lax.psum(product_pair(sources, residual), "zslab")
        if iteration + 1 < ITERS:
            blend_coef = multiply_pair(
                divide_pair(bilinear_new, bilinear), divide_pair(advance, relax_coef)
            )
            direction = residual + scaled(blend_coef, direction - scaled(relax_coef, image))
            bilinear = bilinear_new
    return solution


def iterate_on_device(background, absorb, density, profiles, adjoint_source, port_modes, design_start):
    planes_dev = density.shape[0]
    rows_all = density.shape[1]
    first_plane = lax.axis_index("zslab") * planes_dev
    design_depth = planes_dev * lax.axis_size("zslab") // 2
    planes = first_plane + jnp.arange(planes_dev)
    in_design = (planes >= design_start[0]) & (planes < design_start[0] + design_depth)
    in_design = in_design[:, None, None]
    permittivity = jnp.where(in_design, low_perm + perm_span * density, background)
    diag_re = 6.0 - wave_sq * permittivity
    selector = (port_modes[:, None] == jnp.arange(profiles.shape[0])[None, :]).astype(jnp.float32)
    forward_source = jnp.einsum(
        "pm,mczyx->pczyx", selector, profiles, precision=lax.Precision.HIGHEST
    )
    port_count = forward_source.shape[0]
    sources = jnp.concatenate([forward_source, adjoint_source], axis=0)
    fields = bicgstab(sources, diag_re, absorb)
    forward_field = fields[:port_count]
    adjoint_field = fields[port_count:]
    terms = forward_field[:, 0] * adjoint_field[:, 0] - forward_field[:, 1] * adjoint_field[:, 1]
    local_term = -wave_sq * jnp.sum(terms, axis=0)
    rows_share = rows_all // lax.axis_size("group")
    row_start = lax.axis_index("group") * rows_share
    total = lax.psum(local_term, "group")
    gradient = lax.dynamic_slice_in_dim(total, row_start, rows_share, 1)
    density_rows = lax.dynamic_slice_in_dim(density, row_start, rows_share, 1)
    updated = jnp.where(
        in_design, jnp.clip(density_rows - step_size * perm_span * gradient, 0.0, 1.0), density_rows
    )
    extended = with_halo(updated, (("zslab", 0),), 1)
    padded = jnp.pad(extended, ((0, 0), (0, 0), (1, 1)))
    filtered = (
        2.0 * updated
        + padded[2:, :, 1:-1]
        + padded[:-2, :, 1:-1]
        + padded[1:-1, :, 2:]
        + padded[1:-1, :, :-2]
    ) / 6.0
    new_density = (
        jnp.tanh(sharpness * threshold) + jnp.tanh(sharpness * (filtered - threshold))
    ) / (jnp.tanh(sharpness * threshold) + jnp.tanh(sharpness * (1.0 - threshold)))
    return (forward_field, adjoint_field, new_density)


BASIS = 2 * ITERS + 1
CENTRE = 5.3
HALF_RADIUS = 3.0
THIRD = 1.0 / HALF_RADIUS
NUDGE = 1e-6
AGREE = 5e-4
ROWS = 16 * BASIS


def pair_places():
    real, imag, place = {}, {}, 0
    for j in range(BASIS):
        for i in range(j + 1):
            real[(i, j)] = place
            place += 1
    for j in range(BASIS):
        for i in range(j):
            imag[(i, j)] = place
            place += 1
    return real, imag


def gram_tables():
    real, imag = pair_places()
    pick = np.zeros((2 * ROWS + 16, 128), np.float32)
    nudge = np.zeros((2 * ROWS, 128), np.float32)
    rng = np.random.default_rng(7)
    sign_re = {pair: np.where(rng.random(128) < 0.5, -1.0, 1.0) for pair in real}
    sign_im = {pair: np.where(rng.random(128) < 0.5, -1.0, 1.0) for pair in imag}
    for j in range(BASIS):
        for i in range(BASIS):
            row, pair = j * 16 + i, (min(i, j), max(i, j))
            pick[row, real[pair]] = 1.0
            nudge[row] = NUDGE * sign_re[pair]
            if i != j:
                side = 1.0 if i < j else -1.0
                pick[ROWS + row, imag[pair]] = side
                nudge[ROWS + row] = NUDGE * side * sign_im[pair]
        pick[2 * ROWS + j, real[(j, j)]] = 1.0
    nudge[:, 0] = 0.0
    return pick, nudge


def exact_dot(left, right, dims):
    return lax.dot_general(
        left, right, (dims, ((), ())), precision=lax.Precision.HIGHEST,
        preferred_element_type=jnp.float32,
    )


def minus_pair(left, right):
    return (left[0] - right[0], left[1] - right[1])


def plus_pair(left, right):
    return (left[0] + right[0], left[1] + right[1])


def coefficients(gram_re, gram_im):
    row = lax.broadcasted_iota(jnp.int32, (16, 128), 0)
    keep = jnp.where(row == 15, 0.0, HALF_RADIUS)

    def apply(q):
        return tuple(
            CENTRE * v + HALF_RADIUS * pltpu.roll(v, 1, 0) + keep * pltpu.roll(v, 15, 0) for v in q
        )

    def total(v):
        return jnp.sum(v, axis=0, keepdims=True)

    def with_source(q):
        return (
            total(gram_re[0] * q[0] + gram_im[0] * q[1]),
            total(gram_re[0] * q[1] - gram_im[0] * q[0]),
        )

    def times_gram(q):
        out_re = jnp.zeros((16, 128), jnp.float32)
        out_im = jnp.zeros((16, 128), jnp.float32)
        for j in range(BASIS):
            q_re, q_im = q[0][j : j + 1], q[1][j : j + 1]
            out_re = out_re + (gram_re[j] * q_re - gram_im[j] * q_im)
            out_im = out_im + (gram_re[j] * q_im + gram_im[j] * q_re)
        return out_re, out_im

    one = jnp.where(row == 0, 1.0, 0.0)
    zero = jnp.zeros((16, 128), jnp.float32)
    answer, residual, direction = (zero, zero), (one, zero), (one, zero)
    bilinear = with_source(residual)
    for iteration in range(ITERS):
        image = apply(direction)
        advance = divide_pair(bilinear, with_source(image))
        halfway = minus_pair(residual, multiply_pair(advance, image))
        second = apply(halfway)
        weighed = times_gram(second)
        energy = total(second[0] * weighed[0] + second[1] * weighed[1])
        relax = (
            total(weighed[0] * halfway[0] + weighed[1] * halfway[1]) / energy,
            total(weighed[0] * halfway[1] - weighed[1] * halfway[0]) / energy,
        )
        answer = plus_pair(
            answer, plus_pair(multiply_pair(advance, direction), multiply_pair(relax, halfway))
        )
        if iteration + 1 < ITERS:
            residual = minus_pair(halfway, multiply_pair(relax, second))
            bilinear_new = with_source(residual)
            blend = multiply_pair(divide_pair(bilinear_new, bilinear), divide_pair(advance, relax))
            direction = plus_pair(
                residual, multiply_pair(blend, minus_pair(direction, multiply_pair(relax, image)))
            )
            bilinear = bilinear_new
    first = tuple(jnp.broadcast_to(v[:, :1], v.shape) for v in answer)
    apart = minus_pair(answer, first)

    def norm(q):
        weighed = times_gram(q)
        return total(q[0] * weighed[0] + q[1] * weighed[1])

    return first, norm(apart), norm(first)


TILES = 4
SYSTEMS = 8
BLOCK = 12 * TILES // 2 + 1
ROWS_AT = BLOCK - 1
OWN = 16
WINDOW = 32
CORE = 8
VMEM = pl.BlockSpec(memory_space=pltpu.VMEM)
SMEM = pl.BlockSpec(memory_space=pltpu.SMEM)
HBM = pl.BlockSpec(memory_space=pltpu.HBM)
PAIRS = 88
LIMIT = 24 * 1024 * 1024


def call(kernel, outs, specs, out_specs, scratch=(), name=None, flops=0):
    return pl.pallas_call(
        kernel,
        out_shape=outs,
        in_specs=specs,
        out_specs=out_specs,
        scratch_shapes=list(scratch),
        compiler_params=pltpu.CompilerParams(vmem_limit_bytes=LIMIT),
        cost_estimate=pl.CostEstimate(flops=flops, bytes_accessed=1 << 20, transcendentals=0),
        name=name,
    )


def f32(*shape):
    return jax.ShapeDtypeStruct(shape, jnp.float32)


def rows_of(tile):
    return pl.ds(tile, 8, stride=TILES)


def pack_kernel(*refs):
    arguments, out, own, held, sems = refs[:7], refs[7], refs[8], refs[9:16], refs[16]
    modes, start, background, absorb, density, profiles, adjoint = held
    half = SYSTEMS // 2
    place = slab_and_group()
    copies = [
        pltpu.make_async_copy(array, room, sems.at[at])
        for at, (array, room) in enumerate(zip(arguments, held))
    ]
    for copy in copies:
        copy.start()
    for copy in copies[:5]:
        copy.wait()
    for plane in range(2):
        where = place[0] * 2 + plane
        inside = (where >= start[0]) & (where < start[0] + SYSTEMS * SYSTEMS)
        for tile in range(TILES):
            rows = rows_of(tile)
            perm = jnp.where(
                inside, low_perm + perm_span * density[plane, rows], background[plane, rows]
            )
            diag_re = ((6.0 - wave_sq * perm) - CENTRE) * THIRD
            diag_im = absorb[plane, rows] * THIRD
            part = jnp.where(place[1] % 2 == 0, diag_re, diag_im)
            for system in range(SYSTEMS):
                out[system, 16 + plane * TILES + tile] = part
    share = pl.ds(pl.multiple_of(place[1] * 8, 8), 8)
    own[0] = density[0, share]
    own[1] = density[1, share]
    own[2] = jnp.full((8, 128), start[0]).astype(jnp.float32)
    after = (place[0] + 1) % SYSTEMS
    for slab in range(SYSTEMS):
        out[slab, ROWS_AT] = jnp.where(after == slab, density[1, share], density[0, share])
    for copy in copies[5:]:
        copy.wait()
    for system in range(half):
        mode = modes[system]
        for part in range(2):
            for plane in range(2):
                for tile in range(TILES):
                    at = (part * 2 + plane) * TILES + tile
                    out[system, at] = profiles[mode, part, plane, rows_of(tile)]
                    out[half + system, at] = adjoint[system, part, plane, rows_of(tile)]


def slab_and_group():
    return lax.axis_index("zslab"), lax.axis_index("group")


class Stencil:
    def __init__(self):
        row = lax.broadcasted_iota(jnp.int32, (8, 128), 0)
        lane = lax.broadcasted_iota(jnp.int32, (8, 128), 1)
        self.first_row, self.last_row = row == 0, row == 7
        self.first_lane, self.last_lane = lane == 0, lane == 127

    def beside(self, below, here, above):
        up = jnp.where(self.first_row, 0.0, pltpu.roll(here[TILES - 1], 1, 0))
        down = jnp.where(self.last_row, 0.0, pltpu.roll(here[0], 7, 0))
        rows = [up] + list(here) + [down]
        sums = []
        for tile in range(TILES):
            left = jnp.where(self.first_lane, 0.0, pltpu.roll(here[tile], 1, 1))
            right = jnp.where(self.last_lane, 0.0, pltpu.roll(here[tile], 127, 1))
            z_sum = below[tile] + above[tile]
            sums.append((z_sum + (rows[tile] + rows[tile + 2])) + (left + right))
        return sums

    def run(self, basis, diag, level, first, last, third_of):
        def load(at):
            return [[basis[level, part, at, tile] for tile in range(TILES)] for part in range(2)]

        below, here = load(first - 1), load(first)
        for at in range(first, last):
            above = load(at + 1)
            third = third_of(at)
            near = [self.beside(below[part], here[part], above[part]) for part in range(2)]
            for tile in range(TILES):
                diag_re, diag_im = diag[0, at, tile], diag[1, at, tile]
                real, imag = here[0][tile], here[1][tile]
                new_re = diag_re * real - diag_im * imag - third * near[0][tile]
                new_im = diag_re * imag + diag_im * real - third * near[1][tile]
                if level > 0:
                    new_re = new_re - basis[level - 1, 0, at, tile]
                    new_im = new_im - basis[level - 1, 1, at, tile]
                basis[level + 1, 0, at, tile] = new_re
                basis[level + 1, 1, at, tile] = new_im
            below, here = here, above


def gram_pass(basis, acc, columns, ranges, shift):
    real_at, imag_at = pair_places()
    pairs = [(i, j) for j in columns for i in range(j + 1)]
    top = max(columns) + 1
    places = []
    for pair in pairs:
        places.append(real_at[pair])
        if pair[0] != pair[1]:
            places.append(imag_at[pair])

    def position(step, sums, first=0):
        window, tile = first + shift + step // TILES, step % TILES
        field = [(basis[k, 0, window, tile], basis[k, 1, window, tile]) for k in range(top)]
        new = []
        for i, j in pairs:
            (i_re, i_im), (j_re, j_im) = field[i], field[j]
            new.append(i_re * j_re + i_im * j_im)
            if i != j:
                new.append(i_re * j_im - i_im * j_re)
        return tuple(total + term for total, term in zip(sums, new))

    sums = tuple(acc[at] for at in places)
    for first, last in ranges:
        sums = lax.fori_loop(
            0, (last - first) * TILES, functools.partial(position, first=first), sums,
            unroll=8 if (last - first) % 2 == 0 else 4,
        )
    for at, value in zip(places, sums):
        acc[at] = value


def inner_kernel(block, other, basis, diag, acc):
    place = slab_and_group()
    core = place[1] % 2

    def load(chunk, _):
        for plane in range(2):
            for part in range(2):
                for tile in range(TILES):
                    at = part * 8 + plane * TILES + tile
                    basis[0, part, 2 * chunk + plane, tile] = block[chunk, at]
            for tile in range(TILES):
                at = plane * TILES + tile
                diag[core, 2 * chunk + plane, tile] = block[chunk, 16 + at]
                diag[1 - core, 2 * chunk + plane, tile] = other[chunk, at]
        return 0

    lax.fori_loop(0, SYSTEMS, load, 0, unroll=SYSTEMS)
    stencil = Stencil()
    for level in range(SYSTEMS - 1):
        stencil.run(basis, diag, level, level + 1, OWN - 1 - level, lambda at: THIRD)
    acc[...] = jnp.zeros_like(acc)
    for columns, ranges in INNER_PASSES:
        gram_pass(basis, acc, columns, ranges, 0)


INNER_PASSES = (
    ((0, 1, 2, 3, 4), ((4, 12),)),
    ((0, 1, 2), ((2, 4), (12, 14))),
    ((5, 6), ((6, 10),)),
    ((7,), ((7, 9),)),
)
OUTER_PASSES = (
    ((0, 1, 2, 3, 4), ((0, 2), (14, 16))),
    ((3, 4), ((2, 4), (12, 14))),
    ((5, 6), ((0, 6), (10, 16))),
    ((7,), ((0, 6), (6, 7), (9, 10), (10, 16))),
    ((8,), ((0, 16),)),
)


def outer_kernel(
    block, low, high, other, inner, inner_diag, inner_acc, basis, gram, dens, diag, acc
):
    place = slab_and_group()
    core = place[1] % 2

    def load(source, first, at):
        def one(chunk, _):
            for plane in range(2):
                window = at + 2 * chunk + plane
                for part in range(2):
                    for tile in range(TILES):
                        spot = part * 8 + plane * TILES + tile
                        basis[0, part, window, tile] = source[chunk, spot]
                for tile in range(TILES):
                    spot = plane * TILES + tile
                    diag[core, window, tile] = source[chunk, 16 + spot]
                    diag[1 - core, window, tile] = other[first + chunk, spot]
            return 0

        lax.fori_loop(0, SYSTEMS // 2, one, 0, unroll=SYSTEMS // 2)

    load(low, 0, 0)
    load(high, SYSTEMS // 2, CORE + OWN)
    for level in range(SYSTEMS):

        def keep(at, _, level=level):
            for part in range(2):
                for tile in range(TILES):
                    basis[level, part, CORE + at, tile] = inner[level, part, at, tile]
                    if level == 0:
                        diag[part, CORE + at, tile] = inner_diag[part, at, tile]
            return 0

        lax.fori_loop(level, OWN - level, keep, 0, unroll=OWN - 2 * level)
    acc[...] = inner_acc[...]

    me = place[0] % SYSTEMS
    dens[0] = jnp.where(
        me > 0, block[jnp.maximum(me - 1, 0), ROWS_AT], low[SYSTEMS // 2 - 1, ROWS_AT]
    )
    dens[1] = jnp.where(
        me < SYSTEMS - 1, block[jnp.minimum(me + 1, SYSTEMS - 1), ROWS_AT], high[0, ROWS_AT]
    )

    third_low = jnp.where(place[0] >= SYSTEMS, THIRD, 0.0)
    third_high = jnp.where(place[0] < SYSTEMS * (SYSTEMS - 1), THIRD, 0.0)
    stencil = Stencil()
    for level in range(BASIS - 1):
        lower, upper = level + 1, WINDOW - 1 - level
        stencil.run(
            basis, diag, level, lower, lower + CORE,
            lambda at: third_low if at < CORE else THIRD,
        )
        stencil.run(
            basis, diag, level, upper - CORE, upper,
            lambda at: third_high if at >= CORE + OWN else THIRD,
        )
    for columns, ranges in OUTER_PASSES:
        gram_pass(basis, acc, columns, ranges, CORE)
    by_pair = jnp.concatenate(
        [jnp.sum(acc[...], axis=1), jnp.zeros((128 - PAIRS, 128), jnp.float32)], axis=0
    )
    ones = jnp.ones((8, 128), jnp.float32)
    gram[...] = exact_dot(ones, by_pair, ((1,), (1,)))[0:1]


def combine_kernel(grams, pick, nudge, basis, out):
    row = grams[0]
    for other in range(1, SYSTEMS):
        row = row + grams[other]
    ones = jnp.ones((128, 128), jnp.float32)
    picked = exact_dot(pick[...] * row, ones, ((1,), (0,)))
    norms = jnp.sqrt(picked[2 * ROWS :])
    gram = []
    for column in range(2 * BASIS):
        rows = slice(16 * column, 16 * column + 16)
        scale = norms * norms[column % BASIS : column % BASIS + 1]
        gram.append(picked[rows] + nudge[rows] * scale)
    answer, apart, size = coefficients(gram[:BASIS], gram[BASIS:])
    agrees = jnp.max(jnp.where(apart <= AGREE * AGREE * size, 0.0, 1.0))
    flag = jnp.zeros((8, 128), jnp.float32) + agrees
    for slab in range(SYSTEMS):
        out[slab, 32] = flag
    weight = [
        (
            jnp.broadcast_to(answer[0][k : k + 1], (8, 128)),
            jnp.broadcast_to(answer[1][k : k + 1], (8, 128)),
        )
        for k in range(BASIS - 1)
    ]

    def solve_plane(plane, goals):
        for tile in range(TILES):
            real = jnp.zeros((8, 128), jnp.float32)
            imag = jnp.zeros((8, 128), jnp.float32)
            for k in range(BASIS - 1):
                b_re, b_im = basis[k, 0, plane, tile], basis[k, 1, plane, tile]
                real = real + (weight[k][0] * b_re - weight[k][1] * b_im)
                imag = imag + (weight[k][0] * b_im + weight[k][1] * b_re)
            for slab, at in goals:
                out[slab, at * TILES + tile] = real
                out[slab, (4 + at) * TILES + tile] = imag

    def middle(slab, _):
        for plane in range(2):
            solve_plane(CORE - 1 + 2 * slab + plane, ((slab, plane), (slab - 1, 2 + plane)))
        return 0

    for plane in range(2):
        solve_plane(CORE - 1 + plane, ((0, plane),))
        solve_plane(CORE + OWN - 1 + plane, ((SYSTEMS - 1, 2 + plane),))
    lax.fori_loop(1, SYSTEMS, middle, 0)


def fields_kernel(fields, forward, adjoint):
    half = SYSTEMS // 2
    for port in range(half):
        for part in range(2):
            for plane in range(2):
                for tile in range(TILES):
                    at = (part * 4 + 1 + plane) * TILES + tile
                    forward[port, part, plane, rows_of(tile)] = fields[port, at]
                    adjoint[port, part, plane, rows_of(tile)] = fields[half + port, at]


def terms_kernel(fields, mine, beside, across, natural):
    half = SYSTEMS // 2
    for plane in range(4):
        for tile in range(TILES):
            real, imag = plane * TILES + tile, (4 + plane) * TILES + tile
            total = None
            for port in range(half):
                term = fields[port, real] * fields[half + port, real]
                term = term - fields[port, imag] * fields[half + port, imag]
                total = term if total is None else total + term
            natural[plane, rows_of(tile)] = total
    flag = fields[0, 32]
    for system in range(1, SYSTEMS):
        flag = flag + fields[system, 32]
    group = slab_and_group()[1]
    core, chip = group % 2, group // 2
    for out, pair, side in (
        (mine, chip, core),
        (beside, chip, 1 - core),
        (across.at[0], 1 - chip, core),
        (across.at[1], 1 - chip, 1 - core),
    ):
        rows = pl.ds(pl.multiple_of((2 * pair + side) * 8, 8), 8)
        for plane in range(4):
            out[plane] = natural[plane, rows]
        out[4] = flag


def density_kernel(mine, across, beside, own, dens, out, flag):
    lane = lax.broadcasted_iota(jnp.int32, (8, 128), 1)
    updated = []
    for plane in range(4):
        gradient = -wave_sq * (mine[plane] + across[0, plane] + beside[plane])
        where = slab_and_group()[0] * 2 + plane - 1
        depth = where.astype(jnp.float32) - own[2]
        inside = (depth >= 0.0) & (depth < SYSTEMS * SYSTEMS)
        rows = (dens[0], own[0], own[1], dens[1])[plane]
        moved = jnp.clip(rows - step_size * perm_span * gradient, 0.0, 1.0)
        rows = jnp.where(inside, moved, rows)
        exists = (where >= 0) & (where < 2 * SYSTEMS * SYSTEMS)
        updated.append(jnp.where(exists, rows, 0.0))
    for plane in range(2):
        own = updated[plane + 1]
        right = jnp.where(lane == 127, 0.0, pltpu.roll(own, 127, 1))
        left = jnp.where(lane == 0, 0.0, pltpu.roll(own, 1, 1))
        filtered = (2.0 * own + updated[plane + 2] + updated[plane] + right + left) / 6.0
        edge = float(np.tanh(sharpness * threshold))
        other_edge = float(np.tanh(sharpness * (1.0 - threshold)))
        out[plane] = (edge + jnp.tanh(sharpness * (filtered - threshold))) / (edge + other_edge)
    flag[0] = jnp.max(mine[4] + across[0, 4] + beside[4])


def copy_kernel(count, *refs):
    sems = refs[-1]
    arrays = refs[-1 - 2 * count : -1]
    copies = [
        pltpu.make_async_copy(arrays[at], arrays[count + at], sems.at[at]) for at in range(count)
    ]
    for copy in copies:
        copy.start()
    for copy in copies:
        copy.wait()


def row_major(mark, arrays, name):
    count = len(arrays)
    return call(
        functools.partial(copy_kernel, count),
        tuple(jax.ShapeDtypeStruct(array.shape, array.dtype) for array in arrays),
        [SMEM] + [HBM] * count,
        (HBM,) * count,
        [pltpu.SemaphoreType.DMA((count,))],
        name,
    )(mark.reshape(1), *arrays)


def on_device(background, absorb, density, profiles, adjoint_source, port_modes, design_start):
    planes_of = [[z * SYSTEMS + l for l in range(SYSTEMS)] for z in range(SYSTEMS)]
    columns = [[z * SYSTEMS + l for z in range(SYSTEMS)] for l in range(SYSTEMS)]
    packed, own_rows = call(
        pack_kernel,
        (f32(SYSTEMS, BLOCK, 8, 128), f32(3, 8, 128)),
        [HBM] * 7,
        (VMEM, VMEM),
        [pltpu.SMEM(array.shape, array.dtype) for array in (port_modes, design_start)]
        + [
            pltpu.VMEM(array.shape, array.dtype)
            for array in (background, absorb, density, profiles, adjoint_source)
        ]
        + [pltpu.SemaphoreType.DMA((7,))],
        "pack",
    )(port_modes, design_start, background, absorb, density, profiles, adjoint_source)
    block = lax.all_to_all(packed, "zslab", 0, 0, axis_index_groups=planes_of, tiled=True)
    count = SYSTEMS * SYSTEMS
    up = [(i, i + SYSTEMS) for i in range(count - SYSTEMS)]
    down = [(target, source) for source, target in up]
    low = lax.ppermute(block[SYSTEMS // 2 :], "zslab", up)
    high = lax.ppermute(block[: SYSTEMS // 2], "zslab", down)
    swap = [(i, i ^ 1) for i in range(4)]
    other = lax.ppermute(block[:, 16:ROWS_AT], "group", swap)
    inner = call(
        inner_kernel,
        (f32(SYSTEMS, 2, OWN, TILES, 8, 128), f32(2, OWN, TILES, 8, 128), f32(PAIRS, 8, 128)),
        [VMEM, VMEM],
        (VMEM,) * 3,
        (),
        "inner",
        10**8,
    )(block, other)
    low, high, inner = lax.optimization_barrier((low, high, inner))
    ends = jnp.concatenate([low[:, 16:ROWS_AT], high[:, 16:ROWS_AT]], axis=0)
    ends = lax.ppermute(ends, "group", swap)
    plane = (TILES, 8, 128)
    basis, gram, dens = call(
        outer_kernel,
        (f32(BASIS, 2, WINDOW, *plane), f32(1, 128), f32(2, 8, 128)),
        [VMEM] * 7,
        (VMEM, VMEM, VMEM),
        [pltpu.VMEM((2, WINDOW) + plane, jnp.float32), pltpu.VMEM((PAIRS, 8, 128), jnp.float32)],
        "outer",
        2 * 10**8,
    )(block, low, high, ends, *inner)
    grams = lax.all_to_all(
        jnp.broadcast_to(gram[None], (SYSTEMS, 1, 128)), "zslab", 0, 0,
        axis_index_groups=columns, tiled=True,
    )
    pick, nudge = gram_tables()
    solved = call(
        combine_kernel, f32(SYSTEMS, 33, 8, 128), [VMEM, VMEM, VMEM, VMEM], VMEM, (), "combine"
    )(grams, jnp.asarray(pick), jnp.asarray(nudge), basis)
    fields = lax.all_to_all(solved, "zslab", 0, 0, axis_index_groups=planes_of, tiled=True)
    half = f32(SYSTEMS // 2, 2, 2, 8 * TILES, 128)
    forward, adjoint = call(fields_kernel, (half, half), [VMEM], (VMEM,) * 2, (), "fields", 10**7)(fields)
    mine, beside, across = call(
        terms_kernel,
        (f32(5, 8, 128), f32(5, 8, 128), f32(2, 5, 8, 128)),
        [VMEM],
        (VMEM,) * 3,
        [pltpu.VMEM((4, 8 * TILES, 128), jnp.float32)],
        "terms",
    )(fields)
    across = lax.ppermute(across, "group", [(i, i ^ 2) for i in range(4)])
    across, forward, adjoint = lax.optimization_barrier((across, forward, adjoint))
    beside = lax.ppermute(beside + across[1], "group", swap)
    new_density, flag = call(
        density_kernel,
        (f32(2, 8, 128), f32(1)),
        [VMEM] * 5,
        (VMEM, SMEM),
        (),
        "density",
    )(mine, across, beside, own_rows, dens)

    def again(state):
        held = (background, absorb, density, profiles, adjoint_source)
        held = row_major(state[0], held, "arguments")
        results = iterate_on_device(*held, port_modes, design_start)
        return (jnp.zeros((), jnp.float32),) + tuple(row_major(state[0], results, "results"))

    state = (flag[0], forward, adjoint, new_density)
    return lax.while_loop(lambda state: state[0] > 0.0, again, state)[1:]


def solution(mesh):
    return jax.shard_map(
        on_device,
        mesh=mesh,
        in_specs=(
            P("zslab", None, None),
            P("zslab", None, None),
            P("zslab", None, None),
            P(None, None, "zslab", None, None),
            P("group", None, "zslab", None, None),
            P("group"),
            P(),
        ),
        out_specs=(
            P("group", None, "zslab", None, None),
            P("group", None, "zslab", None, None),
            P("zslab", "group", None),
        ),
        check_vma=False,
    )
```
